32 devices in a mesh: sn: 8 (over y, x, core), rhs: 4 (over z).
Axes of the slice: x: 2, y: 2, z: 4, core: 2. Of those that a mesh axis runs over, the one named last changes fastest.
Arguments:
- rhs_leaf: float32 [256, 256, 128], P('sn', 'rhs'), may hold values from -6 to 6
- rhs_top: float32 [8, 256, 128], P('sn', 'rhs'), may hold values from -6 to 6
- leaf_blocks: float32 [256, 3, 128, 128], P('sn', None, 'rhs'), may hold values from -0.078125 to 0.078125
- leaf_dinv: float32 [256, 128, 128], P('sn', 'rhs')
- leaf_struct: int32 [256, 3], P('sn'), may hold values from 1 to 39, as said below
- top_blocks: float32 [8, 8, 128, 128], P(None, 'sn', 'rhs'), may hold values from -0.1875 to 0.1875
- top_dinv: float32 [8, 128, 128], P('sn', 'rhs')
Outputs:
- leaf_solution: float32 [256, 256, 128], P('sn', 'rhs')
- top_solution: float32 [8, 256, 128], P('sn', 'rhs')
The draws below stay inside these ranges and needn't reach their ends.
Inputs may be any that keep to these rules, and one draw needn't show every extreme that they name: `leaf_struct`: subtree d hangs below top supernode a = 4 * (d // 4). Row d * 32 + s names 3 distinct ancestors of leaf supernode s of subtree d: a value v < 32 is supernode v of the same subtree, with v > s; a value 32 + k is a top supernode k on a's path to the root, that is k = a or the factor holds top block (k, a). Column 0 is the elimination tree parent: s + 1, except for the subtree's last supernode, whose parent is 32 + a.
All inputs are finite; a program needn't handle non-finite values.
Results may differ from the reference program's by a relative error of at most 0.00018.
Values sent between devices are 32-bit elements; how exact they have to be, the bound alone decides.
No kernel may reach another device: no remote copies, remote signals or barrier semaphores. Data moves between devices by JAX's collectives and lax.ppermute only.
A program may use at most 64 MiB of HBM per device.

```python
from functools import partial
import jax
import jax.numpy as jnp
from jax import lax

W = 128
NRHS = 256
R = 3
LEAF = 32
TOPS = 8
LEAFS = 256


def dominant_inverse(key, count):
    diag_key, off_key = jax.random.split(key)
    diagonal = jax.random.uniform(diag_key, (count, W), jnp.float32, 0.7, 1.3)
    off_part = jnp.clip(jax.random.normal(off_key, (count, W, W), jnp.float32), -4.0, 4.0) * (0.35 / W ** 0.5)
    identity_mask = jnp.eye(W, dtype=jnp.float32)
    return identity_mask[None] * diagonal[:, :, None] + (1.0 - identity_mask[None]) * off_part


def draw_leaf_dinv(key, part):
    return dominant_inverse(jax.random.fold_in(key, 11), LEAFS)


def draw_top_dinv(key, part):
    return dominant_inverse(jax.random.fold_in(key, 23), TOPS)


def draw_leaf_struct(key, part):
    total_nodes = LEAF + TOPS
    row_keys = jax.random.split(jax.random.fold_in(key, 37), LEAFS)
    candidate = jnp.arange(total_nodes, dtype=jnp.int32)
    top_index = jnp.clip(candidate - LEAF, 0, TOPS - 1).astype(jnp.int32)
    span = jnp.ones((total_nodes,), jnp.int32)
    for place in range(TOPS.bit_length()):
        span = span + ((top_index + 1) % 2 ** (place + 1) == 0).astype(jnp.int32) * 2 ** place
    rows = jnp.arange(LEAFS, dtype=jnp.int32)
    position = rows % LEAF
    attach = (4 * (rows // LEAF // 4)).astype(jnp.int32)
    parent = jnp.where(position < LEAF - 1, position + 1, LEAF + attach).astype(jnp.int32)

    def choose(row_key, place, parent_id, attach_top):
        scores = jax.random.permutation(row_key, total_nodes).astype(jnp.int32)
        on_path = (candidate >= LEAF) & (top_index >= attach_top) & (top_index + 1 - span <= attach_top)
        inside = (candidate > place) & (candidate < LEAF)
        allowed = (inside | on_path) & (candidate != parent_id)
        scores = jnp.where(allowed, scores, -1)
        unused, chosen = lax.top_k(scores, R - 1)
        return jnp.concatenate([parent_id[None], chosen.astype(jnp.int32)]).astype(jnp.int32)
    return jax.vmap(choose)(row_keys, position, parent, attach)


def shard_levels(own_key, dims, cuts, least, top_value):
    def one(axis_at, blocks):
        steps = jax.random.uniform(jax.random.fold_in(jax.random.fold_in(own_key, 6), axis_at), (blocks,), jnp.float32, least / len(cuts), top_value / len(cuts))
        return jnp.repeat(jnp.exp(steps), dims[axis_at] // blocks).reshape((-1,) + (1,) * (len(dims) - axis_at - 1))

    loudness = one(*cuts[0])
    for cut in cuts[1:]:
        loudness = loudness * one(*cut)
    return loudness


def bell_draw(stream_key, shape, width, reach, cuts=(), kind=jnp.bfloat16):
    entries = width * jax.random.normal(stream_key, shape, jnp.float32)
    if cuts:
        entries = entries * shard_levels(stream_key, shape, cuts, -0.22, 0.18)
    return jnp.clip(entries, -reach, reach).astype(kind)


def setup_inputs(seed: int = 0) -> dict:
    splits = jax.random.split(jax.random.key(seed), 8)
    return {
        "rhs_leaf": bell_draw(splits[0], (LEAFS, NRHS, W), 1.0, 6.0, ((0, 8), (1, 4)), jnp.float32),
        "rhs_top": bell_draw(splits[1], (TOPS, NRHS, W), 1.0, 6.0, ((0, 8), (1, 4)), jnp.float32),
        "leaf_blocks": bell_draw(splits[2], (LEAFS, R, W, W), (44 * W) ** -0.5, 0.078125, ((0, 8), (2, 4)), jnp.float32),
        "leaf_dinv": draw_leaf_dinv(jax.random.fold_in(splits[7], 71), 0),
        "leaf_struct": draw_leaf_struct(jax.random.fold_in(splits[7], 71), 0),
        "top_blocks": bell_draw(splits[5], (TOPS, TOPS, W, W), (8 * W) ** -0.5, 0.1875, ((1, 8), (2, 4)), jnp.float32),
        "top_dinv": draw_top_dinv(jax.random.fold_in(splits[7], 71), 0),
    }


highest = lax.Precision.HIGHEST


def top_structure(count):
    levels = count.bit_length()
    index = jnp.arange(count, dtype=jnp.int32)
    span = jnp.ones((count,), jnp.int32)
    for place in range(levels):
        span = span + ((index + 1) % (2 ** (place + 1)) == 0).astype(jnp.int32) * (2 ** place)
    row_index = index[:, None]
    col_index = index[None, :]
    keep = (col_index < row_index) & (col_index >= row_index + 1 - span[:, None])
    return keep.astype(jnp.float32)


def leaf_forward(top_total, rhs_part, blocks, inverses, struct):
    leaf_total = rhs_part.shape[0]
    updates = jnp.zeros((leaf_total + top_total,) + rhs_part.shape[1:], jnp.float32)
    values = jnp.zeros(rhs_part.shape, jnp.float32)

    def advance(position, state_pair):
        updates, values = state_pair
        source = lax.dynamic_index_in_dim(rhs_part, position, 0, False) - lax.dynamic_index_in_dim(updates, position, 0, False)
        solved = jnp.einsum("ck,ik->ci", source, lax.dynamic_index_in_dim(inverses, position, 0, False), precision=highest)
        targets = lax.dynamic_index_in_dim(struct, position, 0, False)
        outgoing = jnp.einsum("ck,rik->rci", solved, lax.dynamic_index_in_dim(blocks, position, 0, False), precision=highest)
        updates = updates.at[targets].add(outgoing)
        values = lax.dynamic_update_index_in_dim(values, solved, position, 0)
        return updates, values

    updates, values = lax.fori_loop(0, leaf_total, advance, (updates, values))
    return values, updates[leaf_total:]


def leaf_backward(forward_values, blocks, inverses, struct, top_values):
    leaf_total = forward_values.shape[0]
    solution_buffer = jnp.concatenate([jnp.zeros_like(forward_values), top_values], axis=0)

    def retreat(offset, solution_buffer):
        position = leaf_total - 1 - offset
        targets = lax.dynamic_index_in_dim(struct, position, 0, False)
        ancestors = jnp.take(solution_buffer, targets, axis=0)
        summed = jnp.einsum("rci,rik->ck", ancestors, lax.dynamic_index_in_dim(blocks, position, 0, False), precision=highest)
        own_rhs = lax.dynamic_index_in_dim(forward_values, position, 0, False)
        solved = jnp.einsum("ci,ik->ck", own_rhs - summed, lax.dynamic_index_in_dim(inverses, position, 0, False), precision=highest)
        return lax.dynamic_update_index_in_dim(solution_buffer, solved, position, 0)

    solution_buffer = lax.fori_loop(0, leaf_total, retreat, solution_buffer)
    return solution_buffer[:leaf_total]


def reference(rhs_leaf, rhs_top, leaf_blocks, leaf_dinv, leaf_struct, top_blocks, top_dinv):
    def shaped(array):
        return array.reshape((TOPS, LEAF) + array.shape[1:])

    keep = top_structure(TOPS)
    forward_leaf, leaf_updates = jax.vmap(partial(leaf_forward, TOPS))(shaped(rhs_leaf), shaped(leaf_blocks), shaped(leaf_dinv), shaped(leaf_struct))
    top_source = rhs_top - jnp.sum(leaf_updates, axis=0)

    def forward_turn(turn, buffer):
        keep_row = lax.dynamic_index_in_dim(keep, turn, 0, False)
        block_row = lax.dynamic_index_in_dim(top_blocks, turn, 0, False) * keep_row[:, None, None]
        pulled = jnp.einsum("jck,jik->ci", buffer, block_row, precision=highest)
        source = lax.dynamic_index_in_dim(top_source, turn, 0, False) - pulled
        solved = jnp.einsum("ck,ik->ci", source, lax.dynamic_index_in_dim(top_dinv, turn, 0, False), precision=highest)
        return lax.dynamic_update_index_in_dim(buffer, solved, turn, 0)

    forward_top = lax.fori_loop(0, TOPS, forward_turn, jnp.zeros(rhs_top.shape, jnp.float32))

    def backward_turn(offset, buffer):
        turn = TOPS - 1 - offset
        keep_col = lax.dynamic_index_in_dim(keep, turn, 1, False)
        block_col = lax.dynamic_index_in_dim(top_blocks, turn, 1, False) * keep_col[:, None, None]
        pushed = jnp.einsum("jci,jik->ck", buffer, block_col, precision=highest)
        source = lax.dynamic_index_in_dim(forward_top, turn, 0, False) - pushed
        solved = jnp.einsum("ci,ik->ck", source, lax.dynamic_index_in_dim(top_dinv, turn, 0, False), precision=highest)
        return lax.dynamic_update_index_in_dim(buffer, solved, turn, 0)

    top_solution = lax.fori_loop(0, TOPS, backward_turn, jnp.zeros(rhs_top.shape, jnp.float32))
    leaf_solution = jax.vmap(leaf_backward, in_axes=(0, 0, 0, 0, None))(forward_leaf, shaped(leaf_blocks), shaped(leaf_dinv), shaped(leaf_struct), top_solution)
    return leaf_solution.reshape(rhs_leaf.shape), top_solution
```

```python
import functools

import jax
import jax.numpy as jnp
import numpy as np
from jax import lax
from jax.experimental import pallas as pl
from jax.experimental.pallas import tpu as pltpu
from jax.sharding import Mesh
from jax.sharding import PartitionSpec as P

CHUNKS = 4
f32 = jnp.float32
bf16 = jnp.bfloat16
SMEM = pl.BlockSpec(memory_space=pltpu.SMEM)
VMEM = pl.BlockSpec(memory_space=pltpu.VMEM)


def params():
    return pltpu.CompilerParams(vmem_limit_bytes=40 * 2**20)


def split(value):
    high = value.astype(bf16)
    return high, (value - high.astype(f32)).astype(bf16)


def product(left, right, transposed):
    dims = (((1,), (1 if transposed else 0,)), ((), ()))

    def dot(a, b):
        return lax.dot_general(a, b, dims, preferred_element_type=f32)

    return dot(left[0], right[0]) + (dot(left[1], right[0]) + dot(left[0], right[1]))


def ancestors_of(tops):
    def level(t):
        return ((t + 1) & -(t + 1)).bit_length() - 1

    return [[t for t in range(j + 1, tops) if t + 1 - 2 ** level(t) <= j] for j in range(tops)]


def paths_of(subtrees, above):
    return [[4 * (d // 4)] + above[4 * (d // 4)] for d in range(subtrees)]


def padded(rows, width):
    return np.array([row + [row[0] if row else 0] * (width - len(row)) for row in rows], np.int32)


def forward_kernel(base, first, last, width, *refs):
    meta, pieces, rhs = refs[0], refs[1:5], refs[5]
    refs = refs[6:]
    if not first:
        acc_in, refs = refs[0], refs[1:]
    acc, high, low, scaled, refs = refs[0], refs[1], refs[2], refs[3], refs[4:]
    if last:
        payload, refs = refs[0], refs[1:]
    full = refs[0]
    steps, rows = rhs.shape[0], pieces[0].shape[2]
    leafs = steps * CHUNKS
    wide = full.shape[2]
    for place, piece in enumerate(pieces):
        offset = pl.multiple_of(meta[3 * leafs + place] * rows, rows)
        full[:, :, pl.ds(offset, rows), :] = piece[...]
    if first:
        acc[...] = jnp.zeros_like(acc)
    else:
        acc[...] = acc_in[...]
    for s in range(steps):
        blocks = split(full[s, 0:3].reshape(3 * wide, wide))
        merged = split(product(blocks, split(full[s, 3]), False))
        high[s] = merged[0]
        low[s] = merged[1]
    for s in range(steps):
        source = split(rhs[s] - acc[base + s])
        outgoing = product(source, (high[s], low[s]), True)
        for r in range(3):
            target = meta[3 * (base + s) + r]
            acc[target] = acc[target] + outgoing[:, r * wide : (r + 1) * wide]
        inverse = split(full[s, 3])
        solved = split(product(source, inverse, True))
        scaled[s] = product(solved, inverse, False)
    if last:
        peers, part = payload.shape[0], payload.shape[2]
        groups = rhs.shape[1] // part
        for i in range(width):
            node = acc[leafs + meta[3 * leafs + 4 + i]]
            for p in range(peers):
                at = (p % groups) * part
                payload[p, i] = node[at : at + part]


def backward_kernel(base, first, width, meta, high, low, scaled, state, out, z):
    steps, wide = scaled.shape[0], scaled.shape[2]
    leafs = steps * CHUNKS
    if first:
        part = state.shape[2]
        groups = scaled.shape[1] // part
        z[...] = jnp.zeros_like(z)
        for i in range(width):
            node = leafs + meta[3 * leafs + 4 + i]
            for p in range(groups):
                z[node, p * part : (p + 1) * part, :] = state[p, i]
    else:
        z[...] = state[...]
    for s in range(steps - 1, -1, -1):
        total = scaled[s]
        for r in (2, 1, 0):
            source = split(z[meta[3 * (base + s) + r]])
            at = slice(r * wide, (r + 1) * wide)
            total = total - product(source, (high[s, at], low[s, at]), False)
        z[base + s] = total
        out[s] = total


def top_prepare_kernel(top, high, low, inverse_high, inverse_low):
    count, wide = top.shape[1] - 1, top.shape[2]
    inverse = split(top[0, count])
    merged = product(split(top[0, :count].reshape(count * wide, wide)), inverse, False)
    high[0], low[0] = split(merged)
    inverse_high[0], inverse_low[0] = inverse


def top_kernel(above, paths, incoming, high, low, inverse_high, inverse_low, outgoing):
    tops, wide = len(above), high.shape[2]
    width = outgoing.shape[1] - 1
    sources = [incoming[t, width] for t in range(tops)]
    for d, path in enumerate(paths):
        for i, t in enumerate(path):
            sources[t] = sources[t] - incoming[d, i]
    scaled = []
    for j in range(tops):
        source = split(sources[j])
        count = len(above[j])
        if count:
            rows = slice(0, count * wide)
            updates = product(source, (high[j, rows], low[j, rows]), True)
            for i, t in enumerate(above[j]):
                sources[t] = sources[t] - updates[:, i * wide : (i + 1) * wide]
        inverse = (inverse_high[j], inverse_low[j])
        scaled.append(product(split(product(source, inverse, True)), inverse, False))
    solved = [None] * tops
    parts = [None] * tops
    for j in range(tops - 1, -1, -1):
        total = scaled[j]
        for i, t in enumerate(above[j]):
            rows = slice(i * wide, (i + 1) * wide)
            total = total - product(parts[t], (high[j, rows], low[j, rows]), False)
        solved[j] = total
        parts[j] = split(total)
    for p in range(outgoing.shape[0]):
        path = paths[p]
        for i in range(width):
            outgoing[p, i] = solved[path[i] if i < len(path) else path[0]]
        outgoing[p, width] = solved[p]


def local(rhs_leaf, rhs_top, leaf_blocks, leaf_dinv, leaf_struct, top_blocks, top_dinv):
    leafs, columns, wide = rhs_leaf.shape
    tops = top_blocks.shape[0]
    steps = leafs // CHUNKS
    above = ancestors_of(tops)
    most = max(len(row) for row in above)
    width = most + 1
    paths = paths_of(tops, above)
    groups = min(tops, columns // 8)
    part = columns // groups

    core, zh, zl = lax.axis_index("core"), lax.axis_index("zh"), lax.axis_index("zl")
    xy = lax.axis_index("xy")

    def swap(value):
        return lax.ppermute(value, ("core", "zh"), [(0, 0), (1, 2), (2, 1), (3, 3)])

    def other(value, axis):
        return lax.ppermute(value, axis, [(0, 1), (1, 0)])

    struct = swap(leaf_struct)
    own_top = swap(rhs_top)
    path = jnp.asarray(padded(paths, width))[2 * xy + zh]
    places = jnp.stack([2 * core + zl, 2 * core + 1 - zl, 2 - 2 * core + zl, 3 - 2 * core - zl])
    meta = jnp.concatenate([struct.reshape(-1), places.astype(jnp.int32), path])

    pieces, sides = [], []
    for k in range(CHUNKS):
        at = slice(k * steps, (k + 1) * steps)
        own = jnp.concatenate([leaf_blocks[at], leaf_dinv[at][:, None]], axis=1)
        x1 = swap(own)
        sides.append(swap(rhs_leaf[at]))
        x2 = other(x1, "zl")
        pieces.append((x1, x2, other(x1, "core"), other(x2, "core")))

    chosen = jnp.take(top_blocks[:, 0], jnp.asarray(padded(above, most))[2 * xy + core], axis=0)
    top = jnp.concatenate([chosen, top_dinv], axis=0)
    top = lax.all_gather(top, ("zh", "zl"), axis=1, tiled=True)
    top = lax.all_gather(top, ("xy", "core"), axis=0, tiled=False)
    def whole(*shape):
        return pl.BlockSpec((1,) + shape, lambda t: (t,) + (0,) * len(shape))

    top_factor = pl.pallas_call(
        top_prepare_kernel,
        grid=(tops,),
        in_specs=[whole(width, wide, wide)],
        out_specs=[whole(most * wide, wide)] * 2 + [whole(wide, wide)] * 2,
        out_shape=[jax.ShapeDtypeStruct((tops, most * wide, wide), bf16)] * 2
        + [jax.ShapeDtypeStruct((tops, wide, wide), bf16)] * 2,
        compiler_params=params(),
        name="top_prepare",
    )(top)

    vectors = jax.ShapeDtypeStruct((leafs + tops, columns, wide), f32)
    merged = jax.ShapeDtypeStruct((steps, 3 * wide, wide), bf16)
    chunk = jax.ShapeDtypeStruct((steps, columns, wide), f32)
    cost = pl.CostEstimate(flops=steps * 8 * 6 * columns * wide * wide, bytes_accessed=8 * 2**20, transcendentals=0)
    factors, state = [], None
    for k in range(CHUNKS):
        last = k == CHUNKS - 1
        shapes = [vectors, merged, merged, chunk]
        if last:
            shapes.append(jax.ShapeDtypeStruct((tops, width, part, wide), f32))
        results = pl.pallas_call(
            functools.partial(forward_kernel, k * steps, k == 0, last, width),
            in_specs=[SMEM] + [VMEM] * (5 + (k > 0)),
            out_specs=[VMEM] * len(shapes),
            out_shape=shapes,
            scratch_shapes=[pltpu.VMEM((steps, 4, wide, wide), f32)],
            compiler_params=params(),
            cost_estimate=cost,
            name="leaf_forward",
        )(meta, *pieces[k], sides[k], *(() if k == 0 else (state,)))
        state = results[0]
        factors.append(results[1:4])
    payload = results[4]

    own_rows = own_top.reshape(groups, 1, part, wide)
    own_rows = jnp.tile(own_rows, (tops // groups, 1, 1, 1))
    payload = jnp.concatenate([payload, own_rows], axis=1)
    incoming = lax.all_to_all(payload, ("xy", "zh"), split_axis=0, concat_axis=0, tiled=True)
    outgoing = pl.pallas_call(
        functools.partial(top_kernel, above, paths),
        in_specs=[VMEM] * 5,
        out_specs=VMEM,
        out_shape=jax.ShapeDtypeStruct((tops, width + 1, part, wide), f32),
        compiler_params=params(),
        name="top_solve",
    )(incoming, *top_factor)
    state = lax.all_to_all(outgoing, ("xy", "zh"), split_axis=0, concat_axis=0, tiled=True)
    top_solution = swap(state[:groups, width].reshape(1, columns, wide))

    found = [None] * CHUNKS
    for k in range(CHUNKS - 1, -1, -1):
        solved, state = pl.pallas_call(
            functools.partial(backward_kernel, k * steps, k == CHUNKS - 1, width),
            in_specs=[SMEM] + [VMEM] * 4,
            out_specs=[VMEM] * 2,
            out_shape=[chunk, vectors],
            compiler_params=params(),
            cost_estimate=cost,
            name="leaf_backward",
        )(meta, *factors[k], state)
        found[k] = swap(solved)
    return (jnp.concatenate(found, axis=0), top_solution)


def solution(mesh):
    subtrees, quarters = mesh.devices.shape
    fine = Mesh(
        mesh.devices.reshape(subtrees // 2, 2, 2, quarters // 2), ("xy", "core", "zh", "zl")
    )
    sn, rhs = ("xy", "core"), ("zh", "zl")
    return jax.shard_map(
        local,
        mesh=fine,
        in_specs=(
            P(sn, rhs, None),
            P(sn, rhs, None),
            P(sn, None, rhs, None),
            P(sn, rhs, None),
            P(sn, None),
            P(None, sn, rhs, None),
            P(sn, rhs, None),
        ),
        out_specs=(P(sn, rhs, None), P(sn, rhs, None)),
        check_vma=False,
    )
```

```python
import functools

import jax
import jax.numpy as jnp
import numpy as np
from jax import lax
from jax.experimental import pallas as pl
from jax.experimental.pallas import tpu as pltpu
from jax.sharding import Mesh
from jax.sharding import PartitionSpec as P

CHUNKS = 4
f32 = jnp.float32
bf16 = jnp.bfloat16
SMEM = pl.BlockSpec(memory_space=pltpu.SMEM)
VMEM = pl.BlockSpec(memory_space=pltpu.VMEM)


def params():
    return pltpu.CompilerParams(vmem_limit_bytes=40 * 2**20)


def split(value):
    high = value.astype(bf16)
    return high, (value - high.astype(f32)).astype(bf16)


def product(left, right, transposed):
    dims = (((1,), (1 if transposed else 0,)), ((), ()))

    def dot(a, b):
        return lax.dot_general(a, b, dims, preferred_element_type=f32)

    return dot(left[0], right[0]) + (dot(left[1], right[0]) + dot(left[0], right[1]))


def ancestors_of(tops):
    def level(t):
        return ((t + 1) & -(t + 1)).bit_length() - 1

    return [[t for t in range(j + 1, tops) if t + 1 - 2 ** level(t) <= j] for j in range(tops)]


def paths_of(subtrees, above):
    return [[4 * (d // 4)] + above[4 * (d // 4)] for d in range(subtrees)]


def padded(rows, width):
    return np.array([row + [row[0] if row else 0] * (width - len(row)) for row in rows], np.int32)


def forward_kernel(base, first, last, width, *refs):
    meta, pieces, sides = refs[0], refs[1:5], refs[5]
    refs = refs[6:]
    if not first:
        acc_in, refs = refs[0], refs[1:]
    acc, high, low, scaled, refs = refs[0], refs[1], refs[2], refs[3], refs[4:]
    if last:
        payload, refs = refs[0], refs[1:]
    full = refs[0]
    steps, columns, rows = scaled.shape[0], scaled.shape[1], pieces[0].shape[2]
    leafs = steps * CHUNKS
    wide = full.shape[2]
    for place, piece in enumerate(pieces):
        offset = pl.multiple_of(meta[3 * leafs + place] * rows, rows)
        full[:, :, pl.ds(offset, rows), :] = piece[...]
    if first:
        acc[...] = jnp.zeros_like(acc)
    else:
        acc[...] = acc_in[...]
    for s in range(steps):
        blocks = split(full[s, 0:3].reshape(3 * wide, wide))
        merged = split(product(blocks, split(full[s, 3]), False))
        high[s] = merged[0]
        low[s] = merged[1]
    for s in range(steps):
        at = (base + s) * columns
        source = split(sides[at : at + columns] - acc[base + s])
        outgoing = product(source, (high[s], low[s]), True)
        for r in range(3):
            target = meta[3 * (base + s) + r]
            acc[target] = acc[target] + outgoing[:, r * wide : (r + 1) * wide]
        inverse = split(full[s, 3])
        solved = split(product(source, inverse, True))
        scaled[s] = product(solved, inverse, False)
    if last:
        peers, part = payload.shape[0], payload.shape[2]
        groups = columns // part
        for i in range(width + 1):
            if i < width:
                node = acc[leafs + meta[3 * leafs + 4 + i]]
            else:
                node = sides[leafs * columns : (leafs + 1) * columns]
            for p in range(peers):
                at = (p % groups) * part
                payload[p, i] = node[at : at + part]


def backward_kernel(base, first, width, meta, high, low, scaled, state, out, z):
    steps, wide = scaled.shape[0], scaled.shape[2]
    leafs = steps * CHUNKS
    if first:
        part = state.shape[2]
        groups = scaled.shape[1] // part
        z[...] = jnp.zeros_like(z)
        for i in range(width):
            node = leafs + meta[3 * leafs + 4 + i]
            for p in range(groups):
                z[node, p * part : (p + 1) * part, :] = state[p, i]
    else:
        z[...] = state[...]
    for s in range(steps - 1, -1, -1):
        total = scaled[s]
        for r in (2, 1, 0):
            source = split(z[meta[3 * (base + s) + r]])
            at = slice(r * wide, (r + 1) * wide)
            total = total - product(source, (high[s, at], low[s, at]), False)
        z[base + s] = total
        out[s] = total


def top_prepare_kernel(meta, top, high, low, inverse_high, inverse_low, full):
    blocks, rows, wide = top.shape[2], top.shape[3], top.shape[4]
    for place in range(top.shape[1]):
        offset = pl.multiple_of(meta[place] * rows, rows)
        full[:, pl.ds(offset, rows), :] = top[0, place]
    inverse = split(full[blocks - 1])
    merged = product(split(full[: blocks - 1].reshape((blocks - 1) * wide, wide)), inverse, False)
    high[0], low[0] = split(merged)
    inverse_high[0], inverse_low[0] = inverse


def top_kernel(above, paths, incoming, high, low, inverse_high, inverse_low, outgoing):
    tops, wide = len(above), high.shape[2]
    width = outgoing.shape[1] - 1
    sources = [incoming[t, width] for t in range(tops)]
    for d, path in enumerate(paths):
        for i, t in enumerate(path):
            sources[t] = sources[t] - incoming[d, i]
    scaled = []
    for j in range(tops):
        source = split(sources[j])
        count = len(above[j])
        if count:
            rows = slice(0, count * wide)
            updates = product(source, (high[j, rows], low[j, rows]), True)
            for i, t in enumerate(above[j]):
                sources[t] = sources[t] - updates[:, i * wide : (i + 1) * wide]
        inverse = (inverse_high[j], inverse_low[j])
        scaled.append(product(split(product(source, inverse, True)), inverse, False))
    solved = [None] * tops
    parts = [None] * tops
    for j in range(tops - 1, -1, -1):
        total = scaled[j]
        for i, t in enumerate(above[j]):
            rows = slice(i * wide, (i + 1) * wide)
            total = total - product(parts[t], (high[j, rows], low[j, rows]), False)
        solved[j] = total
        parts[j] = split(total)
    for p in range(outgoing.shape[0]):
        path = paths[p]
        for i in range(width):
            outgoing[p, i] = solved[path[i] if i < len(path) else path[0]]
        outgoing[p, width] = solved[p]


def local(rhs_leaf, rhs_top, leaf_blocks, leaf_dinv, leaf_struct, top_blocks, top_dinv):
    leafs, columns, wide = rhs_leaf.shape
    tops = top_blocks.shape[0]
    steps = leafs // CHUNKS
    above = ancestors_of(tops)
    most = max(len(row) for row in above)
    width = most + 1
    paths = paths_of(tops, above)
    groups = min(tops, columns // 8)
    part = columns // groups

    core, zh, zl = lax.axis_index("core"), lax.axis_index("zh"), lax.axis_index("zl")
    xy = lax.axis_index("xy")

    def swap(value):
        return lax.ppermute(value, ("core", "zh"), [(0, 0), (1, 2), (2, 1), (3, 3)])

    def other(value, axis):
        return lax.ppermute(value, axis, [(0, 1), (1, 0)])

    def after(first, value):
        return lax.optimization_barrier((first, value))

    own = []
    for k in range(CHUNKS):
        at = slice(k * steps, (k + 1) * steps)
        own.append(jnp.concatenate([leaf_blocks[at], leaf_dinv[at][:, None]], axis=1))
    names = jnp.zeros((8, wide), f32).at[:3, :leafs].set(leaf_struct.T.astype(f32))
    sides = jnp.concatenate([rhs_leaf.reshape(-1, wide), rhs_top.reshape(-1, wide), names], axis=0)

    swapped = [swap(own[0]), swap(own[1])]
    swapped[0], sides = after(swapped[0], sides)
    sides = swap(sides)
    swapped[1], own[2] = after(swapped[1], own[2])
    swapped.append(swap(own[2]))
    sides, own[3] = after(sides, own[3])
    swapped.append(swap(own[3]))

    chosen = jnp.take(top_blocks[:, 0], jnp.asarray(padded(above, most))[2 * xy + core], axis=0)
    top = jnp.concatenate([chosen, top_dinv], axis=0)
    top = jnp.stack([top, other(top, "zh")])
    top = jnp.concatenate([top, other(top, "zl")])
    top = lax.all_gather(top, ("xy", "core"), axis=0, tiled=False)

    pieces = []
    for x1 in swapped:
        x2 = other(x1, "zl")
        pieces.append((x1, x2, other(x1, "core"), other(x2, "core")))

    names = sides[(leafs + 1) * columns :][:3, :leafs].T.astype(jnp.int32).reshape(-1)
    path = jnp.asarray(padded(paths, width))[2 * xy + zh]
    places = jnp.stack([2 * core + zl, 2 * core + 1 - zl, 2 - 2 * core + zl, 3 - 2 * core - zl])
    meta = jnp.concatenate([names, places.astype(jnp.int32), path])

    def whole(*shape):
        return pl.BlockSpec((1,) + shape, lambda t: (t,) + (0,) * len(shape))

    top_places = jnp.stack([2 * zh + zl, 2 - 2 * zh + zl, 2 * zh + 1 - zl, 3 - 2 * zh - zl])
    top_factor = pl.pallas_call(
        top_prepare_kernel,
        grid=(tops,),
        in_specs=[SMEM, whole(*top.shape[1:])],
        out_specs=[whole(most * wide, wide)] * 2 + [whole(wide, wide)] * 2,
        out_shape=[jax.ShapeDtypeStruct((tops, most * wide, wide), bf16)] * 2
        + [jax.ShapeDtypeStruct((tops, wide, wide), bf16)] * 2,
        scratch_shapes=[pltpu.VMEM((width, wide, wide), f32)],
        compiler_params=params(),
        name="top_prepare",
    )(top_places.astype(jnp.int32), top)

    vectors = jax.ShapeDtypeStruct((leafs + tops, columns, wide), f32)
    merged = jax.ShapeDtypeStruct((steps, 3 * wide, wide), bf16)
    chunk = jax.ShapeDtypeStruct((steps, columns, wide), f32)
    cost = pl.CostEstimate(flops=4 * 10**9, bytes_accessed=8 * 2**20, transcendentals=0)
    factors, state = [], None
    for k in range(CHUNKS):
        last = k == CHUNKS - 1
        shapes = [vectors, merged, merged, chunk]
        if last:
            shapes.append(jax.ShapeDtypeStruct((tops, width + 1, part, wide), f32))
            top_factor, state = after(top_factor, state)
        results = pl.pallas_call(
            functools.partial(forward_kernel, k * steps, k == 0, last, width),
            in_specs=[SMEM] + [VMEM] * (5 + (k > 0)),
            out_specs=[VMEM] * len(shapes),
            out_shape=shapes,
            scratch_shapes=[pltpu.VMEM((steps, 4, wide, wide), f32)],
            compiler_params=params(),
            cost_estimate=cost,
            name="leaf_forward",
        )(meta, *pieces[k], sides, *(() if k == 0 else (state,)))
        state = results[0]
        factors.append(results[1:4])

    incoming = lax.all_to_all(results[4], ("xy", "zh"), split_axis=0, concat_axis=0, tiled=True)
    outgoing = pl.pallas_call(
        functools.partial(top_kernel, above, paths),
        in_specs=[VMEM] * 5,
        out_specs=VMEM,
        out_shape=jax.ShapeDtypeStruct((tops, width + 1, part, wide), f32),
        compiler_params=params(),
        name="top_solve",
    )(incoming, *top_factor)
    state = lax.all_to_all(outgoing, ("xy", "zh"), split_axis=0, concat_axis=0, tiled=True)
    own_top = state[:groups, width].reshape(1, columns, wide)

    found = [None] * CHUNKS
    for k in range(CHUNKS - 1, -1, -1):
        found[k], state = pl.pallas_call(
            functools.partial(backward_kernel, k * steps, k == CHUNKS - 1, width),
            in_specs=[SMEM] + [VMEM] * 4,
            out_specs=[VMEM] * 2,
            out_shape=[chunk, vectors],
            compiler_params=params(),
            cost_estimate=cost,
            name="leaf_backward",
        )(meta, *factors[k], state)
    half = CHUNKS // 2
    late = swap(jnp.concatenate(found[half:] + [own_top], axis=0))
    early = swap(jnp.concatenate(found[:half], axis=0))
    leaf_solution = jnp.concatenate([early, late[:-1]], axis=0)
    return (leaf_solution, late[-1:])


def solution(mesh):
    subtrees, quarters = mesh.devices.shape
    fine = Mesh(
        mesh.devices.reshape(subtrees // 2, 2, 2, quarters // 2), ("xy", "core", "zh", "zl")
    )
    sn, rhs = ("xy", "core"), ("zh", "zl")
    return jax.shard_map(
        local,
        mesh=fine,
        in_specs=(
            P(sn, rhs, None),
            P(sn, rhs, None),
            P(sn, None, rhs, None),
            P(sn, rhs, None),
            P(sn, None),
            P(None, sn, rhs, None),
            P(sn, rhs, None),
        ),
        out_specs=(P(sn, rhs, None), P(sn, rhs, None)),
        check_vma=False,
    )
```

```python
import functools

import jax
import jax.numpy as jnp
import numpy as np
from jax import lax
from jax.experimental import pallas as pl
from jax.experimental.pallas import tpu as pltpu
from jax.sharding import Mesh
from jax.sharding import PartitionSpec as P

CHUNKS = 4
f32 = jnp.float32
bf16 = jnp.bfloat16
SMEM = pl.BlockSpec(memory_space=pltpu.SMEM)
VMEM = pl.BlockSpec(memory_space=pltpu.VMEM)


def params():
    return pltpu.CompilerParams(vmem_limit_bytes=40 * 2**20)


def split(value):
    high = value.astype(bf16)
    return high, (value - high.astype(f32)).astype(bf16)


def product(left, right, transposed):
    dims = (((1,), (1 if transposed else 0,)), ((), ()))

    def dot(a, b):
        return lax.dot_general(a, b, dims, preferred_element_type=f32)

    return dot(left[0], right[0]) + (dot(left[1], right[0]) + dot(left[0], right[1]))


def ancestors_of(tops):
    def level(t):
        return ((t + 1) & -(t + 1)).bit_length() - 1

    return [[t for t in range(j + 1, tops) if t + 1 - 2 ** level(t) <= j] for j in range(tops)]


def paths_of(subtrees, above):
    return [[4 * (d // 4)] + above[4 * (d // 4)] for d in range(subtrees)]


def padded(rows, width):
    return np.array([row + [row[0] if row else 0] * (width - len(row)) for row in rows], np.int32)


def forward_kernel(base, first, last, width, *refs):
    meta, pieces, sides = refs[0], refs[1:5], refs[5]
    refs = refs[6:]
    if not first:
        acc_in, refs = refs[0], refs[1:]
    acc, high, low, scaled, refs = refs[0], refs[1], refs[2], refs[3], refs[4:]
    if last:
        payload, refs = refs[0], refs[1:]
    full = refs[0]
    steps, columns, rows = scaled.shape[0], scaled.shape[1], pieces[0].shape[2]
    leafs = steps * CHUNKS
    wide = full.shape[2]
    for place, piece in enumerate(pieces):
        offset = pl.multiple_of(meta[3 * leafs + place] * rows, rows)
        full[:, :, pl.ds(offset, rows), :] = piece[...]
    if first:
        acc[...] = jnp.zeros_like(acc)
    else:
        acc[...] = acc_in[...]
    for s in range(steps):
        blocks = split(full[s, 0:3].reshape(3 * wide, wide))
        merged = split(product(blocks, split(full[s, 3]), False))
        high[s] = merged[0]
        low[s] = merged[1]
    for s in range(steps):
        at = (base + s) * columns
        source = split(sides[at : at + columns] - acc[base + s])
        outgoing = product(source, (high[s], low[s]), True)
        for r in range(3):
            target = meta[3 * (base + s) + r]
            acc[target] = acc[target] + outgoing[:, r * wide : (r + 1) * wide]
        inverse = split(full[s, 3])
        solved = split(product(source, inverse, True))
        scaled[s] = product(solved, inverse, False)
    if last:
        peers, part = payload.shape[0], payload.shape[2]
        groups = columns // part
        for i in range(width + 1):
            if i < width:
                node = acc[leafs + meta[3 * leafs + 4 + i]]
            else:
                node = sides[leafs * columns : (leafs + 1) * columns]
            for p in range(peers):
                at = (p % groups) * part
                payload[p, i] = node[at : at + part]


def backward_kernel(base, first, width, meta, high, low, scaled, state, out, z):
    steps, wide = scaled.shape[0], scaled.shape[2]
    leafs = steps * CHUNKS
    if first:
        part = state.shape[2]
        groups = scaled.shape[1] // part
        z[...] = jnp.zeros_like(z)
        for i in range(width):
            node = leafs + meta[3 * leafs + 4 + i]
            for p in range(groups):
                z[node, p * part : (p + 1) * part, :] = state[p, i]
    else:
        z[...] = state[...]
    for s in range(steps - 1, -1, -1):
        total = scaled[s]
        for r in (2, 1, 0):
            source = split(z[meta[3 * (base + s) + r]])
            at = slice(r * wide, (r + 1) * wide)
            total = total - product(source, (high[s, at], low[s, at]), False)
        z[base + s] = total
        out[s] = total


def top_prepare_kernel(meta, top, high, low, inverse_high, inverse_low, full):
    blocks, rows, wide = top.shape[2], top.shape[3], top.shape[4]
    for place in range(top.shape[1]):
        offset = pl.multiple_of(meta[place] * rows, rows)
        full[:, pl.ds(offset, rows), :] = top[0, place]
    inverse = split(full[blocks - 1])
    merged = product(split(full[: blocks - 1].reshape((blocks - 1) * wide, wide)), inverse, False)
    high[0], low[0] = split(merged)
    inverse_high[0], inverse_low[0] = inverse


def top_kernel(above, paths, incoming, high, low, inverse_high, inverse_low, outgoing):
    tops, wide = len(above), high.shape[2]
    width = outgoing.shape[1] - 1
    sources = [incoming[t, width] for t in range(tops)]
    for d, path in enumerate(paths):
        for i, t in enumerate(path):
            sources[t] = sources[t] - incoming[d, i]
    scaled = []
    for j in range(tops):
        source = split(sources[j])
        count = len(above[j])
        if count:
            rows = slice(0, count * wide)
            updates = product(source, (high[j, rows], low[j, rows]), True)
            for i, t in enumerate(above[j]):
                sources[t] = sources[t] - updates[:, i * wide : (i + 1) * wide]
        inverse = (inverse_high[j], inverse_low[j])
        scaled.append(product(split(product(source, inverse, True)), inverse, False))
    solved = [None] * tops
    parts = [None] * tops
    for j in range(tops - 1, -1, -1):
        total = scaled[j]
        for i, t in enumerate(above[j]):
            rows = slice(i * wide, (i + 1) * wide)
            total = total - product(parts[t], (high[j, rows], low[j, rows]), False)
        solved[j] = total
        parts[j] = split(total)
    for p in range(outgoing.shape[0]):
        path = paths[p]
        for i in range(width):
            outgoing[p, i] = solved[path[i] if i < len(path) else path[0]]
        outgoing[p, width] = solved[p]


def local(rhs_leaf, rhs_top, leaf_blocks, leaf_dinv, leaf_struct, top_blocks, top_dinv):
    leafs, columns, wide = rhs_leaf.shape
    tops = top_blocks.shape[0]
    steps = leafs // CHUNKS
    above = ancestors_of(tops)
    most = max(len(row) for row in above)
    width = most + 1
    paths = paths_of(tops, above)
    groups = min(tops, columns // 8)
    part = columns // groups

    core, zh, zl = lax.axis_index("core"), lax.axis_index("zh"), lax.axis_index("zl")
    xy = lax.axis_index("xy")

    def swap(value):
        return lax.ppermute(value, ("core", "zh"), [(0, 0), (1, 2), (2, 1), (3, 3)])

    def other(value, axis):
        return lax.ppermute(value, axis, [(0, 1), (1, 0)])

    def after(first, value):
        return lax.optimization_barrier((first, value))[1]

    own = []
    for k in range(CHUNKS):
        at = slice(k * steps, (k + 1) * steps)
        own.append(jnp.concatenate([leaf_blocks[at], leaf_dinv[at][:, None]], axis=1))
    names = jnp.zeros((8, wide), f32).at[:3, :leafs].set(leaf_struct.T.astype(f32))
    sides = jnp.concatenate([rhs_leaf.reshape(-1, wide), rhs_top.reshape(-1, wide), names], axis=0)

    swapped = [swap(own[0])]
    sides = swap(sides)
    swapped.append(swap(after(swapped[0], own[1])))
    swapped.append(swap(after(sides, own[2])))
    swapped.append(swap(after(swapped[1], own[3])))

    chosen = jnp.take(top_blocks[:, 0], jnp.asarray(padded(above, most))[2 * xy + core], axis=0)
    top = after(swapped[1], jnp.concatenate([chosen, top_dinv], axis=0))
    top = jnp.stack([top, other(top, "zh")])
    top = jnp.concatenate([top, other(top, "zl")])
    top = lax.all_gather(top, ("xy", "core"), axis=0, tiled=False)

    names = sides[(leafs + 1) * columns :][:3, :leafs].T.astype(jnp.int32).reshape(-1)
    path = jnp.asarray(padded(paths, width))[2 * xy + zh]
    places = jnp.stack([2 * core + zl, 2 * core + 1 - zl, 2 - 2 * core + zl, 3 - 2 * core - zl])
    meta = jnp.concatenate([names, places.astype(jnp.int32), path])

    def whole(*shape):
        return pl.BlockSpec((1,) + shape, lambda t: (t,) + (0,) * len(shape))

    top_places = jnp.stack([2 * zh + zl, 2 - 2 * zh + zl, 2 * zh + 1 - zl, 3 - 2 * zh - zl])
    top_factor = pl.pallas_call(
        top_prepare_kernel,
        grid=(tops,),
        in_specs=[SMEM, whole(*top.shape[1:])],
        out_specs=[whole(most * wide, wide)] * 2 + [whole(wide, wide)] * 2,
        out_shape=[jax.ShapeDtypeStruct((tops, most * wide, wide), bf16)] * 2
        + [jax.ShapeDtypeStruct((tops, wide, wide), bf16)] * 2,
        scratch_shapes=[pltpu.VMEM((width, wide, wide), f32)],
        compiler_params=params(),
        name="top_prepare",
    )(top_places.astype(jnp.int32), top)

    vectors = jax.ShapeDtypeStruct((leafs + tops, columns, wide), f32)
    merged = jax.ShapeDtypeStruct((steps, 3 * wide, wide), bf16)
    chunk = jax.ShapeDtypeStruct((steps, columns, wide), f32)
    cost = pl.CostEstimate(flops=4 * 10**9, bytes_accessed=8 * 2**20, transcendentals=0)
    factors, state = [], None
    for k in range(CHUNKS):
        last = k == CHUNKS - 1
        shapes = [vectors, merged, merged, chunk]
        x1 = swapped[k] if k < 2 else after(earlier, swapped[k])
        x2 = other(x1, "zl")
        x3 = other(after(state, x1) if last else x1, "core")
        pieces = (x1, x2, x3, other(x2, "core"))
        earlier = state
        if last:
            shapes.append(jax.ShapeDtypeStruct((tops, width + 1, part, wide), f32))
        if k == CHUNKS - 2:
            state = after(top_factor, state)
        results = pl.pallas_call(
            functools.partial(forward_kernel, k * steps, k == 0, last, width),
            in_specs=[SMEM] + [VMEM] * (5 + (k > 0)),
            out_specs=[VMEM] * len(shapes),
            out_shape=shapes,
            scratch_shapes=[pltpu.VMEM((steps, 4, wide, wide), f32)],
            compiler_params=params(),
            cost_estimate=cost,
            name="leaf_forward",
        )(meta, *pieces, sides, *(() if k == 0 else (state,)))
        state = results[0]
        factors.append(results[1:4])

    incoming = lax.all_to_all(results[4], ("xy", "zh"), split_axis=0, concat_axis=0, tiled=True)
    outgoing = pl.pallas_call(
        functools.partial(top_kernel, above, paths),
        in_specs=[VMEM] * 5,
        out_specs=VMEM,
        out_shape=jax.ShapeDtypeStruct((tops, width + 1, part, wide), f32),
        compiler_params=params(),
        name="top_solve",
    )(incoming, *top_factor)
    state = lax.all_to_all(outgoing, ("xy", "zh"), split_axis=0, concat_axis=0, tiled=True)
    own_top = state[:groups, width].reshape(1, columns, wide)

    found = [None] * CHUNKS
    for k in range(CHUNKS - 1, -1, -1):
        found[k], state = pl.pallas_call(
            functools.partial(backward_kernel, k * steps, k == CHUNKS - 1, width),
            in_specs=[SMEM] + [VMEM] * 4,
            out_specs=[VMEM] * 2,
            out_shape=[chunk, vectors],
            compiler_params=params(),
            cost_estimate=cost,
            name="leaf_backward",
        )(meta, *factors[k], state)
    late = swap(found[-1])
    middle = swap(jnp.concatenate(found[1:-1] + [own_top], axis=0))
    early = swap(after(late, found[0]))
    leaf_solution = jnp.concatenate([early, middle[:-1], late], axis=0)
    return (leaf_solution, middle[-1:])


def solution(mesh):
    subtrees, quarters = mesh.devices.shape
    fine = Mesh(
        mesh.devices.reshape(subtrees // 2, 2, 2, quarters // 2), ("xy", "core", "zh", "zl")
    )
    sn, rhs = ("xy", "core"), ("zh", "zl")
    return jax.shard_map(
        local,
        mesh=fine,
        in_specs=(
            P(sn, rhs, None),
            P(sn, rhs, None),
            P(sn, None, rhs, None),
            P(sn, rhs, None),
            P(sn, None),
            P(None, sn, rhs, None),
            P(sn, rhs, None),
        ),
        out_specs=(P(sn, rhs, None), P(sn, rhs, None)),
        check_vma=False,
    )
```

```python
import functools

import jax
import jax.numpy as jnp
import numpy as np
from jax import lax
from jax.experimental import pallas as pl
from jax.experimental.pallas import tpu as pltpu
from jax.sharding import Mesh
from jax.sharding import PartitionSpec as P

CHUNKS = 4
f32 = jnp.float32
bf16 = jnp.bfloat16
SMEM = pl.BlockSpec(memory_space=pltpu.SMEM)
VMEM = pl.BlockSpec(memory_space=pltpu.VMEM)


def params():
    return pltpu.CompilerParams(vmem_limit_bytes=40 * 2**20)


def split(value):
    high = value.astype(bf16)
    return high, (value - high.astype(f32)).astype(bf16)


def product(left, right, transposed):
    dims = (((1,), (1 if transposed else 0,)), ((), ()))

    def dot(a, b):
        return lax.dot_general(a, b, dims, preferred_element_type=f32)

    return dot(left[0], right[0]) + (dot(left[1], right[0]) + dot(left[0], right[1]))


def ancestors_of(tops):
    def level(t):
        return ((t + 1) & -(t + 1)).bit_length() - 1

    return [[t for t in range(j + 1, tops) if t + 1 - 2 ** level(t) <= j] for j in range(tops)]


def paths_of(subtrees, above):
    return [[4 * (d // 4)] + above[4 * (d // 4)] for d in range(subtrees)]


def padded(rows, width):
    return np.array([row + [row[0] if row else 0] * (width - len(row)) for row in rows], np.int32)


def forward_kernel(base, first, last, width, *refs):
    meta, pieces, sides = refs[0], refs[1:5], refs[5]
    refs = refs[6:]
    if not first:
        acc_in, refs = refs[0], refs[1:]
    acc, high, low, scaled, refs = refs[0], refs[1], refs[2], refs[3], refs[4:]
    if last:
        payload, refs = refs[0], refs[1:]
    full = refs[0]
    steps, columns, rows = scaled.shape[0], scaled.shape[1], pieces[0].shape[2]
    leafs = steps * CHUNKS
    wide = full.shape[2]
    for place, piece in enumerate(pieces):
        offset = pl.multiple_of(meta[3 * leafs + place] * rows, rows)
        full[:, :, pl.ds(offset, rows), :] = piece[...]
    if first:
        acc[...] = jnp.zeros_like(acc)
    else:
        acc[...] = acc_in[...]
    for s in range(steps):
        blocks = split(full[s, 0:3].reshape(3 * wide, wide))
        merged = split(product(blocks, split(full[s, 3]), False))
        high[s] = merged[0]
        low[s] = merged[1]
    for s in range(steps):
        at = (base + s) * columns
        source = split(sides[at : at + columns] - acc[base + s])
        outgoing = product(source, (high[s], low[s]), True)
        for r in range(3):
            target = meta[3 * (base + s) + r]
            acc[target] = acc[target] + outgoing[:, r * wide : (r + 1) * wide]
        inverse = split(full[s, 3])
        solved = split(product(source, inverse, True))
        scaled[s] = product(solved, inverse, False)
    if last:
        peers, part = payload.shape[0], payload.shape[2]
        groups = columns // part
        for i in range(width + 1):
            if i < width:
                node = acc[leafs + meta[3 * leafs + 4 + i]]
            else:
                node = sides[leafs * columns : (leafs + 1) * columns]
            for p in range(peers):
                at = (p % groups) * part
                payload[p, i] = node[at : at + part]


def backward_kernel(base, first, width, meta, high, low, scaled, state, out, z):
    steps, wide = scaled.shape[0], scaled.shape[2]
    leafs = steps * CHUNKS
    if first:
        part = state.shape[2]
        groups = scaled.shape[1] // part
        z[...] = jnp.zeros_like(z)
        for i in range(width):
            node = leafs + meta[3 * leafs + 4 + i]
            for p in range(groups):
                z[node, p * part : (p + 1) * part, :] = state[p, i]
    else:
        z[...] = state[...]
    for s in range(steps - 1, -1, -1):
        total = scaled[s]
        for r in (2, 1, 0):
            source = split(z[meta[3 * (base + s) + r]])
            at = slice(r * wide, (r + 1) * wide)
            total = total - product(source, (high[s, at], low[s, at]), False)
        z[base + s] = total
        out[s] = total


def top_prepare_kernel(meta, top, high, low, inverse_high, inverse_low, full):
    blocks, rows, wide = top.shape[2], top.shape[3], top.shape[4]
    for place in range(top.shape[1]):
        offset = pl.multiple_of(meta[place] * rows, rows)
        full[:, pl.ds(offset, rows), :] = top[0, place]
    inverse = split(full[blocks - 1])
    merged = product(split(full[: blocks - 1].reshape((blocks - 1) * wide, wide)), inverse, False)
    high[0], low[0] = split(merged)
    inverse_high[0], inverse_low[0] = inverse


def top_kernel(above, paths, incoming, high, low, inverse_high, inverse_low, outgoing):
    tops, wide = len(above), high.shape[2]
    width = outgoing.shape[1] - 1
    sources = [incoming[t, width] for t in range(tops)]
    for d, path in enumerate(paths):
        for i, t in enumerate(path):
            sources[t] = sources[t] - incoming[d, i]
    scaled = []
    for j in range(tops):
        source = split(sources[j])
        count = len(above[j])
        if count:
            rows = slice(0, count * wide)
            updates = product(source, (high[j, rows], low[j, rows]), True)
            for i, t in enumerate(above[j]):
                sources[t] = sources[t] - updates[:, i * wide : (i + 1) * wide]
        inverse = (inverse_high[j], inverse_low[j])
        scaled.append(product(split(product(source, inverse, True)), inverse, False))
    solved = [None] * tops
    parts = [None] * tops
    for j in range(tops - 1, -1, -1):
        total = scaled[j]
        for i, t in enumerate(above[j]):
            rows = slice(i * wide, (i + 1) * wide)
            total = total - product(parts[t], (high[j, rows], low[j, rows]), False)
        solved[j] = total
        parts[j] = split(total)
    for p in range(outgoing.shape[0]):
        path = paths[p]
        for i in range(width):
            outgoing[p, i] = solved[path[i] if i < len(path) else path[0]]
        outgoing[p, width] = solved[p]


def local(rhs_leaf, rhs_top, leaf_blocks, leaf_dinv, leaf_struct, top_blocks, top_dinv):
    leafs, columns, wide = rhs_leaf.shape
    tops = top_blocks.shape[0]
    steps = leafs // CHUNKS
    above = ancestors_of(tops)
    most = max(len(row) for row in above)
    width = most + 1
    paths = paths_of(tops, above)
    groups = min(tops, columns // 8)
    part = columns // groups

    core, zh, zl = lax.axis_index("core"), lax.axis_index("zh"), lax.axis_index("zl")
    xy = lax.axis_index("xy")

    def swap(value):
        return lax.ppermute(value, ("core", "zh"), [(0, 0), (1, 2), (2, 1), (3, 3)])

    def other(value, axis):
        return lax.ppermute(value, axis, [(0, 1), (1, 0)])

    def after(first, value):
        return lax.optimization_barrier((first, value))[1]

    own = []
    for k in range(CHUNKS):
        at = slice(k * steps, (k + 1) * steps)
        own.append(jnp.concatenate([leaf_blocks[at], leaf_dinv[at][:, None]], axis=1))
    names = jnp.zeros((8, wide), f32).at[:3, :leafs].set(leaf_struct.T.astype(f32))
    sides = jnp.concatenate([rhs_leaf.reshape(-1, wide), rhs_top.reshape(-1, wide), names], axis=0)

    swapped = [swap(value) for value in own]
    sides = swap(sides)
    nearby = [other(x1, "zl") for x1 in swapped]

    chosen = jnp.take(top_blocks[:, 0], jnp.asarray(padded(above, most))[2 * xy + core], axis=0)
    top = after(sides, jnp.concatenate([chosen, top_dinv], axis=0))
    top = jnp.stack([top, other(top, "zh")])
    top = jnp.concatenate([top, other(top, "zl")])
    top = lax.all_gather(top, ("xy", "core"), axis=0, tiled=False)

    names = sides[(leafs + 1) * columns :][:3, :leafs].T.astype(jnp.int32).reshape(-1)
    path = jnp.asarray(padded(paths, width))[2 * xy + zh]
    places = jnp.stack([2 * core + zl, 2 * core + 1 - zl, 2 - 2 * core + zl, 3 - 2 * core - zl])
    meta = jnp.concatenate([names, places.astype(jnp.int32), path])

    def whole(*shape):
        return pl.BlockSpec((1,) + shape, lambda t: (t,) + (0,) * len(shape))

    top_places = jnp.stack([2 * zh + zl, 2 - 2 * zh + zl, 2 * zh + 1 - zl, 3 - 2 * zh - zl])
    top_factor = pl.pallas_call(
        top_prepare_kernel,
        grid=(tops,),
        in_specs=[SMEM, whole(*top.shape[1:])],
        out_specs=[whole(most * wide, wide)] * 2 + [whole(wide, wide)] * 2,
        out_shape=[jax.ShapeDtypeStruct((tops, most * wide, wide), bf16)] * 2
        + [jax.ShapeDtypeStruct((tops, wide, wide), bf16)] * 2,
        scratch_shapes=[pltpu.VMEM((width, wide, wide), f32)],
        compiler_params=params(),
        name="top_prepare",
    )(top_places.astype(jnp.int32), top)

    vectors = jax.ShapeDtypeStruct((leafs + tops, columns, wide), f32)
    merged = jax.ShapeDtypeStruct((steps, 3 * wide, wide), bf16)
    chunk = jax.ShapeDtypeStruct((steps, columns, wide), f32)
    cost = pl.CostEstimate(flops=4 * 10**9, bytes_accessed=8 * 2**20, transcendentals=0)
    factors, state = [], None
    for k in range(CHUNKS):
        last = k == CHUNKS - 1
        shapes = [vectors, merged, merged, chunk]
        x1, x2 = after(swapped[-1], swapped[k]), after(swapped[-1], nearby[k])
        if last:
            x2 = after(state, x2)
        pieces = (x1, x2, other(x1, "core"), other(x2, "core"))
        if last:
            shapes.append(jax.ShapeDtypeStruct((tops, width + 1, part, wide), f32))
        if k == CHUNKS - 2:
            state = after(top_factor, state)
        results = pl.pallas_call(
            functools.partial(forward_kernel, k * steps, k == 0, last, width),
            in_specs=[SMEM] + [VMEM] * (5 + (k > 0)),
            out_specs=[VMEM] * len(shapes),
            out_shape=shapes,
            scratch_shapes=[pltpu.VMEM((steps, 4, wide, wide), f32)],
            compiler_params=params(),
            cost_estimate=cost,
            name="leaf_forward",
        )(meta, *pieces, sides, *(() if k == 0 else (state,)))
        state = results[0]
        factors.append(results[1:4])

    incoming = lax.all_to_all(results[4], ("xy", "zh"), split_axis=0, concat_axis=0, tiled=True)
    outgoing = pl.pallas_call(
        functools.partial(top_kernel, above, paths),
        in_specs=[VMEM] * 5,
        out_specs=VMEM,
        out_shape=jax.ShapeDtypeStruct((tops, width + 1, part, wide), f32),
        compiler_params=params(),
        name="top_solve",
    )(incoming, *top_factor)
    state = lax.all_to_all(outgoing, ("xy", "zh"), split_axis=0, concat_axis=0, tiled=True)
    own_top = state[:groups, width].reshape(1, columns, wide)

    found = [None] * CHUNKS
    for k in range(CHUNKS - 1, -1, -1):
        found[k], state = pl.pallas_call(
            functools.partial(backward_kernel, k * steps, k == CHUNKS - 1, width),
            in_specs=[SMEM] + [VMEM] * 4,
            out_specs=[VMEM] * 2,
            out_shape=[chunk, vectors],
            compiler_params=params(),
            cost_estimate=cost,
            name="leaf_backward",
        )(meta, *factors[k], state)
    late = swap(found[-1])
    middle = swap(jnp.concatenate(found[1:-1] + [own_top], axis=0))
    early = swap(after(late, found[0]))
    leaf_solution = jnp.concatenate([early, middle[:-1], late], axis=0)
    return (leaf_solution, middle[-1:])


def solution(mesh):
    subtrees, quarters = mesh.devices.shape
    fine = Mesh(
        mesh.devices.reshape(subtrees // 2, 2, 2, quarters // 2), ("xy", "core", "zh", "zl")
    )
    sn, rhs = ("xy", "core"), ("zh", "zl")
    return jax.shard_map(
        local,
        mesh=fine,
        in_specs=(
            P(sn, rhs, None),
            P(sn, rhs, None),
            P(sn, None, rhs, None),
            P(sn, rhs, None),
            P(sn, None),
            P(None, sn, rhs, None),
            P(sn, rhs, None),
        ),
        out_specs=(P(sn, rhs, None), P(sn, rhs, None)),
        check_vma=False,
    )
```

```python
import functools

import jax
import jax.numpy as jnp
import numpy as np
from jax import lax
from jax.experimental import pallas as pl
from jax.experimental.pallas import tpu as pltpu
from jax.sharding import Mesh
from jax.sharding import PartitionSpec as P

CHUNKS = 4
f32 = jnp.float32
bf16 = jnp.bfloat16
SMEM = pl.BlockSpec(memory_space=pltpu.SMEM)
VMEM = pl.BlockSpec(memory_space=pltpu.VMEM)


def params():
    return pltpu.CompilerParams(vmem_limit_bytes=40 * 2**20)


def split(value):
    high = value.astype(bf16)
    return high, (value - high.astype(f32)).astype(bf16)


def product(left, right, transposed):
    dims = (((1,), (1 if transposed else 0,)), ((), ()))

    def dot(a, b):
        return lax.dot_general(a, b, dims, preferred_element_type=f32)

    return dot(left[0], right[0]) + (dot(left[1], right[0]) + dot(left[0], right[1]))


def ancestors_of(tops):
    def level(t):
        return ((t + 1) & -(t + 1)).bit_length() - 1

    return [[t for t in range(j + 1, tops) if t + 1 - 2 ** level(t) <= j] for j in range(tops)]


def paths_of(subtrees, above):
    return [[4 * (d // 4)] + above[4 * (d // 4)] for d in range(subtrees)]


def padded(rows, width):
    return np.array([row + [row[0] if row else 0] * (width - len(row)) for row in rows], np.int32)


def forward_kernel(base, first, last, width, *refs):
    meta, pieces, sides = refs[0], refs[1:5], refs[5]
    refs = refs[6:]
    if not first:
        acc_in, refs = refs[0], refs[1:]
    acc, high, low, scaled, refs = refs[0], refs[1], refs[2], refs[3], refs[4:]
    if last:
        payload, refs = refs[0], refs[1:]
    full = refs[0]
    steps, columns, rows = scaled.shape[0], scaled.shape[1], pieces[0].shape[2]
    leafs = steps * CHUNKS
    wide = full.shape[2]
    for place, piece in enumerate(pieces):
        offset = pl.multiple_of(meta[3 * leafs + place] * rows, rows)
        full[:, :, pl.ds(offset, rows), :] = piece[...]
    if first:
        acc[...] = jnp.zeros_like(acc)
    else:
        acc[...] = acc_in[...]
    for s in range(steps):
        blocks = split(full[s, 0:3].reshape(3 * wide, wide))
        merged = split(product(blocks, split(full[s, 3]), False))
        high[s] = merged[0]
        low[s] = merged[1]
    for s in range(steps):
        at = (base + s) * columns
        source = split(sides[at : at + columns] - acc[base + s])
        outgoing = product(source, (high[s], low[s]), True)
        for r in range(3):
            target = meta[3 * (base + s) + r]
            acc[target] = acc[target] + outgoing[:, r * wide : (r + 1) * wide]
        inverse = split(full[s, 3])
        solved = split(product(source, inverse, True))
        scaled[s] = product(solved, inverse, False)
    if last:
        peers, part = payload.shape[0], payload.shape[2]
        groups = columns // part
        for i in range(width + 1):
            if i < width:
                node = acc[leafs + meta[3 * leafs + 4 + i]]
            else:
                node = sides[leafs * columns : (leafs + 1) * columns]
            for p in range(peers):
                at = (p % groups) * part
                payload[p, i] = node[at : at + part]


def backward_kernel(base, first, width, meta, high, low, scaled, state, out, z):
    steps, wide = scaled.shape[0], scaled.shape[2]
    leafs = steps * CHUNKS
    if first:
        part = state.shape[2]
        groups = scaled.shape[1] // part
        z[...] = jnp.zeros_like(z)
        for i in range(width):
            node = leafs + meta[3 * leafs + 4 + i]
            for p in range(groups):
                z[node, p * part : (p + 1) * part, :] = state[p, i]
    else:
        z[...] = state[...]
    for s in range(steps - 1, -1, -1):
        total = scaled[s]
        for r in (2, 1, 0):
            source = split(z[meta[3 * (base + s) + r]])
            at = slice(r * wide, (r + 1) * wide)
            total = total - product(source, (high[s, at], low[s, at]), False)
        z[base + s] = total
        out[s] = total


def top_prepare_kernel(meta, top, high, low, inverse_high, inverse_low, full):
    blocks, rows, wide = top.shape[2], top.shape[3], top.shape[4]
    for place in range(top.shape[1]):
        offset = pl.multiple_of(meta[place] * rows, rows)
        full[:, pl.ds(offset, rows), :] = top[0, place]
    inverse = split(full[blocks - 1])
    merged = product(split(full[: blocks - 1].reshape((blocks - 1) * wide, wide)), inverse, False)
    high[0], low[0] = split(merged)
    inverse_high[0], inverse_low[0] = inverse


def top_kernel(above, paths, incoming, high, low, inverse_high, inverse_low, outgoing):
    tops, wide = len(above), high.shape[2]
    width = outgoing.shape[1] - 1
    sources = [incoming[t, width] for t in range(tops)]
    for d, path in enumerate(paths):
        for i, t in enumerate(path):
            sources[t] = sources[t] - incoming[d, i]
    scaled = []
    for j in range(tops):
        source = split(sources[j])
        count = len(above[j])
        if count:
            rows = slice(0, count * wide)
            updates = product(source, (high[j, rows], low[j, rows]), True)
            for i, t in enumerate(above[j]):
                sources[t] = sources[t] - updates[:, i * wide : (i + 1) * wide]
        inverse = (inverse_high[j], inverse_low[j])
        scaled.append(product(split(product(source, inverse, True)), inverse, False))
    solved = [None] * tops
    parts = [None] * tops
    for j in range(tops - 1, -1, -1):
        total = scaled[j]
        for i, t in enumerate(above[j]):
            rows = slice(i * wide, (i + 1) * wide)
            total = total - product(parts[t], (high[j, rows], low[j, rows]), False)
        solved[j] = total
        parts[j] = split(total)
    for p in range(outgoing.shape[0]):
        path = paths[p]
        for i in range(width):
            outgoing[p, i] = solved[path[i] if i < len(path) else path[0]]
        outgoing[p, width] = solved[p]


def local(rhs_leaf, rhs_top, leaf_blocks, leaf_dinv, leaf_struct, top_blocks, top_dinv):
    leafs, columns, wide = rhs_leaf.shape
    tops = top_blocks.shape[0]
    steps = leafs // CHUNKS
    above = ancestors_of(tops)
    most = max(len(row) for row in above)
    width = most + 1
    paths = paths_of(tops, above)
    groups = min(tops, columns // 8)
    part = columns // groups

    core, zh, zl = lax.axis_index("core"), lax.axis_index("zh"), lax.axis_index("zl")
    xy = lax.axis_index("xy")

    def swap(value):
        return lax.ppermute(value, ("core", "zh"), [(0, 0), (1, 2), (2, 1), (3, 3)])

    def other(value, axis):
        return lax.ppermute(value, axis, [(0, 1), (1, 0)])

    def after(first, value):
        return lax.optimization_barrier((first, value))[1]

    own = []
    for k in range(CHUNKS):
        at = slice(k * steps, (k + 1) * steps)
        own.append(jnp.concatenate([leaf_blocks[at], leaf_dinv[at][:, None]], axis=1))
    names = jnp.zeros((8, wide), f32).at[:3, :leafs].set(leaf_struct.T.astype(f32))
    sides = jnp.concatenate([rhs_leaf.reshape(-1, wide), rhs_top.reshape(-1, wide), names], axis=0)

    swapped = [swap(value) for value in own]
    sides = swap(sides)
    nearby = [other(x1, "zl") for x1 in swapped]

    chosen = jnp.take(top_blocks[:, 0], jnp.asarray(padded(above, most))[2 * xy + core], axis=0)
    top = jnp.concatenate([chosen, top_dinv], axis=0)
    top = jnp.stack([top, other(top, "zh")])
    top = jnp.concatenate([top, other(top, "zl")])
    top = lax.all_gather(top, ("xy", "core"), axis=0, tiled=False)

    names = sides[(leafs + 1) * columns :][:3, :leafs].T.astype(jnp.int32).reshape(-1)
    path = jnp.asarray(padded(paths, width))[2 * xy + zh]
    places = jnp.stack([2 * core + zl, 2 * core + 1 - zl, 2 - 2 * core + zl, 3 - 2 * core - zl])
    meta = jnp.concatenate([names, places.astype(jnp.int32), path])

    def whole(*shape):
        return pl.BlockSpec((1,) + shape, lambda t: (t,) + (0,) * len(shape))

    top_places = jnp.stack([2 * zh + zl, 2 - 2 * zh + zl, 2 * zh + 1 - zl, 3 - 2 * zh - zl])
    top_factor = pl.pallas_call(
        top_prepare_kernel,
        grid=(tops,),
        in_specs=[SMEM, whole(*top.shape[1:])],
        out_specs=[whole(most * wide, wide)] * 2 + [whole(wide, wide)] * 2,
        out_shape=[jax.ShapeDtypeStruct((tops, most * wide, wide), bf16)] * 2
        + [jax.ShapeDtypeStruct((tops, wide, wide), bf16)] * 2,
        scratch_shapes=[pltpu.VMEM((width, wide, wide), f32)],
        compiler_params=params(),
        name="top_prepare",
    )(top_places.astype(jnp.int32), top)

    vectors = jax.ShapeDtypeStruct((leafs + tops, columns, wide), f32)
    merged = jax.ShapeDtypeStruct((steps, 3 * wide, wide), bf16)
    chunk = jax.ShapeDtypeStruct((steps, columns, wide), f32)
    cost = pl.CostEstimate(flops=4 * 10**9, bytes_accessed=8 * 2**20, transcendentals=0)
    factors, state = [], None
    for k in range(CHUNKS):
        last = k == CHUNKS - 1
        shapes = [vectors, merged, merged, chunk]
        x1, x2 = after(swapped[-1], swapped[k]), after(swapped[-1], nearby[k])
        if last:
            x2 = after(state, x2)
        pieces = (x1, x2, other(x1, "core"), other(x2, "core"))
        if last:
            shapes.append(jax.ShapeDtypeStruct((tops, width + 1, part, wide), f32))
        results = pl.pallas_call(
            functools.partial(forward_kernel, k * steps, k == 0, last, width),
            in_specs=[SMEM] + [VMEM] * (5 + (k > 0)),
            out_specs=[VMEM] * len(shapes),
            out_shape=shapes,
            scratch_shapes=[pltpu.VMEM((steps, 4, wide, wide), f32)],
            compiler_params=params(),
            cost_estimate=cost,
            name="leaf_forward",
        )(meta, *pieces, sides, *(() if k == 0 else (state,)))
        state = results[0]
        factors.append(results[1:4])

    incoming = lax.all_to_all(results[4], ("xy", "zh"), split_axis=0, concat_axis=0, tiled=True)
    outgoing = pl.pallas_call(
        functools.partial(top_kernel, above, paths),
        in_specs=[VMEM] * 5,
        out_specs=VMEM,
        out_shape=jax.ShapeDtypeStruct((tops, width + 1, part, wide), f32),
        compiler_params=params(),
        name="top_solve",
    )(incoming, *top_factor)
    state = lax.all_to_all(outgoing, ("xy", "zh"), split_axis=0, concat_axis=0, tiled=True)
    own_top = state[:groups, width].reshape(1, columns, wide)

    found = [None] * CHUNKS
    for k in range(CHUNKS - 1, -1, -1):
        found[k], state = pl.pallas_call(
            functools.partial(backward_kernel, k * steps, k == CHUNKS - 1, width),
            in_specs=[SMEM] + [VMEM] * 4,
            out_specs=[VMEM] * 2,
            out_shape=[chunk, vectors],
            compiler_params=params(),
            cost_estimate=cost,
            name="leaf_backward",
        )(meta, *factors[k], state)
    late = swap(found[-1])
    middle = swap(jnp.concatenate(found[1:-1] + [own_top], axis=0))
    early = swap(after(late, found[0]))
    leaf_solution = jnp.concatenate([early, middle[:-1], late], axis=0)
    return (leaf_solution, middle[-1:])


def solution(mesh):
    subtrees, quarters = mesh.devices.shape
    fine = Mesh(
        mesh.devices.reshape(subtrees // 2, 2, 2, quarters // 2), ("xy", "core", "zh", "zl")
    )
    sn, rhs = ("xy", "core"), ("zh", "zl")
    return jax.shard_map(
        local,
        mesh=fine,
        in_specs=(
            P(sn, rhs, None),
            P(sn, rhs, None),
            P(sn, None, rhs, None),
            P(sn, rhs, None),
            P(sn, None),
            P(None, sn, rhs, None),
            P(sn, rhs, None),
        ),
        out_specs=(P(sn, rhs, None), P(sn, rhs, None)),
        check_vma=False,
    )
```

```python
import functools

import jax
import jax.numpy as jnp
import numpy as np
from jax import lax
from jax.experimental import pallas as pl
from jax.experimental.pallas import tpu as pltpu
from jax.sharding import Mesh
from jax.sharding import PartitionSpec as P

CHUNKS = 4
f32 = jnp.float32
bf16 = jnp.bfloat16
SMEM = pl.BlockSpec(memory_space=pltpu.SMEM)
VMEM = pl.BlockSpec(memory_space=pltpu.VMEM)


def params():
    return pltpu.CompilerParams(vmem_limit_bytes=40 * 2**20)


def split(value):
    high = value.astype(bf16)
    return high, (value - high.astype(f32)).astype(bf16)


def product(left, right, transposed):
    dims = (((1,), (1 if transposed else 0,)), ((), ()))

    def dot(a, b):
        return lax.dot_general(a, b, dims, preferred_element_type=f32)

    return dot(left[0], right[0]) + (dot(left[1], right[0]) + dot(left[0], right[1]))


def ancestors_of(tops):
    def level(t):
        return ((t + 1) & -(t + 1)).bit_length() - 1

    return [[t for t in range(j + 1, tops) if t + 1 - 2 ** level(t) <= j] for j in range(tops)]


def paths_of(subtrees, above):
    return [[4 * (d // 4)] + above[4 * (d // 4)] for d in range(subtrees)]


def padded(rows, width):
    return np.array([row + [row[0] if row else 0] * (width - len(row)) for row in rows], np.int32)


def forward_kernel(base, first, last, width, *refs):
    meta, kept, passed, sides = refs[0], refs[1:5], refs[5:9], refs[9]
    refs = refs[10:]
    if not first:
        acc_in, refs = refs[0], refs[1:]
    acc, high, low, scaled, refs = refs[0], refs[1], refs[2], refs[3], refs[4:]
    if last:
        payload, refs = refs[0], refs[1:]
    full = refs[0]
    steps, columns, rows = scaled.shape[0], scaled.shape[1], kept[0].shape[2]
    leafs = steps * CHUNKS
    wide = full.shape[2]

    def assemble(pieces):
        for place, piece in enumerate(pieces):
            offset = pl.multiple_of(meta[3 * leafs + place] * rows, rows)
            full[:, :, pl.ds(offset, rows), :] = piece[...]

    keeps = meta[3 * leafs + 4 + width]
    pl.when(keeps == 1)(lambda: assemble(kept))
    pl.when(keeps == 0)(lambda: assemble(passed))
    if first:
        acc[...] = jnp.zeros_like(acc)
    else:
        acc[...] = acc_in[...]
    for s in range(steps):
        blocks = split(full[s, 0:3].reshape(3 * wide, wide))
        merged = split(product(blocks, split(full[s, 3]), False))
        high[s] = merged[0]
        low[s] = merged[1]
    for s in range(steps):
        at = (base + s) * columns
        source = split(sides[at : at + columns] - acc[base + s])
        outgoing = product(source, (high[s], low[s]), True)
        for r in range(3):
            target = meta[3 * (base + s) + r]
            acc[target] = acc[target] + outgoing[:, r * wide : (r + 1) * wide]
        inverse = split(full[s, 3])
        solved = split(product(source, inverse, True))
        scaled[s] = product(solved, inverse, False)
    if last:
        peers, part = payload.shape[0], payload.shape[2]
        groups = columns // part
        for i in range(width + 1):
            if i < width:
                node = acc[leafs + meta[3 * leafs + 4 + i]]
            else:
                node = sides[leafs * columns : (leafs + 1) * columns]
            for p in range(peers):
                at = (p % groups) * part
                payload[p, i] = node[at : at + part]


def backward_kernel(base, first, width, meta, high, low, scaled, state, out, z):
    steps, wide = scaled.shape[0], scaled.shape[2]
    leafs = steps * CHUNKS
    if first:
        part = state.shape[2]
        groups = scaled.shape[1] // part
        z[...] = jnp.zeros_like(z)
        for i in range(width):
            node = leafs + meta[3 * leafs + 4 + i]
            for p in range(groups):
                z[node, p * part : (p + 1) * part, :] = state[p, i]
    else:
        z[...] = state[...]
    for s in range(steps - 1, -1, -1):
        total = scaled[s]
        for r in (2, 1, 0):
            source = split(z[meta[3 * (base + s) + r]])
            at = slice(r * wide, (r + 1) * wide)
            total = total - product(source, (high[s, at], low[s, at]), False)
        z[base + s] = total
        out[s] = total


def top_prepare_kernel(meta, top, high, low, inverse_high, inverse_low, full):
    blocks, rows, wide = top.shape[2], top.shape[3], top.shape[4]
    for place in range(top.shape[1]):
        offset = pl.multiple_of(meta[place] * rows, rows)
        full[:, pl.ds(offset, rows), :] = top[0, place]
    inverse = split(full[blocks - 1])
    merged = product(split(full[: blocks - 1].reshape((blocks - 1) * wide, wide)), inverse, False)
    high[0], low[0] = split(merged)
    inverse_high[0], inverse_low[0] = inverse


def top_kernel(above, paths, incoming, high, low, inverse_high, inverse_low, outgoing):
    tops, wide = len(above), high.shape[2]
    width = outgoing.shape[1] - 1
    sources = [incoming[t, width] for t in range(tops)]
    for d, path in enumerate(paths):
        for i, t in enumerate(path):
            sources[t] = sources[t] - incoming[d, i]
    scaled = []
    for j in range(tops):
        source = split(sources[j])
        count = len(above[j])
        if count:
            rows = slice(0, count * wide)
            updates = product(source, (high[j, rows], low[j, rows]), True)
            for i, t in enumerate(above[j]):
                sources[t] = sources[t] - updates[:, i * wide : (i + 1) * wide]
        inverse = (inverse_high[j], inverse_low[j])
        scaled.append(product(split(product(source, inverse, True)), inverse, False))
    solved = [None] * tops
    parts = [None] * tops
    for j in range(tops - 1, -1, -1):
        total = scaled[j]
        for i, t in enumerate(above[j]):
            rows = slice(i * wide, (i + 1) * wide)
            total = total - product(parts[t], (high[j, rows], low[j, rows]), False)
        solved[j] = total
        parts[j] = split(total)
    for p in range(outgoing.shape[0]):
        path = paths[p]
        for i in range(width):
            outgoing[p, i] = solved[path[i] if i < len(path) else path[0]]
        outgoing[p, width] = solved[p]


def local(rhs_leaf, rhs_top, leaf_blocks, leaf_dinv, leaf_struct, top_blocks, top_dinv):
    leafs, columns, wide = rhs_leaf.shape
    tops = top_blocks.shape[0]
    steps = leafs // CHUNKS
    above = ancestors_of(tops)
    most = max(len(row) for row in above)
    width = most + 1
    paths = paths_of(tops, above)
    groups = min(tops, columns // 8)
    part = columns // groups

    core, zh, zl = lax.axis_index("core"), lax.axis_index("zh"), lax.axis_index("zl")
    xy = lax.axis_index("xy")

    def swap(value):
        return lax.ppermute(value, ("core", "zh"), [(0, 0), (1, 2), (2, 1), (3, 3)])

    def to_keeper(value):
        return lax.ppermute(value, ("core", "zh"), [(1, 0), (2, 3)])

    def to_trader(value):
        return lax.ppermute(value, ("core", "zh"), [(0, 2), (3, 1)])

    def keepers(value):
        return lax.ppermute(value, ("core", "zh", "zl"), [(0, 1), (1, 0), (6, 7), (7, 6)])

    def other(value, *axes):
        last = 2 ** len(axes) - 1
        return lax.ppermute(value, axes, [(i, last - i) for i in range(last + 1)])

    def after(first, value):
        return lax.optimization_barrier((first, value))[1]

    chosen = jnp.take(top_blocks[:, 0], jnp.asarray(padded(above, most))[2 * xy + core], axis=0)
    top = jnp.concatenate([chosen, top_dinv], axis=0)
    top = jnp.stack([top, other(top, "zh"), other(top, "zl"), other(top, "zh", "zl")])

    names = jnp.zeros((8, wide), f32).at[:3, :leafs].set(leaf_struct.T.astype(f32))
    sides = jnp.concatenate([rhs_leaf.reshape(-1, wide), rhs_top.reshape(-1, wide), names], axis=0)
    blocks, inverses, sides = after(top, (leaf_blocks, leaf_dinv, sides))
    top = lax.all_gather(top, ("xy", "core"), axis=0, tiled=False)

    def joined(at):
        return jnp.concatenate([blocks[at], inverses[at][:, None]], axis=1)

    own = joined(slice(None))
    near = keepers(own)
    sides = swap(sides)
    far, across = [], []
    for k in range(CHUNKS):
        value = joined(slice(k * steps, (k + 1) * steps))
        far.append(to_keeper(after(across[k - 2], value) if k > 1 else value))
        across.append(keepers(after(sides, far[0]) if k == 0 else far[k]))
    own_passed, near_passed = [to_trader(value) for value in after(across[1], (own, near))]

    names = sides[(leafs + 1) * columns :][:3, :leafs].T.astype(jnp.int32).reshape(-1)
    path = jnp.asarray(padded(paths, width))[2 * xy + zh]
    places = jnp.stack([2 * zh + zl, 2 * zh + 1 - zl, 2 - 2 * zh + zl, 3 - 2 * zh - zl])
    keeps = (core == zh).astype(jnp.int32)
    meta = jnp.concatenate([names, places.astype(jnp.int32), path, keeps[None]])

    def whole(*shape):
        return pl.BlockSpec((1,) + shape, lambda t: (t,) + (0,) * len(shape))

    top_places = jnp.stack([2 * zh + zl, 2 - 2 * zh + zl, 2 * zh + 1 - zl, 3 - 2 * zh - zl])
    top_factor = pl.pallas_call(
        top_prepare_kernel,
        grid=(tops,),
        in_specs=[SMEM, whole(*top.shape[1:])],
        out_specs=[whole(most * wide, wide)] * 2 + [whole(wide, wide)] * 2,
        out_shape=[jax.ShapeDtypeStruct((tops, most * wide, wide), bf16)] * 2
        + [jax.ShapeDtypeStruct((tops, wide, wide), bf16)] * 2,
        scratch_shapes=[pltpu.VMEM((width, wide, wide), f32)],
        compiler_params=params(),
        name="top_prepare",
    )(top_places.astype(jnp.int32), top)

    vectors = jax.ShapeDtypeStruct((leafs + tops, columns, wide), f32)
    merged = jax.ShapeDtypeStruct((steps, 3 * wide, wide), bf16)
    chunk = jax.ShapeDtypeStruct((steps, columns, wide), f32)
    cost = pl.CostEstimate(flops=4 * 10**9, bytes_accessed=8 * 2**20, transcendentals=0)
    factors, state = [], None
    for k in range(CHUNKS):
        last = k == CHUNKS - 1
        shapes = [vectors, merged, merged, chunk]
        passed = (to_trader(far[k]), to_trader(after(state, across[k]) if last else across[k]))
        part_of = pl.BlockSpec((steps, 4) + own.shape[2:], functools.partial(lambda k, i: (k, 0, 0, 0), k))
        specs = [SMEM, part_of, part_of, VMEM, VMEM, part_of, part_of, VMEM, VMEM, VMEM]
        if last:
            shapes.append(jax.ShapeDtypeStruct((tops, width + 1, part, wide), f32))
        before = () if k == 0 else (state,)
        results = pl.pallas_call(
            functools.partial(forward_kernel, k * steps, k == 0, last, width),
            grid=(1,),
            in_specs=specs + [VMEM] * (k > 0),
            out_specs=[VMEM] * len(shapes),
            out_shape=shapes,
            scratch_shapes=[pltpu.VMEM((steps, 4, wide, wide), f32)],
            compiler_params=params(),
            cost_estimate=cost,
            name="leaf_forward",
        )(meta, own, near, far[k], across[k], own_passed, near_passed, *passed, sides, *before)
        state = results[0]
        factors.append(results[1:4])

    incoming = lax.all_to_all(results[4], ("xy", "zh"), split_axis=0, concat_axis=0, tiled=True)
    outgoing = pl.pallas_call(
        functools.partial(top_kernel, above, paths),
        in_specs=[VMEM] * 5,
        out_specs=VMEM,
        out_shape=jax.ShapeDtypeStruct((tops, width + 1, part, wide), f32),
        compiler_params=params(),
        name="top_solve",
    )(incoming, *top_factor)
    state = lax.all_to_all(outgoing, ("xy", "zh"), split_axis=0, concat_axis=0, tiled=True)
    own_top = state[:groups, width].reshape(1, columns, wide)

    found = [None] * CHUNKS
    for k in range(CHUNKS - 1, -1, -1):
        found[k], state = pl.pallas_call(
            functools.partial(backward_kernel, k * steps, k == CHUNKS - 1, width),
            in_specs=[SMEM] + [VMEM] * 4,
            out_specs=[VMEM] * 2,
            out_shape=[chunk, vectors],
            compiler_params=params(),
            cost_estimate=cost,
            name="leaf_backward",
        )(meta, *factors[k], state)
    late = swap(found[-1])
    middle = swap(jnp.concatenate(found[1:-1] + [own_top], axis=0))
    early = swap(after(late, found[0]))
    leaf_solution = jnp.concatenate([early, middle[:-1], late], axis=0)
    return (leaf_solution, middle[-1:])


def solution(mesh):
    subtrees, quarters = mesh.devices.shape
    fine = Mesh(
        mesh.devices.reshape(subtrees // 2, 2, 2, quarters // 2), ("xy", "core", "zh", "zl")
    )
    sn, rhs = ("xy", "core"), ("zh", "zl")
    return jax.shard_map(
        local,
        mesh=fine,
        in_specs=(
            P(sn, rhs, None),
            P(sn, rhs, None),
            P(sn, None, rhs, None),
            P(sn, rhs, None),
            P(sn, None),
            P(None, sn, rhs, None),
            P(sn, rhs, None),
        ),
        out_specs=(P(sn, rhs, None), P(sn, rhs, None)),
        check_vma=False,
    )
```

```python
import functools

import jax
import jax.numpy as jnp
import numpy as np
from jax import lax
from jax.experimental import pallas as pl
from jax.experimental.pallas import tpu as pltpu
from jax.sharding import Mesh
from jax.sharding import PartitionSpec as P

CHUNKS = 2
TURNS = 4
f32 = jnp.float32
bf16 = jnp.bfloat16
SMEM = pl.BlockSpec(memory_space=pltpu.SMEM)
VMEM = pl.BlockSpec(memory_space=pltpu.VMEM)


def params():
    return pltpu.CompilerParams(vmem_limit_bytes=48 * 2**20)


def split(value):
    high = value.astype(bf16)
    return high, (value - high.astype(f32)).astype(bf16)


def product(left, right, transposed):
    dims = (((1,), (1 if transposed else 0,)), ((), ()))

    def dot(a, b):
        return lax.dot_general(a, b, dims, preferred_element_type=f32)

    return dot(left[0], right[0]) + (dot(left[1], right[0]) + dot(left[0], right[1]))


def ancestors_of(tops):
    def level(t):
        return ((t + 1) & -(t + 1)).bit_length() - 1

    return [[t for t in range(j + 1, tops) if t + 1 - 2 ** level(t) <= j] for j in range(tops)]


def paths_of(subtrees, above):
    return [[4 * (d // 4)] + above[4 * (d // 4)] for d in range(subtrees)]


def padded(rows, width):
    return np.array([row + [row[0] if row else 0] * (width - len(row)) for row in rows], np.int32)


def forward_kernel(base, first, last, width, *refs):
    meta, kept, passed, sides = refs[0], refs[1:5], refs[5:9], refs[9]
    refs = refs[10:]
    if not first:
        acc_in, refs = refs[0], refs[1:]
    acc, high, low, scaled, refs = refs[0], refs[1], refs[2], refs[3], refs[4:]
    if last:
        payload, refs = refs[0], refs[1:]
    full = refs[0]
    steps, columns, rows = scaled.shape[0], scaled.shape[1], kept[0].shape[2]
    leafs = steps * CHUNKS
    wide = full.shape[2]

    def assemble(pieces):
        for place, piece in enumerate(pieces):
            offset = pl.multiple_of(meta[3 * leafs + place] * rows, rows)
            full[:, :, pl.ds(offset, rows), :] = piece[...]

    keeps = meta[3 * leafs + 4 + width]
    pl.when(keeps == 1)(lambda: assemble(kept))
    pl.when(keeps == 0)(lambda: assemble(passed))
    if first:
        acc[...] = jnp.zeros_like(acc)
    else:
        acc[...] = acc_in[...]
    for s in range(steps):
        blocks = split(full[s, 0:3].reshape(3 * wide, wide))
        merged = split(product(blocks, split(full[s, 3]), False))
        high[s] = merged[0]
        low[s] = merged[1]
    for s in range(steps):
        at = (base + s) * columns
        source = split(sides[at : at + columns] - acc[base + s])
        outgoing = product(source, (high[s], low[s]), True)
        for r in range(3):
            target = meta[3 * (base + s) + r]
            acc[target] = acc[target] + outgoing[:, r * wide : (r + 1) * wide]
        inverse = split(full[s, 3])
        solved = split(product(source, inverse, True))
        scaled[s] = product(solved, inverse, False)
    if last:
        peers, part = payload.shape[0], payload.shape[2]
        groups = columns // part
        for i in range(width + 1):
            if i < width:
                node = acc[leafs + meta[3 * leafs + 4 + i]]
            else:
                node = sides[leafs * columns : (leafs + 1) * columns]
            for p in range(peers):
                at = (p % groups) * part
                payload[p, i] = node[at : at + part]


def backward_kernel(base, first, width, meta, high, low, scaled, state, out, z):
    steps, wide = scaled.shape[0], scaled.shape[2]
    leafs = steps * TURNS
    if first:
        part = state.shape[2]
        groups = scaled.shape[1] // part
        z[...] = jnp.zeros_like(z)
        for i in range(width):
            node = leafs + meta[3 * leafs + 4 + i]
            for p in range(groups):
                z[node, p * part : (p + 1) * part, :] = state[p, i]
    else:
        z[...] = state[...]
    for s in range(steps - 1, -1, -1):
        total = scaled[s]
        for r in (2, 1, 0):
            source = split(z[meta[3 * (base + s) + r]])
            at = slice(r * wide, (r + 1) * wide)
            total = total - product(source, (high[s, at], low[s, at]), False)
        z[base + s] = total
        out[s] = total


def top_prepare_kernel(meta, top, high, low, inverse_high, inverse_low, full):
    blocks, rows, wide = top.shape[2], top.shape[3], top.shape[4]
    for place in range(top.shape[1]):
        offset = pl.multiple_of(meta[place] * rows, rows)
        full[:, pl.ds(offset, rows), :] = top[0, place]
    inverse = split(full[blocks - 1])
    merged = product(split(full[: blocks - 1].reshape((blocks - 1) * wide, wide)), inverse, False)
    high[0], low[0] = split(merged)
    inverse_high[0], inverse_low[0] = inverse


def top_kernel(above, paths, incoming, high, low, inverse_high, inverse_low, outgoing):
    tops, wide = len(above), high.shape[2]
    width = outgoing.shape[1] - 1
    sources = [incoming[t, width] for t in range(tops)]
    for d, path in enumerate(paths):
        for i, t in enumerate(path):
            sources[t] = sources[t] - incoming[d, i]
    scaled = []
    for j in range(tops):
        source = split(sources[j])
        count = len(above[j])
        if count:
            rows = slice(0, count * wide)
            updates = product(source, (high[j, rows], low[j, rows]), True)
            for i, t in enumerate(above[j]):
                sources[t] = sources[t] - updates[:, i * wide : (i + 1) * wide]
        inverse = (inverse_high[j], inverse_low[j])
        scaled.append(product(split(product(source, inverse, True)), inverse, False))
    solved = [None] * tops
    parts = [None] * tops
    for j in range(tops - 1, -1, -1):
        total = scaled[j]
        for i, t in enumerate(above[j]):
            rows = slice(i * wide, (i + 1) * wide)
            total = total - product(parts[t], (high[j, rows], low[j, rows]), False)
        solved[j] = total
        parts[j] = split(total)
    for p in range(outgoing.shape[0]):
        path = paths[p]
        for i in range(width):
            outgoing[p, i] = solved[path[i] if i < len(path) else path[0]]
        outgoing[p, width] = solved[p]


def local(rhs_leaf, rhs_top, leaf_blocks, leaf_dinv, leaf_struct, top_blocks, top_dinv):
    leafs, columns, wide = rhs_leaf.shape
    tops = top_blocks.shape[0]
    steps = leafs // CHUNKS
    above = ancestors_of(tops)
    most = max(len(row) for row in above)
    width = most + 1
    paths = paths_of(tops, above)
    groups = min(tops, columns // 8)
    part = columns // groups

    core, zh, zl = lax.axis_index("core"), lax.axis_index("zh"), lax.axis_index("zl")
    xy = lax.axis_index("xy")

    def swap(value):
        return lax.ppermute(value, ("core", "zh"), [(0, 0), (1, 2), (2, 1), (3, 3)])

    def to_keeper(value):
        return lax.ppermute(value, ("core", "zh"), [(1, 0), (2, 3)])

    def to_trader(value):
        return lax.ppermute(value, ("core", "zh"), [(0, 2), (3, 1)])

    def keepers(value):
        return lax.ppermute(value, ("core", "zh", "zl"), [(0, 1), (1, 0), (6, 7), (7, 6)])

    def other(value, *axes):
        last = 2 ** len(axes) - 1
        return lax.ppermute(value, axes, [(i, last - i) for i in range(last + 1)])

    def after(first, value):
        return lax.optimization_barrier((first, value))[1]

    chosen = jnp.take(top_blocks[:, 0], jnp.asarray(padded(above, most))[2 * xy + core], axis=0)
    top = jnp.concatenate([chosen, top_dinv], axis=0)
    names = jnp.zeros((8, wide), f32).at[:3, :leafs].set(leaf_struct.T.astype(f32))
    sides = jnp.concatenate([rhs_leaf.reshape(-1, wide), rhs_top.reshape(-1, wide), names], axis=0)
    def joined(at):
        return jnp.concatenate([leaf_blocks[at], leaf_dinv[at][:, None]], axis=1)

    own = joined(slice(None))
    parts = [joined(slice(k * steps, (k + 1) * steps)) for k in range(CHUNKS)]
    near = keepers(own)
    sides = swap(sides)
    far = [to_keeper(part) for part in parts]
    across = [keepers(after(sides, far[0]))] + [keepers(value) for value in far[1:]]
    top, own_late, near_late = after(across[0], (top, own, near))
    own_passed, near_passed = to_trader(own_late), to_trader(near_late)
    top = jnp.stack([top, other(top, "zh")])
    top = jnp.concatenate([top, other(top, "zl")])
    top = lax.all_gather(top, ("xy", "core"), axis=0, tiled=False)

    names = sides[(leafs + 1) * columns :][:3, :leafs].T.astype(jnp.int32).reshape(-1)
    path = jnp.asarray(padded(paths, width))[2 * xy + zh]
    places = jnp.stack([2 * zh + zl, 2 * zh + 1 - zl, 2 - 2 * zh + zl, 3 - 2 * zh - zl])
    keeps = (core == zh).astype(jnp.int32)
    meta = jnp.concatenate([names, places.astype(jnp.int32), path, keeps[None]])

    vectors = jax.ShapeDtypeStruct((leafs + tops, columns, wide), f32)
    merged = jax.ShapeDtypeStruct((steps, 3 * wide, wide), bf16)
    chunk = jax.ShapeDtypeStruct((steps, columns, wide), f32)
    cost = pl.CostEstimate(flops=4 * 10**9, bytes_accessed=8 * 2**20, transcendentals=0)
    factors, state = [], None
    for k in range(CHUNKS):
        last = k == CHUNKS - 1
        shapes = [vectors, merged, merged, chunk]
        passed = (to_trader(far[k]), to_trader(across[k]))
        part_of = pl.BlockSpec((steps, 4) + own.shape[2:], functools.partial(lambda k, i: (k, 0, 0, 0), k))
        specs = [SMEM, part_of, part_of, VMEM, VMEM, part_of, part_of, VMEM, VMEM, VMEM]
        if last:
            shapes.append(jax.ShapeDtypeStruct((tops, width + 1, part, wide), f32))
        before = () if k == 0 else (state,)
        results = pl.pallas_call(
            functools.partial(forward_kernel, k * steps, k == 0, last, width),
            grid=(1,),
            in_specs=specs + [VMEM] * (k > 0),
            out_specs=[VMEM] * len(shapes),
            out_shape=shapes,
            scratch_shapes=[pltpu.VMEM((steps, 4, wide, wide), f32)],
            compiler_params=params(),
            cost_estimate=cost,
            name="leaf_forward",
        )(meta, own, near, far[k], across[k], own_passed, near_passed, *passed, sides, *before)
        state = results[0]
        factors.append(results[1:4])

    def whole(*shape):
        return pl.BlockSpec((1,) + shape, lambda t: (t,) + (0,) * len(shape))

    top_places = jnp.stack([2 * zh + zl, 2 - 2 * zh + zl, 2 * zh + 1 - zl, 3 - 2 * zh - zl])
    top_factor = pl.pallas_call(
        top_prepare_kernel,
        grid=(tops,),
        in_specs=[SMEM, whole(*top.shape[1:])],
        out_specs=[whole(most * wide, wide)] * 2 + [whole(wide, wide)] * 2,
        out_shape=[jax.ShapeDtypeStruct((tops, most * wide, wide), bf16)] * 2
        + [jax.ShapeDtypeStruct((tops, wide, wide), bf16)] * 2,
        scratch_shapes=[pltpu.VMEM((width, wide, wide), f32)],
        compiler_params=params(),
        name="top_prepare",
    )(top_places.astype(jnp.int32), after(results[4], top))

    incoming = lax.all_to_all(results[4], ("xy", "zh"), split_axis=0, concat_axis=0, tiled=True)
    outgoing = pl.pallas_call(
        functools.partial(top_kernel, above, paths),
        in_specs=[VMEM] * 5,
        out_specs=VMEM,
        out_shape=jax.ShapeDtypeStruct((tops, width + 1, part, wide), f32),
        compiler_params=params(),
        name="top_solve",
    )(incoming, *top_factor)
    state = lax.all_to_all(outgoing, ("xy", "zh"), split_axis=0, concat_axis=0, tiled=True)
    own_top = state[:groups, width].reshape(1, columns, wide)

    found = [None] * TURNS
    steps = leafs // TURNS
    share = TURNS // CHUNKS
    chunk = jax.ShapeDtypeStruct((steps, columns, wide), f32)
    for k in range(TURNS - 1, -1, -1):
        part_of = [
            pl.BlockSpec((steps,) + shape, functools.partial(lambda k, i: (k, 0, 0), k % share))
            for shape in ((3 * wide, wide), (3 * wide, wide), (columns, wide))
        ]
        found[k], state = pl.pallas_call(
            functools.partial(backward_kernel, k * steps, k == TURNS - 1, width),
            grid=(1,),
            in_specs=[SMEM] + part_of + [VMEM],
            out_specs=[VMEM] * 2,
            out_shape=[chunk, vectors],
            compiler_params=params(),
            cost_estimate=cost,
            name="leaf_backward",
        )(meta, *factors[k // share], state)
    late = swap(found[-1])
    middle = swap(jnp.concatenate(found[1:-1] + [own_top], axis=0))
    early = swap(after(late, found[0]))
    leaf_solution = jnp.concatenate([early, middle[:-1], late], axis=0)
    return (leaf_solution, middle[-1:])


def solution(mesh):
    subtrees, quarters = mesh.devices.shape
    fine = Mesh(
        mesh.devices.reshape(subtrees // 2, 2, 2, quarters // 2), ("xy", "core", "zh", "zl")
    )
    sn, rhs = ("xy", "core"), ("zh", "zl")
    return jax.shard_map(
        local,
        mesh=fine,
        in_specs=(
            P(sn, rhs, None),
            P(sn, rhs, None),
            P(sn, None, rhs, None),
            P(sn, rhs, None),
            P(sn, None),
            P(None, sn, rhs, None),
            P(sn, rhs, None),
        ),
        out_specs=(P(sn, rhs, None), P(sn, rhs, None)),
        check_vma=False,
    )
```

```python
import functools

import jax
import jax.numpy as jnp
import numpy as np
from jax import lax
from jax.experimental import pallas as pl
from jax.experimental.pallas import tpu as pltpu
from jax.sharding import Mesh
from jax.sharding import PartitionSpec as P

CHUNKS = 2
TURNS = 4
f32 = jnp.float32
bf16 = jnp.bfloat16
SMEM = pl.BlockSpec(memory_space=pltpu.SMEM)
VMEM = pl.BlockSpec(memory_space=pltpu.VMEM)


def params():
    return pltpu.CompilerParams(vmem_limit_bytes=48 * 2**20)


def split(value):
    high = value.astype(bf16)
    return high, (value - high.astype(f32)).astype(bf16)


def product(left, right, transposed):
    dims = (((1,), (1 if transposed else 0,)), ((), ()))

    def dot(a, b):
        return lax.dot_general(a, b, dims, preferred_element_type=f32)

    return dot(left[0], right[0]) + (dot(left[1], right[0]) + dot(left[0], right[1]))


def ancestors_of(tops):
    def level(t):
        return ((t + 1) & -(t + 1)).bit_length() - 1

    return [[t for t in range(j + 1, tops) if t + 1 - 2 ** level(t) <= j] for j in range(tops)]


def paths_of(subtrees, above):
    return [[4 * (d // 4)] + above[4 * (d // 4)] for d in range(subtrees)]


def padded(rows, width):
    return np.array([row + [row[0] if row else 0] * (width - len(row)) for row in rows], np.int32)


def forward_kernel(base, first, last, width, *refs):
    meta, kept, passed, sides = refs[0], refs[1:5], refs[5:9], refs[9]
    refs = refs[10:]
    if not first:
        acc_in, refs = refs[0], refs[1:]
    acc, high, low, scaled, refs = refs[0], refs[1], refs[2], refs[3], refs[4:]
    if last:
        payload, refs = refs[0], refs[1:]
    full = refs[0]
    steps, columns, rows = scaled.shape[0], scaled.shape[1], kept[0].shape[2]
    leafs = steps * CHUNKS
    wide = full.shape[2]

    def assemble(pieces):
        for place, piece in enumerate(pieces):
            offset = pl.multiple_of(meta[3 * leafs + place] * rows, rows)
            full[:, :, pl.ds(offset, rows), :] = piece[...]

    keeps = meta[3 * leafs + 4 + width]
    pl.when(keeps == 1)(lambda: assemble(kept))
    pl.when(keeps == 0)(lambda: assemble(passed))
    if first:
        acc[...] = jnp.zeros_like(acc)
    else:
        acc[...] = acc_in[...]
    for s in range(steps):
        blocks = split(full[s, 0:3].reshape(3 * wide, wide))
        merged = split(product(blocks, split(full[s, 3]), False))
        high[s] = merged[0]
        low[s] = merged[1]
    for s in range(steps):
        at = (base + s) * columns
        source = split(sides[at : at + columns] - acc[base + s])
        outgoing = product(source, (high[s], low[s]), True)
        for r in range(3):
            target = meta[3 * (base + s) + r]
            acc[target] = acc[target] + outgoing[:, r * wide : (r + 1) * wide]
        inverse = split(full[s, 3])
        solved = split(product(source, inverse, True))
        scaled[s] = product(solved, inverse, False)
    if last:
        peers, part = payload.shape[0], payload.shape[2]
        groups = columns // part
        for i in range(width + 1):
            if i < width:
                node = acc[leafs + meta[3 * leafs + 4 + i]]
            else:
                node = sides[leafs * columns : (leafs + 1) * columns]
            for p in range(peers):
                at = (p % groups) * part
                payload[p, i] = node[at : at + part]


def backward_kernel(base, first, width, meta, high, low, scaled, state, out, z):
    steps, wide = scaled.shape[0], scaled.shape[2]
    leafs = steps * TURNS
    if first:
        part = state.shape[2]
        groups = scaled.shape[1] // part
        z[...] = jnp.zeros_like(z)
        for i in range(width):
            node = leafs + meta[3 * leafs + 4 + i]
            for p in range(groups):
                z[node, p * part : (p + 1) * part, :] = state[p, i]
    else:
        z[...] = state[...]
    for s in range(steps - 1, -1, -1):
        total = scaled[s]
        for r in (2, 1, 0):
            source = split(z[meta[3 * (base + s) + r]])
            at = slice(r * wide, (r + 1) * wide)
            total = total - product(source, (high[s, at], low[s, at]), False)
        z[base + s] = total
        out[s] = total


def top_prepare_kernel(meta, top, high, low, inverse_high, inverse_low, full):
    blocks, rows, wide = top.shape[2], top.shape[3], top.shape[4]
    for place in range(top.shape[1]):
        offset = pl.multiple_of(meta[place] * rows, rows)
        full[:, pl.ds(offset, rows), :] = top[0, place]
    inverse = split(full[blocks - 1])
    merged = product(split(full[: blocks - 1].reshape((blocks - 1) * wide, wide)), inverse, False)
    high[0], low[0] = split(merged)
    inverse_high[0], inverse_low[0] = inverse


def top_kernel(above, paths, incoming, high, low, inverse_high, inverse_low, outgoing):
    tops, wide = len(above), high.shape[2]
    width = outgoing.shape[1] - 1
    sources = [incoming[t, width] for t in range(tops)]
    for d, path in enumerate(paths):
        for i, t in enumerate(path):
            sources[t] = sources[t] - incoming[d, i]
    scaled = []
    for j in range(tops):
        source = split(sources[j])
        count = len(above[j])
        if count:
            rows = slice(0, count * wide)
            updates = product(source, (high[j, rows], low[j, rows]), True)
            for i, t in enumerate(above[j]):
                sources[t] = sources[t] - updates[:, i * wide : (i + 1) * wide]
        inverse = (inverse_high[j], inverse_low[j])
        scaled.append(product(split(product(source, inverse, True)), inverse, False))
    solved = [None] * tops
    parts = [None] * tops
    for j in range(tops - 1, -1, -1):
        total = scaled[j]
        for i, t in enumerate(above[j]):
            rows = slice(i * wide, (i + 1) * wide)
            total = total - product(parts[t], (high[j, rows], low[j, rows]), False)
        solved[j] = total
        parts[j] = split(total)
    for p in range(outgoing.shape[0]):
        path = paths[p]
        for i in range(width):
            outgoing[p, i] = solved[path[i] if i < len(path) else path[0]]
        outgoing[p, width] = solved[p]


def local(rhs_leaf, rhs_top, leaf_blocks, leaf_dinv, leaf_struct, top_blocks, top_dinv):
    leafs, columns, wide = rhs_leaf.shape
    tops = top_blocks.shape[0]
    steps = leafs // CHUNKS
    above = ancestors_of(tops)
    most = max(len(row) for row in above)
    width = most + 1
    paths = paths_of(tops, above)
    groups = min(tops, columns // 8)
    part = columns // groups

    core, zh, zl = lax.axis_index("core"), lax.axis_index("zh"), lax.axis_index("zl")
    xy = lax.axis_index("xy")

    def swap(value):
        return lax.ppermute(value, ("core", "zh"), [(0, 0), (1, 2), (2, 1), (3, 3)])

    def to_keeper(value):
        return lax.ppermute(value, ("core", "zh"), [(1, 0), (2, 3)])

    def to_trader(value):
        return lax.ppermute(value, ("core", "zh"), [(0, 2), (3, 1)])

    def keepers(value):
        return lax.ppermute(value, ("core", "zh", "zl"), [(0, 1), (1, 0), (6, 7), (7, 6)])

    def other(value, *axes):
        last = 2 ** len(axes) - 1
        return lax.ppermute(value, axes, [(i, last - i) for i in range(last + 1)])

    def after(first, value):
        return lax.optimization_barrier((first, value))[1]

    chosen = jnp.take(top_blocks[:, 0], jnp.asarray(padded(above, most))[2 * xy + core], axis=0)
    top = jnp.concatenate([chosen, top_dinv], axis=0)
    names = jnp.zeros((8, wide), f32).at[:3, :leafs].set(leaf_struct.T.astype(f32))
    sides = jnp.concatenate([rhs_leaf.reshape(-1, wide), rhs_top.reshape(-1, wide), names], axis=0)
    def joined(at):
        return jnp.concatenate([leaf_blocks[at], leaf_dinv[at][:, None]], axis=1)

    own = joined(slice(None))
    parts = [joined(slice(k * steps, (k + 1) * steps)) for k in range(CHUNKS)]
    near = keepers(own)
    sides = swap(sides)
    far = [to_keeper(part) for part in parts]
    across = [keepers(after(sides, far[0]))] + [keepers(value) for value in far[1:]]
    own_late, near_late = after(across[0], (own, near))
    top = after(far[-1], top)
    own_passed, near_passed = to_trader(own_late), to_trader(near_late)
    top = jnp.stack([top, other(top, "zh")])
    top = jnp.concatenate([top, other(top, "zl")])
    top = lax.all_gather(top, ("xy", "core"), axis=0, tiled=False)

    names = sides[(leafs + 1) * columns :][:3, :leafs].T.astype(jnp.int32).reshape(-1)
    path = jnp.asarray(padded(paths, width))[2 * xy + zh]
    places = jnp.stack([2 * zh + zl, 2 * zh + 1 - zl, 2 - 2 * zh + zl, 3 - 2 * zh - zl])
    keeps = (core == zh).astype(jnp.int32)
    meta = jnp.concatenate([names, places.astype(jnp.int32), path, keeps[None]])

    vectors = jax.ShapeDtypeStruct((leafs + tops, columns, wide), f32)
    merged = jax.ShapeDtypeStruct((steps, 3 * wide, wide), bf16)
    chunk = jax.ShapeDtypeStruct((steps, columns, wide), f32)
    cost = pl.CostEstimate(flops=4 * 10**9, bytes_accessed=8 * 2**20, transcendentals=0)
    factors, state = [], None
    for k in range(CHUNKS):
        last = k == CHUNKS - 1
        shapes = [vectors, merged, merged, chunk]
        passed = (to_trader(far[k]), to_trader(across[k]))
        part_of = pl.BlockSpec((steps, 4) + own.shape[2:], functools.partial(lambda k, i: (k, 0, 0, 0), k))
        specs = [SMEM, part_of, part_of, VMEM, VMEM, part_of, part_of, VMEM, VMEM, VMEM]
        if last:
            shapes.append(jax.ShapeDtypeStruct((tops, width + 1, part, wide), f32))
        before = () if k == 0 else (state,)
        results = pl.pallas_call(
            functools.partial(forward_kernel, k * steps, k == 0, last, width),
            grid=(1,),
            in_specs=specs + [VMEM] * (k > 0),
            out_specs=[VMEM] * len(shapes),
            out_shape=shapes,
            scratch_shapes=[pltpu.VMEM((steps, 4, wide, wide), f32)],
            compiler_params=params(),
            cost_estimate=cost,
            name="leaf_forward",
        )(meta, own, near, far[k], across[k], own_passed, near_passed, *passed, sides, *before)
        state = results[0]
        factors.append(results[1:4])

    def whole(*shape):
        return pl.BlockSpec((1,) + shape, lambda t: (t,) + (0,) * len(shape))

    top_places = jnp.stack([2 * zh + zl, 2 - 2 * zh + zl, 2 * zh + 1 - zl, 3 - 2 * zh - zl])
    top_factor = pl.pallas_call(
        top_prepare_kernel,
        grid=(tops,),
        in_specs=[SMEM, whole(*top.shape[1:])],
        out_specs=[whole(most * wide, wide)] * 2 + [whole(wide, wide)] * 2,
        out_shape=[jax.ShapeDtypeStruct((tops, most * wide, wide), bf16)] * 2
        + [jax.ShapeDtypeStruct((tops, wide, wide), bf16)] * 2,
        scratch_shapes=[pltpu.VMEM((width, wide, wide), f32)],
        compiler_params=params(),
        name="top_prepare",
    )(top_places.astype(jnp.int32), after(results[4], top))

    incoming = lax.all_to_all(results[4], ("xy", "zh"), split_axis=0, concat_axis=0, tiled=True)
    outgoing = pl.pallas_call(
        functools.partial(top_kernel, above, paths),
        in_specs=[VMEM] * 5,
        out_specs=VMEM,
        out_shape=jax.ShapeDtypeStruct((tops, width + 1, part, wide), f32),
        compiler_params=params(),
        name="top_solve",
    )(incoming, *top_factor)
    state = lax.all_to_all(outgoing, ("xy", "zh"), split_axis=0, concat_axis=0, tiled=True)
    own_top = state[:groups, width].reshape(1, columns, wide)

    found = [None] * TURNS
    steps = leafs // TURNS
    share = TURNS // CHUNKS
    chunk = jax.ShapeDtypeStruct((steps, columns, wide), f32)
    for k in range(TURNS - 1, -1, -1):
        part_of = [
            pl.BlockSpec((steps,) + shape, functools.partial(lambda k, i: (k, 0, 0), k % share))
            for shape in ((3 * wide, wide), (3 * wide, wide), (columns, wide))
        ]
        found[k], state = pl.pallas_call(
            functools.partial(backward_kernel, k * steps, k == TURNS - 1, width),
            grid=(1,),
            in_specs=[SMEM] + part_of + [VMEM],
            out_specs=[VMEM] * 2,
            out_shape=[chunk, vectors],
            compiler_params=params(),
            cost_estimate=cost,
            name="leaf_backward",
        )(meta, *factors[k // share], state)
    late = swap(found[-1])
    middle = swap(jnp.concatenate(found[1:-1] + [own_top], axis=0))
    early = swap(after(late, found[0]))
    leaf_solution = jnp.concatenate([early, middle[:-1], late], axis=0)
    return (leaf_solution, middle[-1:])


def solution(mesh):
    subtrees, quarters = mesh.devices.shape
    fine = Mesh(
        mesh.devices.reshape(subtrees // 2, 2, 2, quarters // 2), ("xy", "core", "zh", "zl")
    )
    sn, rhs = ("xy", "core"), ("zh", "zl")
    return jax.shard_map(
        local,
        mesh=fine,
        in_specs=(
            P(sn, rhs, None),
            P(sn, rhs, None),
            P(sn, None, rhs, None),
            P(sn, rhs, None),
            P(sn, None),
            P(None, sn, rhs, None),
            P(sn, rhs, None),
        ),
        out_specs=(P(sn, rhs, None), P(sn, rhs, None)),
        check_vma=False,
    )
```

```python
import functools

import jax
import jax.numpy as jnp
import numpy as np
from jax import lax
from jax.experimental import pallas as pl
from jax.experimental.pallas import tpu as pltpu
from jax.sharding import Mesh
from jax.sharding import PartitionSpec as P

CHUNKS = 2
TURNS = 4
GROUP = 4
f32 = jnp.float32
bf16 = jnp.bfloat16
SMEM = pl.BlockSpec(memory_space=pltpu.SMEM)
VMEM = pl.BlockSpec(memory_space=pltpu.VMEM)


def params():
    return pltpu.CompilerParams(vmem_limit_bytes=28 * 2**20)


def split(value):
    high = value.astype(bf16)
    return high, (value - high.astype(f32)).astype(bf16)


def product(left, right, transposed):
    dims = (((1,), (1 if transposed else 0,)), ((), ()))

    def dot(a, b):
        return lax.dot_general(a, b, dims, preferred_element_type=f32)

    return dot(left[0], right[0]) + (dot(left[1], right[0]) + dot(left[0], right[1]))


def ancestors_of(tops):
    def level(t):
        return ((t + 1) & -(t + 1)).bit_length() - 1

    return [[t for t in range(j + 1, tops) if t + 1 - 2 ** level(t) <= j] for j in range(tops)]


def paths_of(subtrees, above):
    return [[4 * (d // 4)] + above[4 * (d // 4)] for d in range(subtrees)]


def padded(rows, width):
    return np.array([row + [row[0] if row else 0] * (width - len(row)) for row in rows], np.int32)


def forward_kernel(base, first, last, width, *refs):
    meta, kept, passed, rhs, rhs_top = refs[0], refs[1:5], refs[5:9], refs[9], refs[10]
    refs = refs[11:]
    if not first:
        acc_in, refs = refs[0], refs[1:]
    acc, high, low, scaled, refs = refs[0], refs[1], refs[2], refs[3], refs[4:]
    if last:
        payload, refs = refs[0], refs[1:]
    full, arrived = refs
    steps, columns, rows = scaled.shape[0], scaled.shape[1], kept[0].shape[2]
    leafs = steps * CHUNKS
    wide = full.shape[2]

    def copies(pieces, group):
        made = []
        for place, piece in enumerate(pieces):
            offset = pl.multiple_of(meta[3 * leafs + place] * rows, rows)
            start = group * GROUP + (base if piece.shape[0] > steps else 0)
            made.append(
                pltpu.make_async_copy(
                    piece.at[pl.ds(start, GROUP)],
                    full.at[pl.ds(group * GROUP, GROUP), :, pl.ds(offset, rows), :],
                    arrived.at[group, place],
                )
            )
        return made

    def start(pieces):
        for group in range(steps // GROUP):
            for copy in copies(pieces, group):
                copy.start()

    keeps = meta[3 * leafs + 4 + width]
    pl.when(keeps == 1)(lambda: start(kept))
    pl.when(keeps == 0)(lambda: start(passed))
    if first:
        acc[...] = jnp.zeros_like(acc)
    else:
        acc[...] = acc_in[...]
    for group in range(steps // GROUP):
        for copy in copies(kept, group):
            copy.wait()
        members = range(group * GROUP, (group + 1) * GROUP)
        for s in members:
            blocks = split(full[s, 0:3].reshape(3 * wide, wide))
            merged = split(product(blocks, split(full[s, 3]), False))
            high[s] = merged[0]
            low[s] = merged[1]
        for s in members:
            at = s * columns
            source = split(rhs[at : at + columns] - acc[base + s])
            outgoing = product(source, (high[s], low[s]), True)
            for r in range(3):
                target = meta[3 * (base + s) + r]
                acc[target] = acc[target] + outgoing[:, r * wide : (r + 1) * wide]
            inverse = split(full[s, 3])
            solved = split(product(source, inverse, True))
            scaled[s] = product(solved, inverse, False)
    if last:
        peers, part = payload.shape[0], payload.shape[2]
        groups = columns // part
        for i in range(width + 1):
            node = acc[leafs + meta[3 * leafs + 4 + i]] if i < width else rhs_top[...]
            for p in range(peers):
                at = (p % groups) * part
                payload[p, i] = node[at : at + part]


def backward_kernel(base, first, width, meta, high, low, scaled, state, out, z):
    steps, wide = scaled.shape[0], scaled.shape[2]
    leafs = steps * TURNS
    if first:
        part = state.shape[2]
        groups = scaled.shape[1] // part
        z[...] = jnp.zeros_like(z)
        for i in range(width):
            node = leafs + meta[3 * leafs + 4 + i]
            for p in range(groups):
                z[node, p * part : (p + 1) * part, :] = state[p, i]
    else:
        z[...] = state[...]
    for s in range(steps - 1, -1, -1):
        total = scaled[s]
        for r in (2, 1, 0):
            source = split(z[meta[3 * (base + s) + r]])
            at = slice(r * wide, (r + 1) * wide)
            total = total - product(source, (high[s, at], low[s, at]), False)
        z[base + s] = total
        out[s] = total


def top_prepare_kernel(top, high, low, inverse_high, inverse_low):
    count, wide = top.shape[1] - 1, top.shape[2]
    inverse = split(top[0, count])
    merged = product(split(top[0, :count].reshape(count * wide, wide)), inverse, False)
    high[0], low[0] = split(merged)
    inverse_high[0], inverse_low[0] = inverse


def top_kernel(above, paths, incoming, high, low, inverse_high, inverse_low, outgoing):
    tops, wide = len(above), high.shape[2]
    width = outgoing.shape[1] - 1
    sources = [incoming[t, width] for t in range(tops)]
    for d, path in enumerate(paths):
        for i, t in enumerate(path):
            sources[t] = sources[t] - incoming[d, i]
    scaled = []
    for j in range(tops):
        source = split(sources[j])
        count = len(above[j])
        if count:
            rows = slice(0, count * wide)
            updates = product(source, (high[j, rows], low[j, rows]), True)
            for i, t in enumerate(above[j]):
                sources[t] = sources[t] - updates[:, i * wide : (i + 1) * wide]
        inverse = (inverse_high[j], inverse_low[j])
        scaled.append(product(split(product(source, inverse, True)), inverse, False))
    solved = [None] * tops
    parts = [None] * tops
    for j in range(tops - 1, -1, -1):
        total = scaled[j]
        for i, t in enumerate(above[j]):
            rows = slice(i * wide, (i + 1) * wide)
            total = total - product(parts[t], (high[j, rows], low[j, rows]), False)
        solved[j] = total
        parts[j] = split(total)
    for p in range(outgoing.shape[0]):
        path = paths[p]
        for i in range(width):
            outgoing[p, i] = solved[path[i] if i < len(path) else path[0]]
        outgoing[p, width] = solved[p]


def local(rhs_leaf, rhs_top, leaf_blocks, leaf_dinv, leaf_struct, top_blocks, top_dinv):
    leafs, columns, wide = rhs_leaf.shape
    tops = top_blocks.shape[0]
    steps = leafs // CHUNKS
    above = ancestors_of(tops)
    most = max(len(row) for row in above)
    width = most + 1
    paths = paths_of(tops, above)
    groups = min(tops, columns // 8)
    part = columns // groups

    core, zh, zl = lax.axis_index("core"), lax.axis_index("zh"), lax.axis_index("zl")
    xy = lax.axis_index("xy")

    def swap(value):
        return lax.ppermute(value, ("core", "zh"), [(0, 0), (1, 2), (2, 1), (3, 3)])

    def to_keeper(value):
        return lax.ppermute(value, ("core", "zh"), [(1, 0), (2, 3)])

    def to_trader(value):
        return lax.ppermute(value, ("core", "zh"), [(0, 2), (3, 1)])

    def keepers(value):
        return lax.ppermute(value, ("core", "zh", "zl"), [(0, 1), (1, 0), (6, 7), (7, 6)])

    def other(value, *axes):
        last = 2 ** len(axes) - 1
        return lax.ppermute(value, axes, [(i, last - i) for i in range(last + 1)])

    def after(first, value):
        return lax.optimization_barrier((first, value))[1]

    chosen = jnp.take(top_blocks[:, 0], jnp.asarray(padded(above, most))[2 * xy + core], axis=0)
    top = jnp.concatenate([chosen, top_dinv], axis=0)
    top = lax.dynamic_update_slice(
        jnp.zeros((width, wide, wide), f32), top, (0, (2 * zh + zl) * top.shape[1], 0)
    )
    summed = lax.psum(top, ("zh", "zl"))
    top = lax.all_gather(summed, ("xy", "core"), axis=0, tiled=False)
    names = jnp.zeros((8, wide), f32).at[:3, :leafs].set(leaf_struct.T.astype(f32))
    sides = jnp.concatenate([rhs_leaf.reshape(-1, wide), rhs_top.reshape(-1, wide), names], axis=0)
    def joined(at):
        return jnp.concatenate([leaf_blocks[at], leaf_dinv[at][:, None]], axis=1)

    own = joined(slice(None))
    parts = [joined(slice(k * steps, (k + 1) * steps)) for k in range(CHUNKS)]
    near = keepers(own)
    sides = swap(sides)
    far = [to_keeper(part) for part in parts]
    across = [keepers(after((sides, summed), far[0]))]
    across += [keepers(after(top, value)) for value in far[1:]]
    own_passed, near_passed = [to_trader(value) for value in after(across[0], (own, near))]

    names = sides[(leafs + 1) * columns :][:3, :leafs].T.astype(jnp.int32).reshape(-1)
    path = jnp.asarray(padded(paths, width))[2 * xy + zh]
    places = jnp.stack([2 * zh + zl, 2 * zh + 1 - zl, 2 - 2 * zh + zl, 3 - 2 * zh - zl])
    keeps = (core == zh).astype(jnp.int32)
    meta = jnp.concatenate([names, places.astype(jnp.int32), path, keeps[None]])

    vectors = jax.ShapeDtypeStruct((leafs + tops, columns, wide), f32)
    merged = jax.ShapeDtypeStruct((steps, 3 * wide, wide), bf16)
    chunk = jax.ShapeDtypeStruct((steps, columns, wide), f32)
    cost = pl.CostEstimate(flops=4 * 10**9, bytes_accessed=8 * 2**20, transcendentals=0)
    factors, state = [], None
    for k in range(CHUNKS):
        last = k == CHUNKS - 1
        shapes = [vectors, merged, merged, chunk]
        passed = (to_trader(far[k]), to_trader(across[k]))
        specs = [SMEM] + [pl.BlockSpec(memory_space=pl.ANY)] * 8 + [
            pl.BlockSpec((steps * columns, wide), functools.partial(lambda k, i: (k, 0), k)),
            pl.BlockSpec((columns, wide), lambda i: (leafs, 0)),
        ]
        if last:
            shapes.append(jax.ShapeDtypeStruct((tops, width + 1, part, wide), f32))
        before = () if k == 0 else (state,)
        results = pl.pallas_call(
            functools.partial(forward_kernel, k * steps, k == 0, last, width),
            grid=(1,),
            in_specs=specs + [VMEM] * (k > 0),
            out_specs=[VMEM] * len(shapes),
            out_shape=shapes,
            scratch_shapes=[
                pltpu.VMEM((steps, 4, wide, wide), f32),
                pltpu.SemaphoreType.DMA((steps // GROUP, 4)),
            ],
            compiler_params=params(),
            cost_estimate=cost,
            name="leaf_forward",
        )(meta, own, near, far[k], across[k], own_passed, near_passed, *passed, sides, sides, *before)
        state = results[0]
        factors.append(results[1:4])

    def whole(*shape):
        return pl.BlockSpec((1,) + shape, lambda t: (t,) + (0,) * len(shape))

    top_factor = pl.pallas_call(
        top_prepare_kernel,
        grid=(tops,),
        in_specs=[whole(*top.shape[1:])],
        out_specs=[whole(most * wide, wide)] * 2 + [whole(wide, wide)] * 2,
        out_shape=[jax.ShapeDtypeStruct((tops, most * wide, wide), bf16)] * 2
        + [jax.ShapeDtypeStruct((tops, wide, wide), bf16)] * 2,
        compiler_params=params(),
        name="top_prepare",
    )(after(results[4], top))

    incoming = lax.all_to_all(results[4], ("xy", "zh"), split_axis=0, concat_axis=0, tiled=True)
    outgoing = pl.pallas_call(
        functools.partial(top_kernel, above, paths),
        in_specs=[VMEM] * 5,
        out_specs=VMEM,
        out_shape=jax.ShapeDtypeStruct((tops, width + 1, part, wide), f32),
        compiler_params=params(),
        name="top_solve",
    )(incoming, *top_factor)
    state = lax.all_to_all(outgoing, ("xy", "zh"), split_axis=0, concat_axis=0, tiled=True)
    own_top = state[:groups, width].reshape(1, columns, wide)

    found = [None] * TURNS
    steps = leafs // TURNS
    share = TURNS // CHUNKS
    chunk = jax.ShapeDtypeStruct((steps, columns, wide), f32)
    for k in range(TURNS - 1, -1, -1):
        part_of = [
            pl.BlockSpec((steps,) + shape, functools.partial(lambda k, i: (k, 0, 0), k % share))
            for shape in ((3 * wide, wide), (3 * wide, wide), (columns, wide))
        ]
        found[k], state = pl.pallas_call(
            functools.partial(backward_kernel, k * steps, k == TURNS - 1, width),
            grid=(1,),
            in_specs=[SMEM] + part_of + [VMEM],
            out_specs=[VMEM] * 2,
            out_shape=[chunk, vectors],
            compiler_params=params(),
            cost_estimate=cost,
            name="leaf_backward",
        )(meta, *factors[k // share], state)
    late = swap(found[-1])
    middle = swap(jnp.concatenate(found[1:-1] + [own_top], axis=0))
    early = swap(after(late, found[0]))
    leaf_solution = jnp.concatenate([early, middle[:-1], late], axis=0)
    return (leaf_solution, middle[-1:])


def solution(mesh):
    subtrees, quarters = mesh.devices.shape
    fine = Mesh(
        mesh.devices.reshape(subtrees // 2, 2, 2, quarters // 2), ("xy", "core", "zh", "zl")
    )
    sn, rhs = ("xy", "core"), ("zh", "zl")
    return jax.shard_map(
        local,
        mesh=fine,
        in_specs=(
            P(sn, rhs, None),
            P(sn, rhs, None),
            P(sn, None, rhs, None),
            P(sn, rhs, None),
            P(sn, None),
            P(None, sn, rhs, None),
            P(sn, rhs, None),
        ),
        out_specs=(P(sn, rhs, None), P(sn, rhs, None)),
        check_vma=False,
    )
```

```python
import functools

import jax
import jax.numpy as jnp
import numpy as np
from jax import lax
from jax.experimental import pallas as pl
from jax.experimental.pallas import tpu as pltpu
from jax.sharding import Mesh
from jax.sharding import PartitionSpec as P

CHUNKS = 2
TURNS = 4
GROUP = 4
f32 = jnp.float32
bf16 = jnp.bfloat16
SMEM = pl.BlockSpec(memory_space=pltpu.SMEM)
VMEM = pl.BlockSpec(memory_space=pltpu.VMEM)


def params():
    return pltpu.CompilerParams(vmem_limit_bytes=28 * 2**20)


def split(value):
    high = value.astype(bf16)
    return high, (value - high.astype(f32)).astype(bf16)


def product(left, right, transposed):
    dims = (((1,), (1 if transposed else 0,)), ((), ()))

    def dot(a, b):
        return lax.dot_general(a, b, dims, preferred_element_type=f32)

    return dot(left[0], right[0]) + (dot(left[1], right[0]) + dot(left[0], right[1]))


def ancestors_of(tops):
    def level(t):
        return ((t + 1) & -(t + 1)).bit_length() - 1

    return [[t for t in range(j + 1, tops) if t + 1 - 2 ** level(t) <= j] for j in range(tops)]


def paths_of(subtrees, above):
    return [[4 * (d // 4)] + above[4 * (d // 4)] for d in range(subtrees)]


def padded(rows, width):
    return np.array([row + [row[0] if row else 0] * (width - len(row)) for row in rows], np.int32)


def forward_kernel(base, first, last, width, *refs):
    meta, kept, passed, rhs, rhs_top = refs[0], refs[1:5], refs[5:9], refs[9], refs[10]
    refs = refs[11:]
    if not first:
        acc_in, refs = refs[0], refs[1:]
    acc, high, low, scaled, refs = refs[0], refs[1], refs[2], refs[3], refs[4:]
    if last:
        payload, refs = refs[0], refs[1:]
    full, arrived = refs
    steps, columns, rows = scaled.shape[0], scaled.shape[1], kept[0].shape[2]
    leafs = steps * CHUNKS
    wide = full.shape[2]

    def copies(pieces, group):
        made = []
        for place, piece in enumerate(pieces):
            offset = pl.multiple_of(meta[3 * leafs + place] * rows, rows)
            start = group * GROUP + (base if piece.shape[0] > steps else 0)
            made.append(
                pltpu.make_async_copy(
                    piece.at[pl.ds(start, GROUP)],
                    full.at[pl.ds(group * GROUP, GROUP), :, pl.ds(offset, rows), :],
                    arrived.at[group, place],
                )
            )
        return made

    def start(pieces):
        for group in range(steps // GROUP):
            for copy in copies(pieces, group):
                copy.start()

    keeps = meta[3 * leafs + 4 + width]
    pl.when(keeps == 1)(lambda: start(kept))
    pl.when(keeps == 0)(lambda: start(passed))
    if first:
        acc[...] = jnp.zeros_like(acc)
    else:
        acc[...] = acc_in[...]
    for group in range(steps // GROUP):
        for copy in copies(kept, group):
            copy.wait()
        members = range(group * GROUP, (group + 1) * GROUP)
        for s in members:
            blocks = split(full[s, 0:3].reshape(3 * wide, wide))
            merged = split(product(blocks, split(full[s, 3]), False))
            high[s] = merged[0]
            low[s] = merged[1]
        for s in members:
            at = s * columns
            source = split(rhs[at : at + columns] - acc[base + s])
            outgoing = product(source, (high[s], low[s]), True)
            for r in range(3):
                target = meta[3 * (base + s) + r]
                acc[target] = acc[target] + outgoing[:, r * wide : (r + 1) * wide]
            inverse = split(full[s, 3])
            solved = split(product(source, inverse, True))
            scaled[s] = product(solved, inverse, False)
    if last:
        peers, part = payload.shape[0], payload.shape[2]
        groups = columns // part
        for i in range(width + 1):
            node = acc[leafs + meta[3 * leafs + 4 + i]] if i < width else rhs_top[...]
            for p in range(peers):
                at = (p % groups) * part
                payload[p, i] = node[at : at + part]


def backward_kernel(base, first, width, meta, high, low, scaled, state, out, z):
    steps, wide = scaled.shape[0], scaled.shape[2]
    leafs = steps * TURNS
    if first:
        part = state.shape[2]
        groups = scaled.shape[1] // part
        z[...] = jnp.zeros_like(z)
        for i in range(width):
            node = leafs + meta[3 * leafs + 4 + i]
            for p in range(groups):
                z[node, p * part : (p + 1) * part, :] = state[p, i]
    else:
        z[...] = state[...]
    for s in range(steps - 1, -1, -1):
        total = scaled[s]
        for r in (2, 1, 0):
            source = split(z[meta[3 * (base + s) + r]])
            at = slice(r * wide, (r + 1) * wide)
            total = total - product(source, (high[s, at], low[s, at]), False)
        z[base + s] = total
        out[s] = total


def top_prepare_kernel(top, high, low, inverse_high, inverse_low):
    count, wide = top.shape[1] - 1, top.shape[2]
    inverse = split(top[0, count])
    merged = product(split(top[0, :count].reshape(count * wide, wide)), inverse, False)
    high[0], low[0] = split(merged)
    inverse_high[0], inverse_low[0] = inverse


def top_kernel(above, paths, incoming, high, low, inverse_high, inverse_low, outgoing):
    tops, wide = len(above), high.shape[2]
    width = outgoing.shape[1] - 1
    sources = [incoming[t, width] for t in range(tops)]
    for d, path in enumerate(paths):
        for i, t in enumerate(path):
            sources[t] = sources[t] - incoming[d, i]
    scaled = []
    for j in range(tops):
        source = split(sources[j])
        count = len(above[j])
        if count:
            rows = slice(0, count * wide)
            updates = product(source, (high[j, rows], low[j, rows]), True)
            for i, t in enumerate(above[j]):
                sources[t] = sources[t] - updates[:, i * wide : (i + 1) * wide]
        inverse = (inverse_high[j], inverse_low[j])
        scaled.append(product(split(product(source, inverse, True)), inverse, False))
    solved = [None] * tops
    parts = [None] * tops
    for j in range(tops - 1, -1, -1):
        total = scaled[j]
        for i, t in enumerate(above[j]):
            rows = slice(i * wide, (i + 1) * wide)
            total = total - product(parts[t], (high[j, rows], low[j, rows]), False)
        solved[j] = total
        parts[j] = split(total)
    for p in range(outgoing.shape[0]):
        path = paths[p]
        for i in range(width):
            outgoing[p, i] = solved[path[i] if i < len(path) else path[0]]
        outgoing[p, width] = solved[p]


def local(rhs_leaf, rhs_top, leaf_blocks, leaf_dinv, leaf_struct, top_blocks, top_dinv):
    leafs, columns, wide = rhs_leaf.shape
    tops = top_blocks.shape[0]
    steps = leafs // CHUNKS
    above = ancestors_of(tops)
    most = max(len(row) for row in above)
    width = most + 1
    paths = paths_of(tops, above)
    groups = min(tops, columns // 8)
    part = columns // groups

    core, zh, zl = lax.axis_index("core"), lax.axis_index("zh"), lax.axis_index("zl")
    xy = lax.axis_index("xy")

    def swap(value):
        return lax.ppermute(value, ("core", "zh"), [(0, 0), (1, 2), (2, 1), (3, 3)])

    def to_keeper(value):
        return lax.ppermute(value, ("core", "zh"), [(1, 0), (2, 3)])

    def to_trader(value):
        return lax.ppermute(value, ("core", "zh"), [(0, 2), (3, 1)])

    def keepers(value):
        return lax.ppermute(value, ("core", "zh", "zl"), [(0, 1), (1, 0), (6, 7), (7, 6)])

    def other(value, *axes):
        last = 2 ** len(axes) - 1
        return lax.ppermute(value, axes, [(i, last - i) for i in range(last + 1)])

    def after(first, value):
        return lax.optimization_barrier((first, value))[1]

    chosen = jnp.take(top_blocks[:, 0], jnp.asarray(padded(above, most))[2 * xy + core], axis=0)
    top = jnp.concatenate([chosen, top_dinv], axis=0)
    top = lax.dynamic_update_slice(
        jnp.zeros((width, wide, wide), f32), top, (0, (2 * zh + zl) * top.shape[1], 0)
    )
    summed = lax.psum(top, ("zh", "zl"))
    names = jnp.zeros((8, wide), f32).at[:3, :leafs].set(leaf_struct.T.astype(f32))
    sides = jnp.concatenate([rhs_leaf.reshape(-1, wide), rhs_top.reshape(-1, wide), names], axis=0)
    def joined(at):
        return jnp.concatenate([leaf_blocks[at], leaf_dinv[at][:, None]], axis=1)

    own = joined(slice(None))
    parts = [joined(slice(k * steps, (k + 1) * steps)) for k in range(CHUNKS)]
    near = keepers(own)
    sides = swap(sides)
    far = [to_keeper(part) for part in parts]
    across = [keepers(after(sides, far[0]))] + [keepers(value) for value in far[1:]]
    top = lax.all_gather(after(far[0], summed), ("xy", "core"), axis=0, tiled=False)
    own_passed, near_passed = [to_trader(value) for value in after(across[0], (own, near))]

    names = sides[(leafs + 1) * columns :][:3, :leafs].T.astype(jnp.int32).reshape(-1)
    path = jnp.asarray(padded(paths, width))[2 * xy + zh]
    places = jnp.stack([2 * zh + zl, 2 * zh + 1 - zl, 2 - 2 * zh + zl, 3 - 2 * zh - zl])
    keeps = (core == zh).astype(jnp.int32)
    meta = jnp.concatenate([names, places.astype(jnp.int32), path, keeps[None]])

    vectors = jax.ShapeDtypeStruct((leafs + tops, columns, wide), f32)
    merged = jax.ShapeDtypeStruct((steps, 3 * wide, wide), bf16)
    chunk = jax.ShapeDtypeStruct((steps, columns, wide), f32)
    cost = pl.CostEstimate(flops=4 * 10**9, bytes_accessed=8 * 2**20, transcendentals=0)
    factors, state = [], None
    for k in range(CHUNKS):
        last = k == CHUNKS - 1
        shapes = [vectors, merged, merged, chunk]
        passed = (to_trader(far[k]), to_trader(across[k]))
        specs = [SMEM] + [pl.BlockSpec(memory_space=pl.ANY)] * 8 + [
            pl.BlockSpec((steps * columns, wide), functools.partial(lambda k, i: (k, 0), k)),
            pl.BlockSpec((columns, wide), lambda i: (leafs, 0)),
        ]
        if last:
            shapes.append(jax.ShapeDtypeStruct((tops, width + 1, part, wide), f32))
        before = () if k == 0 else (state,)
        results = pl.pallas_call(
            functools.partial(forward_kernel, k * steps, k == 0, last, width),
            grid=(1,),
            in_specs=specs + [VMEM] * (k > 0),
            out_specs=[VMEM] * len(shapes),
            out_shape=shapes,
            scratch_shapes=[
                pltpu.VMEM((steps, 4, wide, wide), f32),
                pltpu.SemaphoreType.DMA((steps // GROUP, 4)),
            ],
            compiler_params=params(),
            cost_estimate=cost,
            name="leaf_forward",
        )(meta, own, near, far[k], across[k], own_passed, near_passed, *passed, sides, sides, *before)
        state = results[0]
        factors.append(results[1:4])

    def whole(*shape):
        return pl.BlockSpec((1,) + shape, lambda t: (t,) + (0,) * len(shape))

    top_factor = pl.pallas_call(
        top_prepare_kernel,
        grid=(tops,),
        in_specs=[whole(*top.shape[1:])],
        out_specs=[whole(most * wide, wide)] * 2 + [whole(wide, wide)] * 2,
        out_shape=[jax.ShapeDtypeStruct((tops, most * wide, wide), bf16)] * 2
        + [jax.ShapeDtypeStruct((tops, wide, wide), bf16)] * 2,
        compiler_params=params(),
        name="top_prepare",
    )(after(results[4], top))

    incoming = lax.all_to_all(results[4], ("xy", "zh"), split_axis=0, concat_axis=0, tiled=True)
    outgoing = pl.pallas_call(
        functools.partial(top_kernel, above, paths),
        in_specs=[VMEM] * 5,
        out_specs=VMEM,
        out_shape=jax.ShapeDtypeStruct((tops, width + 1, part, wide), f32),
        compiler_params=params(),
        name="top_solve",
    )(incoming, *top_factor)
    state = lax.all_to_all(outgoing, ("xy", "zh"), split_axis=0, concat_axis=0, tiled=True)
    own_top = state[:groups, width].reshape(1, columns, wide)

    found = [None] * TURNS
    steps = leafs // TURNS
    share = TURNS // CHUNKS
    chunk = jax.ShapeDtypeStruct((steps, columns, wide), f32)
    for k in range(TURNS - 1, -1, -1):
        part_of = [
            pl.BlockSpec((steps,) + shape, functools.partial(lambda k, i: (k, 0, 0), k % share))
            for shape in ((3 * wide, wide), (3 * wide, wide), (columns, wide))
        ]
        found[k], state = pl.pallas_call(
            functools.partial(backward_kernel, k * steps, k == TURNS - 1, width),
            grid=(1,),
            in_specs=[SMEM] + part_of + [VMEM],
            out_specs=[VMEM] * 2,
            out_shape=[chunk, vectors],
            compiler_params=params(),
            cost_estimate=cost,
            name="leaf_backward",
        )(meta, *factors[k // share], state)
    late = swap(found[-1])
    middle = swap(jnp.concatenate(found[1:-1] + [own_top], axis=0))
    early = swap(after(late, found[0]))
    leaf_solution = jnp.concatenate([early, middle[:-1], late], axis=0)
    return (leaf_solution, middle[-1:])


def solution(mesh):
    subtrees, quarters = mesh.devices.shape
    fine = Mesh(
        mesh.devices.reshape(subtrees // 2, 2, 2, quarters // 2), ("xy", "core", "zh", "zl")
    )
    sn, rhs = ("xy", "core"), ("zh", "zl")
    return jax.shard_map(
        local,
        mesh=fine,
        in_specs=(
            P(sn, rhs, None),
            P(sn, rhs, None),
            P(sn, None, rhs, None),
            P(sn, rhs, None),
            P(sn, None),
            P(None, sn, rhs, None),
            P(sn, rhs, None),
        ),
        out_specs=(P(sn, rhs, None), P(sn, rhs, None)),
        check_vma=False,
    )
```

```python
import functools

import jax
import jax.numpy as jnp
import numpy as np
from jax import lax
from jax.experimental import pallas as pl
from jax.experimental.pallas import tpu as pltpu
from jax.sharding import Mesh
from jax.sharding import PartitionSpec as P

CHUNKS = 2
TURNS = 4
GROUP = 4
f32 = jnp.float32
bf16 = jnp.bfloat16
SMEM = pl.BlockSpec(memory_space=pltpu.SMEM)
VMEM = pl.BlockSpec(memory_space=pltpu.VMEM)


def params():
    return pltpu.CompilerParams(vmem_limit_bytes=28 * 2**20)


def split(value):
    high = value.astype(bf16)
    return high, (value - high.astype(f32)).astype(bf16)


def product(left, right, transposed):
    dims = (((1,), (1 if transposed else 0,)), ((), ()))

    def dot(a, b):
        return lax.dot_general(a, b, dims, preferred_element_type=f32)

    rows = left[0].shape[0]
    if rows % 16:
        return dot(left[0], right[0]) + (dot(left[1], right[0]) + dot(left[0], right[1]))
    both = dot(jnp.concatenate(left, axis=0), right[0])
    return both[:rows] + (both[rows:] + dot(left[0], right[1]))


def ancestors_of(tops):
    def level(t):
        return ((t + 1) & -(t + 1)).bit_length() - 1

    return [[t for t in range(j + 1, tops) if t + 1 - 2 ** level(t) <= j] for j in range(tops)]


def paths_of(subtrees, above):
    return [[4 * (d // 4)] + above[4 * (d // 4)] for d in range(subtrees)]


def padded(rows, width):
    return np.array([row + [row[0] if row else 0] * (width - len(row)) for row in rows], np.int32)


def forward_kernel(base, first, last, width, *refs):
    meta, kept, passed, rhs, rhs_top = refs[0], refs[1:5], refs[5:9], refs[9], refs[10]
    refs = refs[11:]
    if not first:
        acc_in, refs = refs[0], refs[1:]
    acc, high, low, scaled, refs = refs[0], refs[1], refs[2], refs[3], refs[4:]
    if last:
        payload, refs = refs[0], refs[1:]
    full, arrived = refs
    steps, columns, rows = scaled.shape[0], scaled.shape[1], kept[0].shape[2]
    leafs = steps * CHUNKS
    wide = full.shape[2]

    def copies(pieces, group):
        made = []
        for place, piece in enumerate(pieces):
            offset = pl.multiple_of(meta[3 * leafs + place] * rows, rows)
            start = group * GROUP + (base if piece.shape[0] > steps else 0)
            made.append(
                pltpu.make_async_copy(
                    piece.at[pl.ds(start, GROUP)],
                    full.at[pl.ds(group * GROUP, GROUP), :, pl.ds(offset, rows), :],
                    arrived.at[group, place],
                )
            )
        return made

    def start(pieces):
        for group in range(steps // GROUP):
            for copy in copies(pieces, group):
                copy.start()

    keeps = meta[3 * leafs + 4 + width]
    pl.when(keeps == 1)(lambda: start(kept))
    pl.when(keeps == 0)(lambda: start(passed))
    if first:
        acc[...] = jnp.zeros_like(acc)
    else:
        acc[...] = acc_in[...]
    for group in range(steps // GROUP):
        for copy in copies(kept, group):
            copy.wait()
        members = range(group * GROUP, (group + 1) * GROUP)
        for s in members:
            blocks = split(full[s, 0:3].reshape(3 * wide, wide))
            merged = split(product(blocks, split(full[s, 3]), False))
            high[s] = merged[0]
            low[s] = merged[1]
        for s in members:
            at = s * columns
            source = split(rhs[at : at + columns] - acc[base + s])
            outgoing = product(source, (high[s], low[s]), True)
            for r in range(3):
                target = meta[3 * (base + s) + r]
                acc[target] = acc[target] + outgoing[:, r * wide : (r + 1) * wide]
            inverse = split(full[s, 3])
            solved = split(product(source, inverse, True))
            scaled[s] = product(solved, inverse, False)
    if last:
        peers, part = payload.shape[0], payload.shape[2]
        groups = columns // part
        for i in range(width + 1):
            node = acc[leafs + meta[3 * leafs + 4 + i]] if i < width else rhs_top[...]
            for p in range(peers):
                at = (p % groups) * part
                payload[p, i] = node[at : at + part]


def backward_kernel(base, first, width, meta, high, low, scaled, state, out, z):
    steps, wide = scaled.shape[0], scaled.shape[2]
    leafs = steps * TURNS
    if first:
        part = state.shape[2]
        groups = scaled.shape[1] // part
        z[...] = jnp.zeros_like(z)
        for i in range(width):
            node = leafs + meta[3 * leafs + 4 + i]
            for p in range(groups):
                z[node, p * part : (p + 1) * part, :] = state[p, i]
    else:
        z[...] = state[...]
    for s in range(steps - 1, -1, -1):
        total = scaled[s]
        for r in (2, 1, 0):
            source = split(z[meta[3 * (base + s) + r]])
            at = slice(r * wide, (r + 1) * wide)
            total = total - product(source, (high[s, at], low[s, at]), False)
        z[base + s] = total
        out[s] = total


def top_prepare_kernel(top, high, low, inverse_high, inverse_low):
    count, wide = top.shape[1] - 1, top.shape[2]
    inverse = split(top[0, count])
    merged = product(split(top[0, :count].reshape(count * wide, wide)), inverse, False)
    high[0], low[0] = split(merged)
    inverse_high[0], inverse_low[0] = inverse


def top_kernel(above, paths, incoming, high, low, inverse_high, inverse_low, outgoing):
    tops, wide = len(above), high.shape[2]
    width = outgoing.shape[1] - 1
    sources = [incoming[t, width] for t in range(tops)]
    for d, path in enumerate(paths):
        for i, t in enumerate(path):
            sources[t] = sources[t] - incoming[d, i]
    scaled = []
    for j in range(tops):
        source = split(sources[j])
        count = len(above[j])
        if count:
            rows = slice(0, count * wide)
            updates = product(source, (high[j, rows], low[j, rows]), True)
            for i, t in enumerate(above[j]):
                sources[t] = sources[t] - updates[:, i * wide : (i + 1) * wide]
        inverse = (inverse_high[j], inverse_low[j])
        scaled.append(product(split(product(source, inverse, True)), inverse, False))
    solved = [None] * tops
    parts = [None] * tops
    for j in range(tops - 1, -1, -1):
        total = scaled[j]
        for i, t in enumerate(above[j]):
            rows = slice(i * wide, (i + 1) * wide)
            total = total - product(parts[t], (high[j, rows], low[j, rows]), False)
        solved[j] = total
        parts[j] = split(total)
    for p in range(outgoing.shape[0]):
        path = paths[p]
        for i in range(width):
            outgoing[p, i] = solved[path[i] if i < len(path) else path[0]]
        outgoing[p, width] = solved[p]


def local(rhs_leaf, rhs_top, leaf_blocks, leaf_dinv, leaf_struct, top_blocks, top_dinv):
    leafs, columns, wide = rhs_leaf.shape
    tops = top_blocks.shape[0]
    steps = leafs // CHUNKS
    above = ancestors_of(tops)
    most = max(len(row) for row in above)
    width = most + 1
    paths = paths_of(tops, above)
    groups = min(tops, columns // 8)
    part = columns // groups

    core, zh, zl = lax.axis_index("core"), lax.axis_index("zh"), lax.axis_index("zl")
    xy = lax.axis_index("xy")

    def swap(value):
        return lax.ppermute(value, ("core", "zh"), [(0, 0), (1, 2), (2, 1), (3, 3)])

    def to_keeper(value):
        return lax.ppermute(value, ("core", "zh"), [(1, 0), (2, 3)])

    def to_trader(value):
        return lax.ppermute(value, ("core", "zh"), [(0, 2), (3, 1)])

    def keepers(value):
        return lax.ppermute(value, ("core", "zh", "zl"), [(0, 1), (1, 0), (6, 7), (7, 6)])

    def other(value, *axes):
        last = 2 ** len(axes) - 1
        return lax.ppermute(value, axes, [(i, last - i) for i in range(last + 1)])

    def after(first, value):
        return lax.optimization_barrier((first, value))[1]

    chosen = jnp.take(top_blocks[:, 0], jnp.asarray(padded(above, most))[2 * xy + core], axis=0)
    top = jnp.concatenate([chosen, top_dinv], axis=0)
    top = lax.dynamic_update_slice(
        jnp.zeros((width, wide, wide), f32), top, (0, (2 * zh + zl) * top.shape[1], 0)
    )
    summed = lax.psum(top, ("zh", "zl"))
    names = jnp.zeros((8, wide), f32).at[:3, :leafs].set(leaf_struct.T.astype(f32))
    sides = jnp.concatenate([rhs_leaf.reshape(-1, wide), rhs_top.reshape(-1, wide), names], axis=0)
    def joined(at):
        return jnp.concatenate([leaf_blocks[at], leaf_dinv[at][:, None]], axis=1)

    own = joined(slice(None))
    parts = [joined(slice(k * steps, (k + 1) * steps)) for k in range(CHUNKS)]
    near = keepers(own)
    sides = swap(sides)
    far = [to_keeper(part) for part in parts]
    across = [keepers(after((sides, summed), far[0]))] + [keepers(value) for value in far[1:]]
    top = lax.all_gather(after(far[-1], summed), ("xy", "core"), axis=0, tiled=False)
    own_passed, near_passed = [to_trader(value) for value in after(across[0], (own, near))]

    names = sides[(leafs + 1) * columns :][:3, :leafs].T.astype(jnp.int32).reshape(-1)
    path = jnp.asarray(padded(paths, width))[2 * xy + zh]
    places = jnp.stack([2 * zh + zl, 2 * zh + 1 - zl, 2 - 2 * zh + zl, 3 - 2 * zh - zl])
    keeps = (core == zh).astype(jnp.int32)
    meta = jnp.concatenate([names, places.astype(jnp.int32), path, keeps[None]])

    vectors = jax.ShapeDtypeStruct((leafs + tops, columns, wide), f32)
    merged = jax.ShapeDtypeStruct((steps, 3 * wide, wide), bf16)
    chunk = jax.ShapeDtypeStruct((steps, columns, wide), f32)
    cost = pl.CostEstimate(flops=4 * 10**9, bytes_accessed=8 * 2**20, transcendentals=0)
    factors, state = [], None
    for k in range(CHUNKS):
        last = k == CHUNKS - 1
        shapes = [vectors, merged, merged, chunk]
        passed = (to_trader(far[k]), to_trader(across[k]))
        specs = [SMEM] + [pl.BlockSpec(memory_space=pl.ANY)] * 8 + [
            pl.BlockSpec((steps * columns, wide), functools.partial(lambda k, i: (k, 0), k)),
            pl.BlockSpec((columns, wide), lambda i: (leafs, 0)),
        ]
        if last:
            shapes.append(jax.ShapeDtypeStruct((tops, width + 1, part, wide), f32))
        before = () if k == 0 else (state,)
        results = pl.pallas_call(
            functools.partial(forward_kernel, k * steps, k == 0, last, width),
            grid=(1,),
            in_specs=specs + [VMEM] * (k > 0),
            out_specs=[VMEM] * len(shapes),
            out_shape=shapes,
            scratch_shapes=[
                pltpu.VMEM((steps, 4, wide, wide), f32),
                pltpu.SemaphoreType.DMA((steps // GROUP, 4)),
            ],
            compiler_params=params(),
            cost_estimate=cost,
            name="leaf_forward",
        )(meta, own, near, far[k], across[k], own_passed, near_passed, *passed, sides, sides, *before)
        state = results[0]
        factors.append(results[1:4])

    def whole(*shape):
        return pl.BlockSpec((1,) + shape, lambda t: (t,) + (0,) * len(shape))

    top_factor = pl.pallas_call(
        top_prepare_kernel,
        grid=(tops,),
        in_specs=[whole(*top.shape[1:])],
        out_specs=[whole(most * wide, wide)] * 2 + [whole(wide, wide)] * 2,
        out_shape=[jax.ShapeDtypeStruct((tops, most * wide, wide), bf16)] * 2
        + [jax.ShapeDtypeStruct((tops, wide, wide), bf16)] * 2,
        compiler_params=params(),
        name="top_prepare",
    )(after(results[4], top))

    incoming = lax.all_to_all(results[4], ("xy", "zh"), split_axis=0, concat_axis=0, tiled=True)
    outgoing = pl.pallas_call(
        functools.partial(top_kernel, above, paths),
        in_specs=[VMEM] * 5,
        out_specs=VMEM,
        out_shape=jax.ShapeDtypeStruct((tops, width + 1, part, wide), f32),
        compiler_params=params(),
        name="top_solve",
    )(incoming, *top_factor)
    state = lax.all_to_all(outgoing, ("xy", "zh"), split_axis=0, concat_axis=0, tiled=True)
    own_top = state[:groups, width].reshape(1, columns, wide)

    found = [None] * TURNS
    steps = leafs // TURNS
    share = TURNS // CHUNKS
    chunk = jax.ShapeDtypeStruct((steps, columns, wide), f32)
    for k in range(TURNS - 1, -1, -1):
        part_of = [
            pl.BlockSpec((steps,) + shape, functools.partial(lambda k, i: (k, 0, 0), k % share))
            for shape in ((3 * wide, wide), (3 * wide, wide), (columns, wide))
        ]
        found[k], state = pl.pallas_call(
            functools.partial(backward_kernel, k * steps, k == TURNS - 1, width),
            grid=(1,),
            in_specs=[SMEM] + part_of + [VMEM],
            out_specs=[VMEM] * 2,
            out_shape=[chunk, vectors],
            compiler_params=params(),
            cost_estimate=cost,
            name="leaf_backward",
        )(meta, *factors[k // share], state)
    late = swap(found[-1])
    middle = swap(jnp.concatenate(found[1:-1] + [own_top], axis=0))
    early = swap(after(late, found[0]))
    leaf_solution = jnp.concatenate([early, middle[:-1], late], axis=0)
    return (leaf_solution, middle[-1:])


def solution(mesh):
    subtrees, quarters = mesh.devices.shape
    fine = Mesh(
        mesh.devices.reshape(subtrees // 2, 2, 2, quarters // 2), ("xy", "core", "zh", "zl")
    )
    sn, rhs = ("xy", "core"), ("zh", "zl")
    return jax.shard_map(
        local,
        mesh=fine,
        in_specs=(
            P(sn, rhs, None),
            P(sn, rhs, None),
            P(sn, None, rhs, None),
            P(sn, rhs, None),
            P(sn, None),
            P(None, sn, rhs, None),
            P(sn, rhs, None),
        ),
        out_specs=(P(sn, rhs, None), P(sn, rhs, None)),
        check_vma=False,
    )
```

```python
import functools

import jax
import jax.numpy as jnp
import numpy as np
from jax import lax
from jax.experimental import pallas as pl
from jax.experimental.pallas import tpu as pltpu
from jax.sharding import Mesh
from jax.sharding import PartitionSpec as P

CHUNKS = 2
TURNS = 4
GROUP = 4
f32 = jnp.float32
bf16 = jnp.bfloat16
SMEM = pl.BlockSpec(memory_space=pltpu.SMEM)
VMEM = pl.BlockSpec(memory_space=pltpu.VMEM)


def params():
    return pltpu.CompilerParams(vmem_limit_bytes=56 * 2**20)


def split(value):
    high = value.astype(bf16)
    return high, (value - high.astype(f32)).astype(bf16)


def product(left, right, transposed):
    dims = (((1,), (1 if transposed else 0,)), ((), ()))

    def dot(a, b):
        return lax.dot_general(a, b, dims, preferred_element_type=f32)

    rows = left[0].shape[0]
    if rows % 16:
        return dot(left[0], right[0]) + (dot(left[1], right[0]) + dot(left[0], right[1]))
    both = dot(jnp.concatenate(left, axis=0), right[0])
    return both[:rows] + (both[rows:] + dot(left[0], right[1]))


def ancestors_of(tops):
    def level(t):
        return ((t + 1) & -(t + 1)).bit_length() - 1

    return [[t for t in range(j + 1, tops) if t + 1 - 2 ** level(t) <= j] for j in range(tops)]


def paths_of(subtrees, above):
    return [[4 * (d // 4)] + above[4 * (d // 4)] for d in range(subtrees)]


def padded(rows, width):
    return np.array([row + [row[0] if row else 0] * (width - len(row)) for row in rows], np.int32)


def forward_kernel(base, first, last, width, *refs):
    meta, kept, passed, rhs, rhs_top = refs[0], refs[1:5], refs[5:9], refs[9], refs[10]
    refs = refs[11:]
    if not first:
        acc_in, refs = refs[0], refs[1:]
    acc, high, low, scaled, refs = refs[0], refs[1], refs[2], refs[3], refs[4:]
    if last:
        payload, refs = refs[0], refs[1:]
    full, arrived = refs
    steps, columns, rows = scaled.shape[0], scaled.shape[1], kept[0].shape[2]
    leafs = steps * CHUNKS
    wide = full.shape[2]

    def copies(pieces, group):
        made = []
        for place, piece in enumerate(pieces):
            offset = pl.multiple_of(meta[3 * leafs + place] * rows, rows)
            start = group * GROUP + (base if piece.shape[0] > steps else 0)
            made.append(
                pltpu.make_async_copy(
                    piece.at[pl.ds(start, GROUP)],
                    full.at[pl.ds(group * GROUP, GROUP), :, pl.ds(offset, rows), :],
                    arrived.at[group, place],
                )
            )
        return made

    def start(pieces):
        for group in range(steps // GROUP):
            for copy in copies(pieces, group):
                copy.start()

    keeps = meta[3 * leafs + 4 + width]
    pl.when(keeps == 1)(lambda: start(kept))
    pl.when(keeps == 0)(lambda: start(passed))
    if first:
        acc[...] = jnp.zeros_like(acc)
    else:
        acc[...] = acc_in[...]
    for group in range(steps // GROUP):
        for copy in copies(kept, group):
            copy.wait()
        members = range(group * GROUP, (group + 1) * GROUP)
        for s in members:
            blocks = split(full[s, 0:3].reshape(3 * wide, wide))
            merged = split(product(blocks, split(full[s, 3]), False))
            high[s] = merged[0]
            low[s] = merged[1]
        for s in members:
            at = s * columns
            source = split(rhs[at : at + columns] - acc[base + s])
            outgoing = product(source, (high[s], low[s]), True)
            for r in range(3):
                target = meta[3 * (base + s) + r]
                acc[target] = acc[target] + outgoing[:, r * wide : (r + 1) * wide]
            inverse = split(full[s, 3])
            solved = split(product(source, inverse, True))
            scaled[s] = product(solved, inverse, False)
    if last:
        peers, part = payload.shape[0], payload.shape[2]
        groups = columns // part
        for i in range(width + 1):
            node = acc[leafs + meta[3 * leafs + 4 + i]] if i < width else rhs_top[...]
            for p in range(peers):
                at = (p % groups) * part
                payload[p, i] = node[at : at + part]


def backward_kernel(base, first, width, meta, high, low, scaled, state, out, z):
    steps, wide = scaled.shape[0], scaled.shape[2]
    leafs = steps * TURNS
    if first:
        part = state.shape[2]
        groups = scaled.shape[1] // part
        z[...] = jnp.zeros_like(z)
        for i in range(width):
            node = leafs + meta[3 * leafs + 4 + i]
            for p in range(groups):
                z[node, p * part : (p + 1) * part, :] = state[p, i]
    else:
        z[...] = state[...]
    for s in range(steps - 1, -1, -1):
        total = scaled[s]
        for r in (2, 1, 0):
            source = split(z[meta[3 * (base + s) + r]])
            at = slice(r * wide, (r + 1) * wide)
            total = total - product(source, (high[s, at], low[s, at]), False)
        z[base + s] = total
        out[s] = total


def top_prepare_kernel(top, high, low, inverse_high, inverse_low):
    count, wide = top.shape[1] - 1, top.shape[2]
    inverse = split(top[0, count])
    merged = product(split(top[0, :count].reshape(count * wide, wide)), inverse, False)
    high[0], low[0] = split(merged)
    inverse_high[0], inverse_low[0] = inverse


def top_kernel(above, paths, incoming, high, low, inverse_high, inverse_low, outgoing):
    tops, wide = len(above), high.shape[2]
    width = outgoing.shape[1] - 1
    sources = [incoming[t, width] for t in range(tops)]
    for d, path in enumerate(paths):
        for i, t in enumerate(path):
            sources[t] = sources[t] - incoming[d, i]
    scaled = []
    for j in range(tops):
        source = split(sources[j])
        count = len(above[j])
        if count:
            rows = slice(0, count * wide)
            updates = product(source, (high[j, rows], low[j, rows]), True)
            for i, t in enumerate(above[j]):
                sources[t] = sources[t] - updates[:, i * wide : (i + 1) * wide]
        inverse = (inverse_high[j], inverse_low[j])
        scaled.append(product(split(product(source, inverse, True)), inverse, False))
    solved = [None] * tops
    parts = [None] * tops
    for j in range(tops - 1, -1, -1):
        total = scaled[j]
        for i, t in enumerate(above[j]):
            rows = slice(i * wide, (i + 1) * wide)
            total = total - product(parts[t], (high[j, rows], low[j, rows]), False)
        solved[j] = total
        parts[j] = split(total)
    for p in range(outgoing.shape[0]):
        path = paths[p]
        for i in range(width):
            outgoing[p, i] = solved[path[i] if i < len(path) else path[0]]
        outgoing[p, width] = solved[p]


def local(rhs_leaf, rhs_top, leaf_blocks, leaf_dinv, leaf_struct, top_blocks, top_dinv):
    leafs, columns, wide = rhs_leaf.shape
    tops = top_blocks.shape[0]
    steps = leafs // CHUNKS
    above = ancestors_of(tops)
    most = max(len(row) for row in above)
    width = most + 1
    paths = paths_of(tops, above)
    groups = min(tops, columns // 8)
    part = columns // groups

    core, zh, zl = lax.axis_index("core"), lax.axis_index("zh"), lax.axis_index("zl")
    xy = lax.axis_index("xy")

    def swap(value):
        return lax.ppermute(value, ("core", "zh"), [(0, 0), (1, 2), (2, 1), (3, 3)])

    def to_keeper(value):
        return lax.ppermute(value, ("core", "zh"), [(1, 0), (2, 3)])

    def to_trader(value):
        return lax.ppermute(value, ("core", "zh"), [(0, 2), (3, 1)])

    def keepers(value):
        return lax.ppermute(value, ("core", "zh", "zl"), [(0, 1), (1, 0), (6, 7), (7, 6)])

    def other(value, *axes):
        last = 2 ** len(axes) - 1
        return lax.ppermute(value, axes, [(i, last - i) for i in range(last + 1)])

    def after(first, value):
        return lax.optimization_barrier((first, value))[1]

    chosen = jnp.take(top_blocks[:, 0], jnp.asarray(padded(above, most))[2 * xy + core], axis=0)
    top = jnp.concatenate([chosen, top_dinv], axis=0)
    top = lax.dynamic_update_slice(
        jnp.zeros((width, wide, wide), f32), top, (0, (2 * zh + zl) * top.shape[1], 0)
    )
    summed = lax.psum(top, ("zh", "zl"))
    names = jnp.zeros((8, wide), f32).at[:3, :leafs].set(leaf_struct.T.astype(f32))
    sides = jnp.concatenate([rhs_leaf.reshape(-1, wide), rhs_top.reshape(-1, wide), names], axis=0)
    def joined(at):
        return jnp.concatenate([leaf_blocks[at], leaf_dinv[at][:, None]], axis=1)

    own = joined(slice(None))
    parts = [joined(slice(k * steps, (k + 1) * steps)) for k in range(CHUNKS)]
    near = keepers(own)
    sides = swap(sides)
    far = [to_keeper(part) for part in parts]
    across = [keepers(after((sides, summed), far[0]))]
    early = [to_trader(value) for value in after(far[0], (own, near))] + [to_trader(far[0])]
    across += [keepers(after(early, value)) for value in far[1:]]
    top = lax.all_gather(after(far[-1], summed), ("xy", "core"), axis=0, tiled=False)

    names = sides[(leafs + 1) * columns :][:3, :leafs].T.astype(jnp.int32).reshape(-1)
    path = jnp.asarray(padded(paths, width))[2 * xy + zh]
    places = jnp.stack([2 * zh + zl, 2 * zh + 1 - zl, 2 - 2 * zh + zl, 3 - 2 * zh - zl])
    keeps = (core == zh).astype(jnp.int32)
    meta = jnp.concatenate([names, places.astype(jnp.int32), path, keeps[None]])

    vectors = jax.ShapeDtypeStruct((leafs + tops, columns, wide), f32)
    merged = jax.ShapeDtypeStruct((steps, 3 * wide, wide), bf16)
    chunk = jax.ShapeDtypeStruct((steps, columns, wide), f32)
    cost = pl.CostEstimate(flops=4 * 10**9, bytes_accessed=8 * 2**20, transcendentals=0)
    factors, state = [], None
    for k in range(CHUNKS):
        last = k == CHUNKS - 1
        shapes = [vectors, merged, merged, chunk]
        if k == 0:
            passed = (early[2], to_trader(across[k]))
        else:
            passed = (to_trader(far[k]), to_trader(after(state, across[k])))
        specs = [SMEM] + [pl.BlockSpec(memory_space=pl.ANY)] * 8 + [
            pl.BlockSpec((steps * columns, wide), functools.partial(lambda k, i: (k, 0), k)),
            pl.BlockSpec((columns, wide), lambda i: (leafs, 0)),
        ]
        if last:
            shapes.append(jax.ShapeDtypeStruct((tops, width + 1, part, wide), f32))
        before = () if k == 0 else (state,)
        results = pl.pallas_call(
            functools.partial(forward_kernel, k * steps, k == 0, last, width),
            grid=(1,),
            in_specs=specs + [VMEM] * (k > 0),
            out_specs=[VMEM] * len(shapes),
            out_shape=shapes,
            scratch_shapes=[
                pltpu.VMEM((steps, 4, wide, wide), f32),
                pltpu.SemaphoreType.DMA((steps // GROUP, 4)),
            ],
            compiler_params=params(),
            cost_estimate=cost,
            name="leaf_forward",
        )(meta, own, near, far[k], across[k], *early[:2], *passed, sides, sides, *before)
        state = results[0]
        factors.append(results[1:4])

    def whole(*shape):
        return pl.BlockSpec((1,) + shape, lambda t: (t,) + (0,) * len(shape))

    top_factor = pl.pallas_call(
        top_prepare_kernel,
        grid=(tops,),
        in_specs=[whole(*top.shape[1:])],
        out_specs=[whole(most * wide, wide)] * 2 + [whole(wide, wide)] * 2,
        out_shape=[jax.ShapeDtypeStruct((tops, most * wide, wide), bf16)] * 2
        + [jax.ShapeDtypeStruct((tops, wide, wide), bf16)] * 2,
        compiler_params=params(),
        name="top_prepare",
    )(after(results[4], top))

    incoming = lax.all_to_all(results[4], ("xy", "zh"), split_axis=0, concat_axis=0, tiled=True)
    outgoing = pl.pallas_call(
        functools.partial(top_kernel, above, paths),
        in_specs=[VMEM] * 5,
        out_specs=VMEM,
        out_shape=jax.ShapeDtypeStruct((tops, width + 1, part, wide), f32),
        compiler_params=params(),
        name="top_solve",
    )(incoming, *top_factor)
    state = lax.all_to_all(outgoing, ("xy", "zh"), split_axis=0, concat_axis=0, tiled=True)
    own_top = state[:groups, width].reshape(1, columns, wide)

    found = [None] * TURNS
    steps = leafs // TURNS
    share = TURNS // CHUNKS
    chunk = jax.ShapeDtypeStruct((steps, columns, wide), f32)
    for k in range(TURNS - 1, -1, -1):
        part_of = [
            pl.BlockSpec((steps,) + shape, functools.partial(lambda k, i: (k, 0, 0), k % share))
            for shape in ((3 * wide, wide), (3 * wide, wide), (columns, wide))
        ]
        found[k], state = pl.pallas_call(
            functools.partial(backward_kernel, k * steps, k == TURNS - 1, width),
            grid=(1,),
            in_specs=[SMEM] + part_of + [VMEM],
            out_specs=[VMEM] * 2,
            out_shape=[chunk, vectors],
            compiler_params=params(),
            cost_estimate=cost,
            name="leaf_backward",
        )(meta, *factors[k // share], state)
    late = swap(found[-1])
    middle = swap(jnp.concatenate(found[1:-1] + [own_top], axis=0))
    first = swap(after(late, found[0]))
    leaf_solution = jnp.concatenate([first, middle[:-1], late], axis=0)
    return (leaf_solution, middle[-1:])


def solution(mesh):
    subtrees, quarters = mesh.devices.shape
    fine = Mesh(
        mesh.devices.reshape(subtrees // 2, 2, 2, quarters // 2), ("xy", "core", "zh", "zl")
    )
    sn, rhs = ("xy", "core"), ("zh", "zl")
    return jax.shard_map(
        local,
        mesh=fine,
        in_specs=(
            P(sn, rhs, None),
            P(sn, rhs, None),
            P(sn, None, rhs, None),
            P(sn, rhs, None),
            P(sn, None),
            P(None, sn, rhs, None),
            P(sn, rhs, None),
        ),
        out_specs=(P(sn, rhs, None), P(sn, rhs, None)),
        check_vma=False,
    )
```

```python
import functools

import jax
import jax.numpy as jnp
import numpy as np
from jax import lax
from jax.experimental import pallas as pl
from jax.experimental.pallas import tpu as pltpu
from jax.sharding import Mesh
from jax.sharding import PartitionSpec as P

CHUNKS = 2
TURNS = 4
GROUP = 4
f32 = jnp.float32
bf16 = jnp.bfloat16
SMEM = pl.BlockSpec(memory_space=pltpu.SMEM)
VMEM = pl.BlockSpec(memory_space=pltpu.VMEM)


def params():
    return pltpu.CompilerParams(vmem_limit_bytes=28 * 2**20)


def split(value):
    high = value.astype(bf16)
    return high, (value - high.astype(f32)).astype(bf16)


def product(left, right, transposed):
    dims = (((1,), (1 if transposed else 0,)), ((), ()))

    def dot(a, b):
        return lax.dot_general(a, b, dims, preferred_element_type=f32)

    rows = left[0].shape[0]
    if rows % 16:
        return dot(left[0], right[0]) + (dot(left[1], right[0]) + dot(left[0], right[1]))
    both = dot(jnp.concatenate(left, axis=0), right[0])
    return both[:rows] + (both[rows:] + dot(left[0], right[1]))


def ancestors_of(tops):
    def level(t):
        return ((t + 1) & -(t + 1)).bit_length() - 1

    return [[t for t in range(j + 1, tops) if t + 1 - 2 ** level(t) <= j] for j in range(tops)]


def paths_of(subtrees, above):
    return [[4 * (d // 4)] + above[4 * (d // 4)] for d in range(subtrees)]


def padded(rows, width):
    return np.array([row + [row[0] if row else 0] * (width - len(row)) for row in rows], np.int32)


def forward_kernel(base, first, last, width, *refs):
    meta, kept, passed, rhs, rhs_top = refs[0], refs[1:5], refs[5:9], refs[9], refs[10]
    refs = refs[11:]
    if not first:
        acc_in, refs = refs[0], refs[1:]
    acc, high, low, scaled, refs = refs[0], refs[1], refs[2], refs[3], refs[4:]
    if last:
        payload, refs = refs[0], refs[1:]
    full, arrived = refs
    steps, columns, rows = scaled.shape[0], scaled.shape[1], kept[0].shape[2]
    leafs = steps * CHUNKS
    wide = full.shape[2]

    def copies(pieces, group):
        made = []
        for place, piece in enumerate(pieces):
            offset = pl.multiple_of(meta[3 * leafs + place] * rows, rows)
            start = group * GROUP + (base if piece.shape[0] > steps else 0)
            made.append(
                pltpu.make_async_copy(
                    piece.at[pl.ds(start, GROUP)],
                    full.at[pl.ds(group * GROUP, GROUP), :, pl.ds(offset, rows), :],
                    arrived.at[group, place],
                )
            )
        return made

    def start(pieces):
        for group in range(steps // GROUP):
            for copy in copies(pieces, group):
                copy.start()

    keeps = meta[3 * leafs + 4 + width]
    pl.when(keeps == 1)(lambda: start(kept))
    pl.when(keeps == 0)(lambda: start(passed))
    if first:
        acc[...] = jnp.zeros_like(acc)
    else:
        acc[...] = acc_in[...]
    for group in range(steps // GROUP):
        for copy in copies(kept, group):
            copy.wait()
        members = range(group * GROUP, (group + 1) * GROUP)
        for s in members:
            blocks = split(full[s, 0:3].reshape(3 * wide, wide))
            merged = split(product(blocks, split(full[s, 3]), False))
            high[s] = merged[0]
            low[s] = merged[1]
        for s in members:
            at = s * columns
            source = split(rhs[at : at + columns] - acc[base + s])
            outgoing = product(source, (high[s], low[s]), True)
            for r in range(3):
                target = meta[3 * (base + s) + r]
                acc[target] = acc[target] + outgoing[:, r * wide : (r + 1) * wide]
            inverse = split(full[s, 3])
            solved = split(product(source, inverse, True))
            scaled[s] = product(solved, inverse, False)
    if last:
        peers, part = payload.shape[0], payload.shape[2]
        groups = columns // part
        for i in range(width + 1):
            node = acc[leafs + meta[3 * leafs + 4 + i]] if i < width else rhs_top[...]
            for p in range(peers):
                at = (p % groups) * part
                payload[p, i] = node[at : at + part]


def backward_kernel(base, first, width, meta, high, low, scaled, state, out, z):
    steps, wide = scaled.shape[0], scaled.shape[2]
    leafs = steps * TURNS
    if first:
        part = state.shape[2]
        groups = scaled.shape[1] // part
        z[...] = jnp.zeros_like(z)
        for i in range(width):
            node = leafs + meta[3 * leafs + 4 + i]
            for p in range(groups):
                z[node, p * part : (p + 1) * part, :] = state[p, i]
    else:
        z[...] = state[...]
    for s in range(steps - 1, -1, -1):
        total = scaled[s]
        for r in (2, 1, 0):
            source = split(z[meta[3 * (base + s) + r]])
            at = slice(r * wide, (r + 1) * wide)
            total = total - product(source, (high[s, at], low[s, at]), False)
        z[base + s] = total
        out[s] = total


def top_prepare_kernel(top, high, low, inverse_high, inverse_low):
    count, wide = top.shape[1] - 1, top.shape[2]
    inverse = split(top[0, count])
    merged = product(split(top[0, :count].reshape(count * wide, wide)), inverse, False)
    high[0], low[0] = split(merged)
    inverse_high[0], inverse_low[0] = inverse


def top_kernel(above, paths, incoming, high, low, inverse_high, inverse_low, outgoing):
    tops, wide = len(above), high.shape[2]
    width = outgoing.shape[1] - 1
    sources = [incoming[t, width] for t in range(tops)]
    for d, path in enumerate(paths):
        for i, t in enumerate(path):
            sources[t] = sources[t] - incoming[d, i]
    scaled = []
    for j in range(tops):
        source = split(sources[j])
        count = len(above[j])
        if count:
            rows = slice(0, count * wide)
            updates = product(source, (high[j, rows], low[j, rows]), True)
            for i, t in enumerate(above[j]):
                sources[t] = sources[t] - updates[:, i * wide : (i + 1) * wide]
        inverse = (inverse_high[j], inverse_low[j])
        scaled.append(product(split(product(source, inverse, True)), inverse, False))
    solved = [None] * tops
    parts = [None] * tops
    for j in range(tops - 1, -1, -1):
        total = scaled[j]
        for i, t in enumerate(above[j]):
            rows = slice(i * wide, (i + 1) * wide)
            total = total - product(parts[t], (high[j, rows], low[j, rows]), False)
        solved[j] = total
        parts[j] = split(total)
    for p in range(outgoing.shape[0]):
        path = paths[p]
        for i in range(width):
            outgoing[p, i] = solved[path[i] if i < len(path) else path[0]]
        outgoing[p, width] = solved[p]


def local(rhs_leaf, rhs_top, leaf_blocks, leaf_dinv, leaf_struct, top_blocks, top_dinv):
    leafs, columns, wide = rhs_leaf.shape
    tops = top_blocks.shape[0]
    steps = leafs // CHUNKS
    above = ancestors_of(tops)
    most = max(len(row) for row in above)
    width = most + 1
    paths = paths_of(tops, above)
    groups = min(tops, columns // 8)
    part = columns // groups

    core, zh, zl = lax.axis_index("core"), lax.axis_index("zh"), lax.axis_index("zl")
    xy = lax.axis_index("xy")

    def swap(value):
        return lax.ppermute(value, ("core", "zh"), [(0, 0), (1, 2), (2, 1), (3, 3)])

    def to_keeper(value):
        return lax.ppermute(value, ("core", "zh"), [(1, 0), (2, 3)])

    def to_trader(value):
        return lax.ppermute(value, ("core", "zh"), [(0, 2), (3, 1)])

    def keepers(value):
        return lax.ppermute(value, ("core", "zh", "zl"), [(0, 1), (1, 0), (6, 7), (7, 6)])

    def other(value, *axes):
        last = 2 ** len(axes) - 1
        return lax.ppermute(value, axes, [(i, last - i) for i in range(last + 1)])

    def after(first, value):
        return lax.optimization_barrier((first, value))[1]

    chosen = jnp.take(top_blocks[:, 0], jnp.asarray(padded(above, most))[2 * xy + core], axis=0)
    top = jnp.concatenate([chosen, top_dinv], axis=0)
    top = lax.dynamic_update_slice(
        jnp.zeros((width, wide, wide), f32), top, (0, (2 * zh + zl) * top.shape[1], 0)
    )
    summed = lax.psum(top, ("zh", "zl"))
    names = jnp.zeros((8, wide), f32).at[:3, :leafs].set(leaf_struct.T.astype(f32))
    sides = jnp.concatenate([rhs_leaf.reshape(-1, wide), rhs_top.reshape(-1, wide), names], axis=0)
    def joined(at):
        return jnp.concatenate([leaf_blocks[at], leaf_dinv[at][:, None]], axis=1)

    own = joined(slice(None))
    parts = [joined(slice(k * steps, (k + 1) * steps)) for k in range(CHUNKS)]
    near = keepers(own)
    sides = swap(sides)
    far = [to_keeper(part) for part in parts]
    across = [keepers(after((sides, summed), far[0]))]
    early = [to_trader(value) for value in after(summed, (own, near, far[0]))]
    across += [keepers(after(early, value)) for value in far[1:]]
    top = lax.all_gather(after(far[-1], summed), ("xy", "core"), axis=0, tiled=False)

    names = sides[(leafs + 1) * columns :][:3, :leafs].T.astype(jnp.int32).reshape(-1)
    path = jnp.asarray(padded(paths, width))[2 * xy + zh]
    places = jnp.stack([2 * zh + zl, 2 * zh + 1 - zl, 2 - 2 * zh + zl, 3 - 2 * zh - zl])
    keeps = (core == zh).astype(jnp.int32)
    meta = jnp.concatenate([names, places.astype(jnp.int32), path, keeps[None]])

    vectors = jax.ShapeDtypeStruct((leafs + tops, columns, wide), f32)
    merged = jax.ShapeDtypeStruct((steps, 3 * wide, wide), bf16)
    chunk = jax.ShapeDtypeStruct((steps, columns, wide), f32)
    cost = pl.CostEstimate(flops=4 * 10**9, bytes_accessed=8 * 2**20, transcendentals=0)
    factors, state = [], None
    for k in range(CHUNKS):
        last = k == CHUNKS - 1
        shapes = [vectors, merged, merged, chunk]
        if k == 0:
            passed = (early[2], to_trader(across[k]))
        else:
            passed = (to_trader(far[k]), to_trader(after(state, across[k])))
        specs = [SMEM] + [pl.BlockSpec(memory_space=pl.ANY)] * 8 + [
            pl.BlockSpec((steps * columns, wide), functools.partial(lambda k, i: (k, 0), k)),
            pl.BlockSpec((columns, wide), lambda i: (leafs, 0)),
        ]
        if last:
            shapes.append(jax.ShapeDtypeStruct((tops, width + 1, part, wide), f32))
        before = () if k == 0 else (state,)
        results = pl.pallas_call(
            functools.partial(forward_kernel, k * steps, k == 0, last, width),
            grid=(1,),
            in_specs=specs + [VMEM] * (k > 0),
            out_specs=[VMEM] * len(shapes),
            out_shape=shapes,
            scratch_shapes=[
                pltpu.VMEM((steps, 4, wide, wide), f32),
                pltpu.SemaphoreType.DMA((steps // GROUP, 4)),
            ],
            compiler_params=params(),
            cost_estimate=cost,
            name="leaf_forward",
        )(meta, own, near, far[k], across[k], *early[:2], *passed, sides, sides, *before)
        state = results[0]
        factors.append(results[1:4])

    def whole(*shape):
        return pl.BlockSpec((1,) + shape, lambda t: (t,) + (0,) * len(shape))

    top_factor = pl.pallas_call(
        top_prepare_kernel,
        grid=(tops,),
        in_specs=[whole(*top.shape[1:])],
        out_specs=[whole(most * wide, wide)] * 2 + [whole(wide, wide)] * 2,
        out_shape=[jax.ShapeDtypeStruct((tops, most * wide, wide), bf16)] * 2
        + [jax.ShapeDtypeStruct((tops, wide, wide), bf16)] * 2,
        compiler_params=params(),
        name="top_prepare",
    )(after(results[4], top))

    incoming = lax.all_to_all(results[4], ("xy", "zh"), split_axis=0, concat_axis=0, tiled=True)
    outgoing = pl.pallas_call(
        functools.partial(top_kernel, above, paths),
        in_specs=[VMEM] * 5,
        out_specs=VMEM,
        out_shape=jax.ShapeDtypeStruct((tops, width + 1, part, wide), f32),
        compiler_params=params(),
        name="top_solve",
    )(incoming, *top_factor)
    state = lax.all_to_all(outgoing, ("xy", "zh"), split_axis=0, concat_axis=0, tiled=True)
    own_top = state[:groups, width].reshape(1, columns, wide)

    found = [None] * TURNS
    steps = leafs // TURNS
    share = TURNS // CHUNKS
    chunk = jax.ShapeDtypeStruct((steps, columns, wide), f32)
    for k in range(TURNS - 1, -1, -1):
        part_of = [
            pl.BlockSpec((steps,) + shape, functools.partial(lambda k, i: (k, 0, 0), k % share))
            for shape in ((3 * wide, wide), (3 * wide, wide), (columns, wide))
        ]
        found[k], state = pl.pallas_call(
            functools.partial(backward_kernel, k * steps, k == TURNS - 1, width),
            grid=(1,),
            in_specs=[SMEM] + part_of + [VMEM],
            out_specs=[VMEM] * 2,
            out_shape=[chunk, vectors],
            compiler_params=params(),
            cost_estimate=cost,
            name="leaf_backward",
        )(meta, *factors[k // share], state)
    late = swap(found[-1])
    middle = swap(jnp.concatenate(found[1:-1] + [own_top], axis=0))
    first = swap(after(late, found[0]))
    leaf_solution = jnp.concatenate([first, middle[:-1], late], axis=0)
    return (leaf_solution, middle[-1:])


def solution(mesh):
    subtrees, quarters = mesh.devices.shape
    fine = Mesh(
        mesh.devices.reshape(subtrees // 2, 2, 2, quarters // 2), ("xy", "core", "zh", "zl")
    )
    sn, rhs = ("xy", "core"), ("zh", "zl")
    return jax.shard_map(
        local,
        mesh=fine,
        in_specs=(
            P(sn, rhs, None),
            P(sn, rhs, None),
            P(sn, None, rhs, None),
            P(sn, rhs, None),
            P(sn, None),
            P(None, sn, rhs, None),
            P(sn, rhs, None),
        ),
        out_specs=(P(sn, rhs, None), P(sn, rhs, None)),
        check_vma=False,
    )
```

```python
import functools

import jax
import jax.numpy as jnp
import numpy as np
from jax import lax
from jax.experimental import pallas as pl
from jax.experimental.pallas import tpu as pltpu
from jax.sharding import Mesh
from jax.sharding import PartitionSpec as P

CHUNKS = (3, 1)
TURNS = 4
GROUP = 4
f32 = jnp.float32
bf16 = jnp.bfloat16
SMEM = pl.BlockSpec(memory_space=pltpu.SMEM)
VMEM = pl.BlockSpec(memory_space=pltpu.VMEM)


def params():
    return pltpu.CompilerParams(vmem_limit_bytes=28 * 2**20)


def split(value):
    high = value.astype(bf16)
    return high, (value - high.astype(f32)).astype(bf16)


def product(left, right, transposed):
    dims = (((1,), (1 if transposed else 0,)), ((), ()))

    def dot(a, b):
        return lax.dot_general(a, b, dims, preferred_element_type=f32)

    rows = left[0].shape[0]
    if rows % 16:
        return dot(left[0], right[0]) + (dot(left[1], right[0]) + dot(left[0], right[1]))
    both = dot(jnp.concatenate(left, axis=0), right[0])
    return both[:rows] + (both[rows:] + dot(left[0], right[1]))


def ancestors_of(tops):
    def level(t):
        return ((t + 1) & -(t + 1)).bit_length() - 1

    return [[t for t in range(j + 1, tops) if t + 1 - 2 ** level(t) <= j] for j in range(tops)]


def paths_of(subtrees, above):
    return [[4 * (d // 4)] + above[4 * (d // 4)] for d in range(subtrees)]


def padded(rows, width):
    return np.array([row + [row[0] if row else 0] * (width - len(row)) for row in rows], np.int32)


def forward_kernel(base, leafs, first, last, width, *refs):
    meta, kept, passed, rhs, rhs_top = refs[0], refs[1:5], refs[5:9], refs[9], refs[10]
    refs = refs[11:]
    if not first:
        acc_in, refs = refs[0], refs[1:]
    acc, high, low, scaled, refs = refs[0], refs[1], refs[2], refs[3], refs[4:]
    if last:
        payload, refs = refs[0], refs[1:]
    full, arrived = refs
    steps, columns, rows = scaled.shape[0], scaled.shape[1], kept[0].shape[2]
    wide = full.shape[2]

    def copies(pieces, group):
        made = []
        for place, piece in enumerate(pieces):
            offset = pl.multiple_of(meta[3 * leafs + place] * rows, rows)
            start = group * GROUP + (base if piece.shape[0] > steps else 0)
            made.append(
                pltpu.make_async_copy(
                    piece.at[pl.ds(start, GROUP)],
                    full.at[pl.ds(group * GROUP, GROUP), :, pl.ds(offset, rows), :],
                    arrived.at[group, place],
                )
            )
        return made

    def start(pieces):
        for group in range(steps // GROUP):
            for copy in copies(pieces, group):
                copy.start()

    keeps = meta[3 * leafs + 4 + width]
    pl.when(keeps == 1)(lambda: start(kept))
    pl.when(keeps == 0)(lambda: start(passed))
    if first:
        acc[...] = jnp.zeros_like(acc)
    else:
        acc[...] = acc_in[...]
    for group in range(steps // GROUP):
        for copy in copies(kept, group):
            copy.wait()
        members = range(group * GROUP, (group + 1) * GROUP)
        for s in members:
            blocks = split(full[s, 0:3].reshape(3 * wide, wide))
            merged = split(product(blocks, split(full[s, 3]), False))
            high[s] = merged[0]
            low[s] = merged[1]
        for s in members:
            at = s * columns
            source = split(rhs[at : at + columns] - acc[base + s])
            outgoing = product(source, (high[s], low[s]), True)
            for r in range(3):
                target = meta[3 * (base + s) + r]
                acc[target] = acc[target] + outgoing[:, r * wide : (r + 1) * wide]
            inverse = split(full[s, 3])
            solved = split(product(source, inverse, True))
            scaled[s] = product(solved, inverse, False)
    if last:
        peers, part = payload.shape[0], payload.shape[2]
        groups = columns // part
        for i in range(width + 1):
            node = acc[leafs + meta[3 * leafs + 4 + i]] if i < width else rhs_top[...]
            for p in range(peers):
                at = (p % groups) * part
                payload[p, i] = node[at : at + part]


def backward_kernel(base, first, width, meta, high, low, scaled, state, out, z):
    steps, wide = scaled.shape[0], scaled.shape[2]
    leafs = steps * TURNS
    if first:
        part = state.shape[2]
        groups = scaled.shape[1] // part
        z[...] = jnp.zeros_like(z)
        for i in range(width):
            node = leafs + meta[3 * leafs + 4 + i]
            for p in range(groups):
                z[node, p * part : (p + 1) * part, :] = state[p, i]
    else:
        z[...] = state[...]
    for s in range(steps - 1, -1, -1):
        total = scaled[s]
        for r in (2, 1, 0):
            source = split(z[meta[3 * (base + s) + r]])
            at = slice(r * wide, (r + 1) * wide)
            total = total - product(source, (high[s, at], low[s, at]), False)
        z[base + s] = total
        out[s] = total


def top_prepare_kernel(places, top, high, low, inverse_high, inverse_low, full):
    blocks, rows, wide = top.shape[2], top.shape[3], top.shape[4]
    for place in range(top.shape[1]):
        offset = pl.multiple_of(places[place] * rows, rows)
        full[:, pl.ds(offset, rows), :] = top[0, place]
    inverse = split(full[blocks - 1])
    merged = product(split(full[: blocks - 1].reshape((blocks - 1) * wide, wide)), inverse, False)
    high[0], low[0] = split(merged)
    inverse_high[0], inverse_low[0] = inverse


def top_kernel(above, paths, incoming, high, low, inverse_high, inverse_low, outgoing):
    tops, wide = len(above), high.shape[2]
    width = outgoing.shape[1] - 1
    sources = [incoming[t, width] for t in range(tops)]
    for d, path in enumerate(paths):
        for i, t in enumerate(path):
            sources[t] = sources[t] - incoming[d, i]
    scaled = []
    for j in range(tops):
        source = split(sources[j])
        count = len(above[j])
        if count:
            rows = slice(0, count * wide)
            updates = product(source, (high[j, rows], low[j, rows]), True)
            for i, t in enumerate(above[j]):
                sources[t] = sources[t] - updates[:, i * wide : (i + 1) * wide]
        inverse = (inverse_high[j], inverse_low[j])
        scaled.append(product(split(product(source, inverse, True)), inverse, False))
    solved = [None] * tops
    parts = [None] * tops
    for j in range(tops - 1, -1, -1):
        total = scaled[j]
        for i, t in enumerate(above[j]):
            rows = slice(i * wide, (i + 1) * wide)
            total = total - product(parts[t], (high[j, rows], low[j, rows]), False)
        solved[j] = total
        parts[j] = split(total)
    for p in range(outgoing.shape[0]):
        path = paths[p]
        for i in range(width):
            outgoing[p, i] = solved[path[i] if i < len(path) else path[0]]
        outgoing[p, width] = solved[p]


def local(rhs_leaf, rhs_top, leaf_blocks, leaf_dinv, leaf_struct, top_blocks, top_dinv):
    leafs, columns, wide = rhs_leaf.shape
    tops = top_blocks.shape[0]
    turn = leafs // TURNS
    starts = [turn * sum(CHUNKS[:k]) for k in range(len(CHUNKS) + 1)]
    above = ancestors_of(tops)
    most = max(len(row) for row in above)
    width = most + 1
    paths = paths_of(tops, above)
    groups = min(tops, columns // 8)
    part = columns // groups

    core, zh, zl = lax.axis_index("core"), lax.axis_index("zh"), lax.axis_index("zl")
    xy = lax.axis_index("xy")

    def swap(value):
        return lax.ppermute(value, ("core", "zh"), [(0, 0), (1, 2), (2, 1), (3, 3)])

    def to_keeper(value):
        return lax.ppermute(value, ("core", "zh"), [(1, 0), (2, 3)])

    def to_trader(value):
        return lax.ppermute(value, ("core", "zh"), [(0, 2), (3, 1)])

    def keepers(value):
        return lax.ppermute(value, ("core", "zh", "zl"), [(0, 1), (1, 0), (6, 7), (7, 6)])

    def other(value, *axes):
        last = 2 ** len(axes) - 1
        return lax.ppermute(value, axes, [(i, last - i) for i in range(last + 1)])

    def after(first, value):
        return lax.optimization_barrier((first, value))[1]

    chosen = jnp.take(top_blocks[:, 0], jnp.asarray(padded(above, most))[2 * xy + core], axis=0)
    top = jnp.concatenate([chosen, top_dinv], axis=0)
    top = jnp.stack([top, other(top, "zh")])
    top = jnp.concatenate([top, other(top, "zl")])

    names = jnp.zeros((8, wide), f32).at[:3, :leafs].set(leaf_struct.T.astype(f32))
    sides = jnp.concatenate([rhs_leaf.reshape(-1, wide), rhs_top.reshape(-1, wide), names], axis=0)
    def joined(at):
        return jnp.concatenate([leaf_blocks[at], leaf_dinv[at][:, None]], axis=1)

    own = joined(slice(None))
    parts = [joined(slice(at, end)) for at, end in zip(starts, starts[1:])]
    own, parts, sides = after(top, (own, parts, sides))

    near = keepers(own)
    sides = swap(sides)
    far = [to_keeper(part) for part in parts]
    across = [keepers(after(sides, far[0]))]
    early = [to_trader(value) for value in (own, near, far[0])]
    across += [keepers(after(early, value)) for value in far[1:]]
    top = lax.all_gather(after(far[-1], top), ("xy", "core"), axis=0, tiled=False)

    names = sides[(leafs + 1) * columns :][:3, :leafs].T.astype(jnp.int32).reshape(-1)
    path = jnp.asarray(padded(paths, width))[2 * xy + zh]
    places = jnp.stack([2 * zh + zl, 2 * zh + 1 - zl, 2 - 2 * zh + zl, 3 - 2 * zh - zl])
    keeps = (core == zh).astype(jnp.int32)
    meta = jnp.concatenate([names, places.astype(jnp.int32), path, keeps[None]])

    vectors = jax.ShapeDtypeStruct((leafs + tops, columns, wide), f32)
    cost = pl.CostEstimate(flops=4 * 10**9, bytes_accessed=8 * 2**20, transcendentals=0)
    factors, state = [], None
    for k, base in enumerate(starts[:-1]):
        last = k == len(CHUNKS) - 1
        steps = starts[k + 1] - base
        merged = jax.ShapeDtypeStruct((steps, 3 * wide, wide), bf16)
        chunk = jax.ShapeDtypeStruct((steps, columns, wide), f32)
        shapes = [vectors, merged, merged, chunk]
        if k == 0:
            passed = (early[2], to_trader(after(far[-1], across[k])))
        else:
            passed = (to_trader(far[k]), to_trader(after(state, across[k])))
        specs = [SMEM] + [pl.BlockSpec(memory_space=pl.ANY)] * 8 + [
            pl.BlockSpec((steps * columns, wide), functools.partial(lambda k, i: (k, 0), base // steps)),
            pl.BlockSpec((columns, wide), lambda i: (leafs, 0)),
        ]
        if last:
            shapes.append(jax.ShapeDtypeStruct((tops, width + 1, part, wide), f32))
        before = () if k == 0 else (state,)
        results = pl.pallas_call(
            functools.partial(forward_kernel, base, leafs, k == 0, last, width),
            grid=(1,),
            in_specs=specs + [VMEM] * (k > 0),
            out_specs=[VMEM] * len(shapes),
            out_shape=shapes,
            scratch_shapes=[
                pltpu.VMEM((steps, 4, wide, wide), f32),
                pltpu.SemaphoreType.DMA((steps // GROUP, 4)),
            ],
            compiler_params=params(),
            cost_estimate=cost,
            name="leaf_forward",
        )(meta, own, near, far[k], across[k], *early[:2], *passed, sides, sides, *before)
        state = results[0]
        factors.append(results[1:4])

    def whole(*shape):
        return pl.BlockSpec((1,) + shape, lambda t: (t,) + (0,) * len(shape))

    top_places = jnp.stack([2 * zh + zl, 2 - 2 * zh + zl, 2 * zh + 1 - zl, 3 - 2 * zh - zl])
    top_factor = pl.pallas_call(
        top_prepare_kernel,
        grid=(tops,),
        in_specs=[SMEM, whole(*top.shape[1:])],
        out_specs=[whole(most * wide, wide)] * 2 + [whole(wide, wide)] * 2,
        out_shape=[jax.ShapeDtypeStruct((tops, most * wide, wide), bf16)] * 2
        + [jax.ShapeDtypeStruct((tops, wide, wide), bf16)] * 2,
        scratch_shapes=[pltpu.VMEM((width, wide, wide), f32)],
        compiler_params=params(),
        name="top_prepare",
    )(top_places.astype(jnp.int32), after(results[4], top))

    incoming = lax.all_to_all(results[4], ("xy", "zh"), split_axis=0, concat_axis=0, tiled=True)
    outgoing = pl.pallas_call(
        functools.partial(top_kernel, above, paths),
        in_specs=[VMEM] * 5,
        out_specs=VMEM,
        out_shape=jax.ShapeDtypeStruct((tops, width + 1, part, wide), f32),
        compiler_params=params(),
        name="top_solve",
    )(incoming, *top_factor)
    state = lax.all_to_all(outgoing, ("xy", "zh"), split_axis=0, concat_axis=0, tiled=True)
    own_top = state[:groups, width].reshape(1, columns, wide)

    found = [None] * TURNS
    chunk = jax.ShapeDtypeStruct((turn, columns, wide), f32)
    for k in range(TURNS - 1, -1, -1):
        held = max(i for i, at in enumerate(starts[:-1]) if at <= k * turn)
        part_of = [
            pl.BlockSpec(
                (turn,) + shape, functools.partial(lambda at, i: (at, 0, 0), k - starts[held] // turn)
            )
            for shape in ((3 * wide, wide), (3 * wide, wide), (columns, wide))
        ]
        found[k], state = pl.pallas_call(
            functools.partial(backward_kernel, k * turn, k == TURNS - 1, width),
            grid=(1,),
            in_specs=[SMEM] + part_of + [VMEM],
            out_specs=[VMEM] * 2,
            out_shape=[chunk, vectors],
            compiler_params=params(),
            cost_estimate=cost,
            name="leaf_backward",
        )(meta, *factors[held], state)
    late = swap(found[-1])
    middle = swap(jnp.concatenate(found[1:-1] + [own_top], axis=0))
    first = swap(after(late, found[0]))
    leaf_solution = jnp.concatenate([first, middle[:-1], late], axis=0)
    return (leaf_solution, middle[-1:])


def solution(mesh):
    subtrees, quarters = mesh.devices.shape
    fine = Mesh(
        mesh.devices.reshape(subtrees // 2, 2, 2, quarters // 2), ("xy", "core", "zh", "zl")
    )
    sn, rhs = ("xy", "core"), ("zh", "zl")
    return jax.shard_map(
        local,
        mesh=fine,
        in_specs=(
            P(sn, rhs, None),
            P(sn, rhs, None),
            P(sn, None, rhs, None),
            P(sn, rhs, None),
            P(sn, None),
            P(None, sn, rhs, None),
            P(sn, rhs, None),
        ),
        out_specs=(P(sn, rhs, None), P(sn, rhs, None)),
        check_vma=False,
    )
```

```python
import functools

import jax
import jax.numpy as jnp
import numpy as np
from jax import lax
from jax.experimental import pallas as pl
from jax.experimental.pallas import tpu as pltpu
from jax.sharding import Mesh
from jax.sharding import PartitionSpec as P

CHUNKS = (3, 1)
TURNS = 4
GROUP = 4
f32 = jnp.float32
bf16 = jnp.bfloat16
SMEM = pl.BlockSpec(memory_space=pltpu.SMEM)
VMEM = pl.BlockSpec(memory_space=pltpu.VMEM)


def params():
    return pltpu.CompilerParams(vmem_limit_bytes=28 * 2**20)


def split(value):
    high = value.astype(bf16)
    return high, (value - high.astype(f32)).astype(bf16)


def product(left, right, transposed):
    dims = (((1,), (1 if transposed else 0,)), ((), ()))

    def dot(a, b):
        return lax.dot_general(a, b, dims, preferred_element_type=f32)

    rows = left[0].shape[0]
    if rows % 16:
        return dot(left[0], right[0]) + (dot(left[1], right[0]) + dot(left[0], right[1]))
    both = dot(jnp.concatenate(left, axis=0), right[0])
    return both[:rows] + (both[rows:] + dot(left[0], right[1]))


def ancestors_of(tops):
    def level(t):
        return ((t + 1) & -(t + 1)).bit_length() - 1

    return [[t for t in range(j + 1, tops) if t + 1 - 2 ** level(t) <= j] for j in range(tops)]


def paths_of(subtrees, above):
    return [[4 * (d // 4)] + above[4 * (d // 4)] for d in range(subtrees)]


def padded(rows, width):
    return np.array([row + [row[0] if row else 0] * (width - len(row)) for row in rows], np.int32)


def forward_kernel(base, leafs, first, last, width, *refs):
    meta, kept, passed, rhs, rhs_top = refs[0], refs[1:5], refs[5:9], refs[9], refs[10]
    refs = refs[11:]
    if not first:
        acc_in, refs = refs[0], refs[1:]
    acc, high, low, scaled, refs = refs[0], refs[1], refs[2], refs[3], refs[4:]
    if last:
        payload, refs = refs[0], refs[1:]
    full, arrived = refs
    steps, columns, rows = scaled.shape[0], scaled.shape[1], kept[0].shape[2]
    wide = full.shape[2]

    def copies(pieces, group):
        made = []
        for place, piece in enumerate(pieces):
            offset = pl.multiple_of(meta[3 * leafs + place] * rows, rows)
            start = group * GROUP + (base if piece.shape[0] > steps else 0)
            made.append(
                pltpu.make_async_copy(
                    piece.at[pl.ds(start, GROUP)],
                    full.at[pl.ds(group * GROUP, GROUP), :, pl.ds(offset, rows), :],
                    arrived.at[group, place],
                )
            )
        return made

    def start(pieces):
        for group in range(steps // GROUP):
            for copy in copies(pieces, group):
                copy.start()

    keeps = meta[3 * leafs + 4 + width]
    pl.when(keeps == 1)(lambda: start(kept))
    pl.when(keeps == 0)(lambda: start(passed))
    if first:
        acc[...] = jnp.zeros_like(acc)
    else:
        acc[...] = acc_in[...]
    for group in range(steps // GROUP):
        for copy in copies(kept, group):
            copy.wait()
        members = range(group * GROUP, (group + 1) * GROUP)
        for s in members:
            blocks = split(full[s, 0:3].reshape(3 * wide, wide))
            merged = split(product(blocks, split(full[s, 3]), False))
            high[s] = merged[0]
            low[s] = merged[1]
        for s in members:
            at = s * columns
            source = split(rhs[at : at + columns] - acc[base + s])
            outgoing = product(source, (high[s], low[s]), True)
            for r in range(3):
                target = meta[3 * (base + s) + r]
                acc[target] = acc[target] + outgoing[:, r * wide : (r + 1) * wide]
            inverse = split(full[s, 3])
            solved = split(product(source, inverse, True))
            scaled[s] = product(solved, inverse, False)
    if last:
        peers, part = payload.shape[0], payload.shape[2]
        groups = columns // part
        for i in range(width + 1):
            node = acc[leafs + meta[3 * leafs + 4 + i]] if i < width else rhs_top[...]
            for p in range(peers):
                at = (p % groups) * part
                payload[p, i] = node[at : at + part]


def backward_kernel(base, first, width, meta, high, low, scaled, state, out, z):
    steps, wide = scaled.shape[0], scaled.shape[2]
    leafs = steps * TURNS
    if first:
        part = state.shape[2]
        groups = scaled.shape[1] // part
        z[...] = jnp.zeros_like(z)
        for i in range(width):
            node = leafs + meta[3 * leafs + 4 + i]
            for p in range(groups):
                z[node, p * part : (p + 1) * part, :] = state[p, i]
    else:
        z[...] = state[...]
    for s in range(steps - 1, -1, -1):
        total = scaled[s]
        for r in (2, 1, 0):
            source = split(z[meta[3 * (base + s) + r]])
            at = slice(r * wide, (r + 1) * wide)
            total = total - product(source, (high[s, at], low[s, at]), False)
        z[base + s] = total
        out[s] = total


def top_prepare_kernel(places, top, high, low, inverse_high, inverse_low, full):
    blocks, rows, wide = top.shape[2], top.shape[3], top.shape[4]
    for place in range(top.shape[1]):
        offset = pl.multiple_of(places[place] * rows, rows)
        full[:, pl.ds(offset, rows), :] = top[0, place]
    inverse = split(full[blocks - 1])
    merged = product(split(full[: blocks - 1].reshape((blocks - 1) * wide, wide)), inverse, False)
    high[0], low[0] = split(merged)
    inverse_high[0], inverse_low[0] = inverse


def top_kernel(above, paths, incoming, high, low, inverse_high, inverse_low, outgoing):
    tops, wide = len(above), high.shape[2]
    width = outgoing.shape[1] - 1
    sources = [incoming[t, width] for t in range(tops)]
    for d, path in enumerate(paths):
        for i, t in enumerate(path):
            sources[t] = sources[t] - incoming[d, i]
    scaled = []
    for j in range(tops):
        source = split(sources[j])
        count = len(above[j])
        if count:
            rows = slice(0, count * wide)
            updates = product(source, (high[j, rows], low[j, rows]), True)
            for i, t in enumerate(above[j]):
                sources[t] = sources[t] - updates[:, i * wide : (i + 1) * wide]
        inverse = (inverse_high[j], inverse_low[j])
        scaled.append(product(split(product(source, inverse, True)), inverse, False))
    solved = [None] * tops
    parts = [None] * tops
    for j in range(tops - 1, -1, -1):
        total = scaled[j]
        for i, t in enumerate(above[j]):
            rows = slice(i * wide, (i + 1) * wide)
            total = total - product(parts[t], (high[j, rows], low[j, rows]), False)
        solved[j] = total
        parts[j] = split(total)
    for p in range(outgoing.shape[0]):
        path = paths[p]
        for i in range(width):
            outgoing[p, i] = solved[path[i] if i < len(path) else path[0]]
        outgoing[p, width] = solved[p]


def local(rhs_leaf, rhs_top, leaf_blocks, leaf_dinv, leaf_struct, top_blocks, top_dinv):
    leafs, columns, wide = rhs_leaf.shape
    tops = top_blocks.shape[0]
    turn = leafs // TURNS
    starts = [turn * sum(CHUNKS[:k]) for k in range(len(CHUNKS) + 1)]
    above = ancestors_of(tops)
    most = max(len(row) for row in above)
    width = most + 1
    paths = paths_of(tops, above)
    groups = min(tops, columns // 8)
    part = columns // groups

    core, zh, zl = lax.axis_index("core"), lax.axis_index("zh"), lax.axis_index("zl")
    xy = lax.axis_index("xy")

    def swap(value):
        return lax.ppermute(value, ("core", "zh"), [(0, 0), (1, 2), (2, 1), (3, 3)])

    def to_keeper(value):
        return lax.ppermute(value, ("core", "zh"), [(1, 0), (2, 3)])

    def to_trader(value):
        return lax.ppermute(value, ("core", "zh"), [(0, 2), (3, 1)])

    def keepers(value):
        return lax.ppermute(value, ("core", "zh", "zl"), [(0, 1), (1, 0), (6, 7), (7, 6)])

    def other(value, *axes):
        last = 2 ** len(axes) - 1
        return lax.ppermute(value, axes, [(i, last - i) for i in range(last + 1)])

    def after(first, value):
        return lax.optimization_barrier((first, value))[1]

    chosen = jnp.take(top_blocks[:, 0], jnp.asarray(padded(above, most))[2 * xy + core], axis=0)
    top = jnp.concatenate([chosen, top_dinv], axis=0)
    top = jnp.stack([top, other(top, "zh")])
    top = jnp.concatenate([top, other(top, "zl")])

    names = jnp.zeros((8, wide), f32).at[:3, :leafs].set(leaf_struct.T.astype(f32))
    sides = jnp.concatenate([rhs_leaf.reshape(-1, wide), rhs_top.reshape(-1, wide), names], axis=0)
    def joined(at):
        return jnp.concatenate([leaf_blocks[at], leaf_dinv[at][:, None]], axis=1)

    own = joined(slice(None))
    parts = [joined(slice(at, end)) for at, end in zip(starts, starts[1:])]
    own, parts, sides = after(top, (own, parts, sides))

    near = keepers(own)
    sides = swap(sides)
    far = [to_keeper(part) for part in parts]
    across = [keepers(far[0])]
    early = [to_trader(value) for value in (own, near, far[0])]
    across += [keepers(after(early[:2], value)) for value in far[1:]]
    top = lax.all_gather(after((far[-1], sides), top), ("xy", "core"), axis=0, tiled=False)

    names = sides[(leafs + 1) * columns :][:3, :leafs].T.astype(jnp.int32).reshape(-1)
    path = jnp.asarray(padded(paths, width))[2 * xy + zh]
    places = jnp.stack([2 * zh + zl, 2 * zh + 1 - zl, 2 - 2 * zh + zl, 3 - 2 * zh - zl])
    keeps = (core == zh).astype(jnp.int32)
    meta = jnp.concatenate([names, places.astype(jnp.int32), path, keeps[None]])

    vectors = jax.ShapeDtypeStruct((leafs + tops, columns, wide), f32)
    cost = pl.CostEstimate(flops=2**20, bytes_accessed=2**10, transcendentals=0)
    factors, state = [], None
    for k, base in enumerate(starts[:-1]):
        last = k == len(CHUNKS) - 1
        steps = starts[k + 1] - base
        merged = jax.ShapeDtypeStruct((steps, 3 * wide, wide), bf16)
        chunk = jax.ShapeDtypeStruct((steps, columns, wide), f32)
        shapes = [vectors, merged, merged, chunk]
        if k == 0:
            passed = (early[2], to_trader(after(far[-1], across[k])))
        else:
            passed = (to_trader(far[k]), to_trader(after(state, across[k])))
        specs = [SMEM] + [pl.BlockSpec(memory_space=pl.ANY)] * 8 + [
            pl.BlockSpec((steps * columns, wide), functools.partial(lambda k, i: (k, 0), base // steps)),
            pl.BlockSpec((columns, wide), lambda i: (leafs, 0)),
        ]
        if last:
            shapes.append(jax.ShapeDtypeStruct((tops, width + 1, part, wide), f32))
        before = () if k == 0 else (state,)
        results = pl.pallas_call(
            functools.partial(forward_kernel, base, leafs, k == 0, last, width),
            grid=(1,),
            in_specs=specs + [VMEM] * (k > 0),
            out_specs=[VMEM] * len(shapes),
            out_shape=shapes,
            scratch_shapes=[
                pltpu.VMEM((steps, 4, wide, wide), f32),
                pltpu.SemaphoreType.DMA((steps // GROUP, 4)),
            ],
            compiler_params=params(),
            cost_estimate=cost,
            name="leaf_forward",
        )(meta, own, near, far[k], across[k], *early[:2], *passed, sides, sides, *before)
        state = results[0]
        factors.append(results[1:4])

    def whole(*shape):
        return pl.BlockSpec((1,) + shape, lambda t: (t,) + (0,) * len(shape))

    top_places = jnp.stack([2 * zh + zl, 2 - 2 * zh + zl, 2 * zh + 1 - zl, 3 - 2 * zh - zl])
    top_factor = pl.pallas_call(
        top_prepare_kernel,
        grid=(tops,),
        in_specs=[SMEM, whole(*top.shape[1:])],
        out_specs=[whole(most * wide, wide)] * 2 + [whole(wide, wide)] * 2,
        out_shape=[jax.ShapeDtypeStruct((tops, most * wide, wide), bf16)] * 2
        + [jax.ShapeDtypeStruct((tops, wide, wide), bf16)] * 2,
        scratch_shapes=[pltpu.VMEM((width, wide, wide), f32)],
        compiler_params=params(),
        name="top_prepare",
    )(top_places.astype(jnp.int32), after(results[4], top))

    incoming = lax.all_to_all(results[4], ("xy", "zh"), split_axis=0, concat_axis=0, tiled=True)
    outgoing = pl.pallas_call(
        functools.partial(top_kernel, above, paths),
        in_specs=[VMEM] * 5,
        out_specs=VMEM,
        out_shape=jax.ShapeDtypeStruct((tops, width + 1, part, wide), f32),
        compiler_params=params(),
        name="top_solve",
    )(incoming, *top_factor)
    state = lax.all_to_all(outgoing, ("xy", "zh"), split_axis=0, concat_axis=0, tiled=True)
    own_top = state[:groups, width].reshape(1, columns, wide)

    found = [None] * TURNS
    chunk = jax.ShapeDtypeStruct((turn, columns, wide), f32)
    for k in range(TURNS - 1, -1, -1):
        held = max(i for i, at in enumerate(starts[:-1]) if at <= k * turn)
        part_of = [
            pl.BlockSpec(
                (turn,) + shape, functools.partial(lambda at, i: (at, 0, 0), k - starts[held] // turn)
            )
            for shape in ((3 * wide, wide), (3 * wide, wide), (columns, wide))
        ]
        found[k], state = pl.pallas_call(
            functools.partial(backward_kernel, k * turn, k == TURNS - 1, width),
            grid=(1,),
            in_specs=[SMEM] + part_of + [VMEM],
            out_specs=[VMEM] * 2,
            out_shape=[chunk, vectors],
            compiler_params=params(),
            cost_estimate=cost,
            name="leaf_backward",
        )(meta, *factors[held], state)
    half = TURNS // 2
    late = swap(jnp.concatenate(found[half:] + [own_top], axis=0))
    first = swap(jnp.concatenate(found[:half], axis=0))
    leaf_solution = jnp.concatenate([first, late[:-1]], axis=0)
    return (leaf_solution, late[-1:])


def solution(mesh):
    subtrees, quarters = mesh.devices.shape
    fine = Mesh(
        mesh.devices.reshape(subtrees // 2, 2, 2, quarters // 2), ("xy", "core", "zh", "zl")
    )
    sn, rhs = ("xy", "core"), ("zh", "zl")
    return jax.shard_map(
        local,
        mesh=fine,
        in_specs=(
            P(sn, rhs, None),
            P(sn, rhs, None),
            P(sn, None, rhs, None),
            P(sn, rhs, None),
            P(sn, None),
            P(None, sn, rhs, None),
            P(sn, rhs, None),
        ),
        out_specs=(P(sn, rhs, None), P(sn, rhs, None)),
        check_vma=False,
    )
```

```python
import functools

import jax
import jax.numpy as jnp
import numpy as np
from jax import lax
from jax.experimental import pallas as pl
from jax.experimental.pallas import tpu as pltpu
from jax.sharding import Mesh
from jax.sharding import PartitionSpec as P

CHUNKS = (3, 1)
TURNS = 4
GROUP = 4
f32 = jnp.float32
bf16 = jnp.bfloat16
SMEM = pl.BlockSpec(memory_space=pltpu.SMEM)
VMEM = pl.BlockSpec(memory_space=pltpu.VMEM)


def params():
    return pltpu.CompilerParams(vmem_limit_bytes=28 * 2**20)


def split(value):
    high = value.astype(bf16)
    return high, (value - high.astype(f32)).astype(bf16)


def product(left, right, transposed):
    dims = (((1,), (1 if transposed else 0,)), ((), ()))

    def dot(a, b):
        return lax.dot_general(a, b, dims, preferred_element_type=f32)

    rows = left[0].shape[0]
    if rows % 16:
        return dot(left[0], right[0]) + (dot(left[1], right[0]) + dot(left[0], right[1]))
    both = dot(jnp.concatenate(left, axis=0), right[0])
    return both[:rows] + (both[rows:] + dot(left[0], right[1]))


def ancestors_of(tops):
    def level(t):
        return ((t + 1) & -(t + 1)).bit_length() - 1

    return [[t for t in range(j + 1, tops) if t + 1 - 2 ** level(t) <= j] for j in range(tops)]


def paths_of(subtrees, above):
    return [[4 * (d // 4)] + above[4 * (d // 4)] for d in range(subtrees)]


def padded(rows, width):
    return np.array([row + [row[0] if row else 0] * (width - len(row)) for row in rows], np.int32)


def forward_kernel(base, leafs, first, last, width, *refs):
    meta, kept, passed, rhs, rhs_top = refs[0], refs[1:5], refs[5:9], refs[9], refs[10]
    refs = refs[11:]
    if not first:
        acc_in, refs = refs[0], refs[1:]
    acc, high, low, scaled, refs = refs[0], refs[1], refs[2], refs[3], refs[4:]
    if last:
        payload, refs = refs[0], refs[1:]
    full, arrived = refs
    steps, columns, rows = scaled.shape[0], scaled.shape[1], kept[0].shape[2]
    wide = full.shape[2]

    def copies(pieces, group):
        made = []
        for place, piece in enumerate(pieces):
            offset = pl.multiple_of(meta[3 * leafs + place] * rows, rows)
            start = group * GROUP + (base if piece.shape[0] > steps else 0)
            made.append(
                pltpu.make_async_copy(
                    piece.at[pl.ds(start, GROUP)],
                    full.at[pl.ds(group * GROUP, GROUP), :, pl.ds(offset, rows), :],
                    arrived.at[group, place],
                )
            )
        return made

    def start(pieces):
        for group in range(steps // GROUP):
            for copy in copies(pieces, group):
                copy.start()

    keeps = meta[3 * leafs + 4 + width]
    pl.when(keeps == 1)(lambda: start(kept))
    pl.when(keeps == 0)(lambda: start(passed))
    if first:
        acc[...] = jnp.zeros_like(acc)
    else:
        acc[...] = acc_in[...]
    for group in range(steps // GROUP):
        for copy in copies(kept, group):
            copy.wait()
        members = range(group * GROUP, (group + 1) * GROUP)
        for s in members:
            blocks = split(full[s, 0:3].reshape(3 * wide, wide))
            merged = split(product(blocks, split(full[s, 3]), False))
            high[s] = merged[0]
            low[s] = merged[1]
        for s in members:
            at = s * columns
            source = split(rhs[at : at + columns] - acc[base + s])
            outgoing = product(source, (high[s], low[s]), True)
            for r in range(3):
                target = meta[3 * (base + s) + r]
                acc[target] = acc[target] + outgoing[:, r * wide : (r + 1) * wide]
            inverse = split(full[s, 3])
            solved = split(product(source, inverse, True))
            scaled[s] = product(solved, inverse, False)
    if last:
        peers, part = payload.shape[0], payload.shape[2]
        groups = columns // part
        for i in range(width + 1):
            node = acc[leafs + meta[3 * leafs + 4 + i]] if i < width else rhs_top[...]
            for p in range(peers):
                at = (p % groups) * part
                payload[p, i] = node[at : at + part]


def backward_kernel(base, first, width, meta, high, low, scaled, state, out, z):
    steps, wide = scaled.shape[0], scaled.shape[2]
    leafs = steps * TURNS
    if first:
        part = state.shape[2]
        groups = scaled.shape[1] // part
        z[...] = jnp.zeros_like(z)
        for i in range(width):
            node = leafs + meta[3 * leafs + 4 + i]
            for p in range(groups):
                z[node, p * part : (p + 1) * part, :] = state[p, i]
    else:
        z[...] = state[...]
    for s in range(steps - 1, -1, -1):
        total = scaled[s]
        for r in (2, 1, 0):
            source = split(z[meta[3 * (base + s) + r]])
            at = slice(r * wide, (r + 1) * wide)
            total = total - product(source, (high[s, at], low[s, at]), False)
        z[base + s] = total
        out[s] = total


def top_prepare_kernel(places, top, high, low, inverse_high, inverse_low, full):
    blocks, rows, wide = top.shape[2], top.shape[3], top.shape[4]
    for place in range(top.shape[1]):
        offset = pl.multiple_of(places[place] * rows, rows)
        full[:, pl.ds(offset, rows), :] = top[0, place]
    inverse = split(full[blocks - 1])
    merged = product(split(full[: blocks - 1].reshape((blocks - 1) * wide, wide)), inverse, False)
    high[0], low[0] = split(merged)
    inverse_high[0], inverse_low[0] = inverse


def top_kernel(above, paths, incoming, high, low, inverse_high, inverse_low, outgoing):
    tops, wide = len(above), high.shape[2]
    width = outgoing.shape[1] - 1
    sources = [incoming[t, width] for t in range(tops)]
    for d, path in enumerate(paths):
        for i, t in enumerate(path):
            sources[t] = sources[t] - incoming[d, i]
    scaled = []
    for j in range(tops):
        source = split(sources[j])
        count = len(above[j])
        if count:
            rows = slice(0, count * wide)
            updates = product(source, (high[j, rows], low[j, rows]), True)
            for i, t in enumerate(above[j]):
                sources[t] = sources[t] - updates[:, i * wide : (i + 1) * wide]
        inverse = (inverse_high[j], inverse_low[j])
        scaled.append(product(split(product(source, inverse, True)), inverse, False))
    solved = [None] * tops
    parts = [None] * tops
    for j in range(tops - 1, -1, -1):
        total = scaled[j]
        for i, t in enumerate(above[j]):
            rows = slice(i * wide, (i + 1) * wide)
            total = total - product(parts[t], (high[j, rows], low[j, rows]), False)
        solved[j] = total
        parts[j] = split(total)
    for p in range(outgoing.shape[0]):
        path = paths[p]
        for i in range(width):
            outgoing[p, i] = solved[path[i] if i < len(path) else path[0]]
        outgoing[p, width] = solved[p]


def local(rhs_leaf, rhs_top, leaf_blocks, leaf_dinv, leaf_struct, top_blocks, top_dinv):
    leafs, columns, wide = rhs_leaf.shape
    tops = top_blocks.shape[0]
    turn = leafs // TURNS
    starts = [turn * sum(CHUNKS[:k]) for k in range(len(CHUNKS) + 1)]
    above = ancestors_of(tops)
    most = max(len(row) for row in above)
    width = most + 1
    paths = paths_of(tops, above)
    groups = min(tops, columns // 8)
    part = columns // groups

    core, zh, zl = lax.axis_index("core"), lax.axis_index("zh"), lax.axis_index("zl")
    xy = lax.axis_index("xy")

    def swap(value):
        return lax.ppermute(value, ("core", "zh"), [(0, 0), (1, 2), (2, 1), (3, 3)])

    def to_keeper(value):
        return lax.ppermute(value, ("core", "zh"), [(1, 0), (2, 3)])

    def to_trader(value):
        return lax.ppermute(value, ("core", "zh"), [(0, 2), (3, 1)])

    def keepers(value):
        return lax.ppermute(value, ("core", "zh", "zl"), [(0, 1), (1, 0), (6, 7), (7, 6)])

    def other(value, *axes):
        last = 2 ** len(axes) - 1
        return lax.ppermute(value, axes, [(i, last - i) for i in range(last + 1)])

    def after(first, value):
        return lax.optimization_barrier((first, value))[1]

    chosen = jnp.take(top_blocks[:, 0], jnp.asarray(padded(above, most))[2 * xy + core], axis=0)
    top = jnp.concatenate([chosen, top_dinv], axis=0)
    top = jnp.stack([top, other(top, "zh")])
    top = jnp.concatenate([top, other(top, "zl")])

    names = jnp.zeros((8, wide), f32).at[:3, :leafs].set(leaf_struct.T.astype(f32))
    sides = jnp.concatenate([rhs_leaf.reshape(-1, wide), rhs_top.reshape(-1, wide), names], axis=0)
    def joined(at):
        return jnp.concatenate([leaf_blocks[at], leaf_dinv[at][:, None]], axis=1)

    own = joined(slice(None))
    parts = [joined(slice(at, end)) for at, end in zip(starts, starts[1:])]
    own, parts, sides = after(top, (own, parts, sides))

    near = keepers(own)
    sides = swap(sides)
    far = [to_keeper(part) for part in parts]
    early = [to_trader(value) for value in (own, near, far[0])]
    across = [keepers(after(early, far[0]))] + [keepers(value) for value in far[1:]]
    top = lax.all_gather(after((far[-1], sides), top), ("xy", "core"), axis=0, tiled=False)

    names = sides[(leafs + 1) * columns :][:3, :leafs].T.astype(jnp.int32).reshape(-1)
    path = jnp.asarray(padded(paths, width))[2 * xy + zh]
    places = jnp.stack([2 * zh + zl, 2 * zh + 1 - zl, 2 - 2 * zh + zl, 3 - 2 * zh - zl])
    keeps = (core == zh).astype(jnp.int32)
    meta = jnp.concatenate([names, places.astype(jnp.int32), path, keeps[None]])

    vectors = jax.ShapeDtypeStruct((leafs + tops, columns, wide), f32)
    cost = pl.CostEstimate(flops=2**20, bytes_accessed=8 * 2**20, transcendentals=0)
    factors, state = [], None
    for k, base in enumerate(starts[:-1]):
        last = k == len(CHUNKS) - 1
        steps = starts[k + 1] - base
        merged = jax.ShapeDtypeStruct((steps, 3 * wide, wide), bf16)
        chunk = jax.ShapeDtypeStruct((steps, columns, wide), f32)
        shapes = [vectors, merged, merged, chunk]
        if k == 0:
            passed = (early[2], to_trader(across[k]))
        else:
            passed = (to_trader(far[k]), to_trader(after(state, across[k])))
        specs = [SMEM] + [pl.BlockSpec(memory_space=pl.ANY)] * 8 + [
            pl.BlockSpec((steps * columns, wide), functools.partial(lambda k, i: (k, 0), base // steps)),
            pl.BlockSpec((columns, wide), lambda i: (leafs, 0)),
        ]
        if last:
            shapes.append(jax.ShapeDtypeStruct((tops, width + 1, part, wide), f32))
        before = () if k == 0 else (state,)
        results = pl.pallas_call(
            functools.partial(forward_kernel, base, leafs, k == 0, last, width),
            grid=(1,),
            in_specs=specs + [VMEM] * (k > 0),
            out_specs=[VMEM] * len(shapes),
            out_shape=shapes,
            scratch_shapes=[
                pltpu.VMEM((steps, 4, wide, wide), f32),
                pltpu.SemaphoreType.DMA((steps // GROUP, 4)),
            ],
            compiler_params=params(),
            cost_estimate=cost,
            name="leaf_forward",
        )(meta, own, near, far[k], across[k], *early[:2], *passed, sides, sides, *before)
        state = results[0]
        factors.append(results[1:4])

    def whole(*shape):
        return pl.BlockSpec((1,) + shape, lambda t: (t,) + (0,) * len(shape))

    top_places = jnp.stack([2 * zh + zl, 2 - 2 * zh + zl, 2 * zh + 1 - zl, 3 - 2 * zh - zl])
    top_factor = pl.pallas_call(
        top_prepare_kernel,
        grid=(tops,),
        in_specs=[SMEM, whole(*top.shape[1:])],
        out_specs=[whole(most * wide, wide)] * 2 + [whole(wide, wide)] * 2,
        out_shape=[jax.ShapeDtypeStruct((tops, most * wide, wide), bf16)] * 2
        + [jax.ShapeDtypeStruct((tops, wide, wide), bf16)] * 2,
        scratch_shapes=[pltpu.VMEM((width, wide, wide), f32)],
        compiler_params=params(),
        name="top_prepare",
    )(top_places.astype(jnp.int32), after(results[4], top))

    incoming = lax.all_to_all(results[4], ("xy", "zh"), split_axis=0, concat_axis=0, tiled=True)
    outgoing = pl.pallas_call(
        functools.partial(top_kernel, above, paths),
        in_specs=[VMEM] * 5,
        out_specs=VMEM,
        out_shape=jax.ShapeDtypeStruct((tops, width + 1, part, wide), f32),
        compiler_params=params(),
        name="top_solve",
    )(incoming, *top_factor)
    state = lax.all_to_all(outgoing, ("xy", "zh"), split_axis=0, concat_axis=0, tiled=True)
    own_top = state[:groups, width].reshape(1, columns, wide)

    found = [None] * TURNS
    chunk = jax.ShapeDtypeStruct((turn, columns, wide), f32)
    cost = pl.CostEstimate(flops=4 * 10**9, bytes_accessed=8 * 2**20, transcendentals=0)
    for k in range(TURNS - 1, -1, -1):
        held = max(i for i, at in enumerate(starts[:-1]) if at <= k * turn)
        part_of = [
            pl.BlockSpec(
                (turn,) + shape, functools.partial(lambda at, i: (at, 0, 0), k - starts[held] // turn)
            )
            for shape in ((3 * wide, wide), (3 * wide, wide), (columns, wide))
        ]
        found[k], state = pl.pallas_call(
            functools.partial(backward_kernel, k * turn, k == TURNS - 1, width),
            grid=(1,),
            in_specs=[SMEM] + part_of + [VMEM],
            out_specs=[VMEM] * 2,
            out_shape=[chunk, vectors],
            compiler_params=params(),
            cost_estimate=cost,
            name="leaf_backward",
        )(meta, *factors[held], state)
    half = TURNS // 2
    late = swap(jnp.concatenate(found[half:] + [own_top], axis=0))
    first = swap(jnp.concatenate(found[:half], axis=0))
    leaf_solution = jnp.concatenate([first, late[:-1]], axis=0)
    return (leaf_solution, late[-1:])


def solution(mesh):
    subtrees, quarters = mesh.devices.shape
    fine = Mesh(
        mesh.devices.reshape(subtrees // 2, 2, 2, quarters // 2), ("xy", "core", "zh", "zl")
    )
    sn, rhs = ("xy", "core"), ("zh", "zl")
    return jax.shard_map(
        local,
        mesh=fine,
        in_specs=(
            P(sn, rhs, None),
            P(sn, rhs, None),
            P(sn, None, rhs, None),
            P(sn, rhs, None),
            P(sn, None),
            P(None, sn, rhs, None),
            P(sn, rhs, None),
        ),
        out_specs=(P(sn, rhs, None), P(sn, rhs, None)),
        check_vma=False,
    )
```

```python
import functools

import jax
import jax.numpy as jnp
import numpy as np
from jax import lax
from jax.experimental import pallas as pl
from jax.experimental.pallas import tpu as pltpu
from jax.sharding import Mesh
from jax.sharding import PartitionSpec as P

CHUNKS = (3, 1)
TURNS = 4
GROUP = 4
f32 = jnp.float32
bf16 = jnp.bfloat16
SMEM = pl.BlockSpec(memory_space=pltpu.SMEM)
VMEM = pl.BlockSpec(memory_space=pltpu.VMEM)


def params():
    return pltpu.CompilerParams(vmem_limit_bytes=28 * 2**20)


def split(value):
    high = value.astype(bf16)
    return high, (value - high.astype(f32)).astype(bf16)


def product(left, right, transposed):
    dims = (((1,), (1 if transposed else 0,)), ((), ()))

    def dot(a, b):
        return lax.dot_general(a, b, dims, preferred_element_type=f32)

    rows = left[0].shape[0]
    if rows % 16:
        return dot(left[0], right[0]) + (dot(left[1], right[0]) + dot(left[0], right[1]))
    both = dot(jnp.concatenate(left, axis=0), right[0])
    return both[:rows] + (both[rows:] + dot(left[0], right[1]))


def ancestors_of(tops):
    def level(t):
        return ((t + 1) & -(t + 1)).bit_length() - 1

    return [[t for t in range(j + 1, tops) if t + 1 - 2 ** level(t) <= j] for j in range(tops)]


def paths_of(subtrees, above):
    return [[4 * (d // 4)] + above[4 * (d // 4)] for d in range(subtrees)]


def padded(rows, width):
    return np.array([row + [row[0] if row else 0] * (width - len(row)) for row in rows], np.int32)


def forward_kernel(base, leafs, first, last, width, *refs):
    meta, kept, passed, rhs, rhs_top = refs[0], refs[1:5], refs[5:9], refs[9], refs[10]
    refs = refs[11:]
    if not first:
        acc_in, refs = refs[0], refs[1:]
    acc, high, low, scaled, refs = refs[0], refs[1], refs[2], refs[3], refs[4:]
    if last:
        payload, refs = refs[0], refs[1:]
    full, arrived = refs
    steps, columns, rows = scaled.shape[0], scaled.shape[1], kept[0].shape[2]
    wide = full.shape[2]

    def copies(pieces, group):
        made = []
        for place, piece in enumerate(pieces):
            offset = pl.multiple_of(meta[3 * leafs + place] * rows, rows)
            start = group * GROUP + (base if piece.shape[0] > steps else 0)
            made.append(
                pltpu.make_async_copy(
                    piece.at[pl.ds(start, GROUP)],
                    full.at[pl.ds(group * GROUP, GROUP), :, pl.ds(offset, rows), :],
                    arrived.at[group, place],
                )
            )
        return made

    def start(pieces):
        for group in range(steps // GROUP):
            for copy in copies(pieces, group):
                copy.start()

    keeps = meta[3 * leafs + 4 + width]
    pl.when(keeps == 1)(lambda: start(kept))
    pl.when(keeps == 0)(lambda: start(passed))
    if first:
        acc[...] = jnp.zeros_like(acc)
    else:
        acc[...] = acc_in[...]
    for group in range(steps // GROUP):
        for copy in copies(kept, group):
            copy.wait()
        members = range(group * GROUP, (group + 1) * GROUP)
        for s in members:
            blocks = split(full[s, 0:3].reshape(3 * wide, wide))
            merged = split(product(blocks, split(full[s, 3]), False))
            high[s] = merged[0]
            low[s] = merged[1]
        for s in members:
            at = s * columns
            source = split(rhs[at : at + columns] - acc[base + s])
            outgoing = product(source, (high[s], low[s]), True)
            for r in range(3):
                target = meta[3 * (base + s) + r]
                acc[target] = acc[target] + outgoing[:, r * wide : (r + 1) * wide]
            inverse = split(full[s, 3])
            solved = split(product(source, inverse, True))
            scaled[s] = product(solved, inverse, False)
    if last:
        peers, part = payload.shape[0], payload.shape[2]
        groups = columns // part
        for i in range(width + 1):
            node = acc[leafs + meta[3 * leafs + 4 + i]] if i < width else rhs_top[...]
            for p in range(peers):
                at = (p % groups) * part
                payload[p, i] = node[at : at + part]


def backward_kernel(base, first, width, meta, high, low, scaled, state, out, z):
    steps, wide = scaled.shape[0], scaled.shape[2]
    leafs = steps * TURNS
    if first:
        part = state.shape[2]
        groups = scaled.shape[1] // part
        z[...] = jnp.zeros_like(z)
        for i in range(width):
            node = leafs + meta[3 * leafs + 4 + i]
            for p in range(groups):
                z[node, p * part : (p + 1) * part, :] = state[p, i]
    else:
        z[...] = state[...]
    for s in range(steps - 1, -1, -1):
        total = scaled[s]
        for r in (2, 1, 0):
            source = split(z[meta[3 * (base + s) + r]])
            at = slice(r * wide, (r + 1) * wide)
            total = total - product(source, (high[s, at], low[s, at]), False)
        z[base + s] = total
        out[s] = total


def top_prepare_kernel(places, top, high, low, inverse_high, inverse_low, full):
    blocks, rows, wide = top.shape[2], top.shape[3], top.shape[4]
    for place in range(top.shape[1]):
        offset = pl.multiple_of(places[place] * rows, rows)
        full[:, pl.ds(offset, rows), :] = top[0, place]
    inverse = split(full[blocks - 1])
    merged = product(split(full[: blocks - 1].reshape((blocks - 1) * wide, wide)), inverse, False)
    high[0], low[0] = split(merged)
    inverse_high[0], inverse_low[0] = inverse


def top_kernel(above, paths, incoming, high, low, inverse_high, inverse_low, outgoing):
    tops, wide = len(above), high.shape[2]
    width = outgoing.shape[1] - 1
    sources = [incoming[t, width] for t in range(tops)]
    for d, path in enumerate(paths):
        for i, t in enumerate(path):
            sources[t] = sources[t] - incoming[d, i]
    scaled = []
    for j in range(tops):
        source = split(sources[j])
        count = len(above[j])
        if count:
            rows = slice(0, count * wide)
            updates = product(source, (high[j, rows], low[j, rows]), True)
            for i, t in enumerate(above[j]):
                sources[t] = sources[t] - updates[:, i * wide : (i + 1) * wide]
        inverse = (inverse_high[j], inverse_low[j])
        scaled.append(product(split(product(source, inverse, True)), inverse, False))
    solved = [None] * tops
    parts = [None] * tops
    for j in range(tops - 1, -1, -1):
        total = scaled[j]
        for i, t in enumerate(above[j]):
            rows = slice(i * wide, (i + 1) * wide)
            total = total - product(parts[t], (high[j, rows], low[j, rows]), False)
        solved[j] = total
        parts[j] = split(total)
    for p in range(outgoing.shape[0]):
        path = paths[p]
        for i in range(width):
            outgoing[p, i] = solved[path[i] if i < len(path) else path[0]]
        outgoing[p, width] = solved[p]


def local(rhs_leaf, rhs_top, leaf_blocks, leaf_dinv, leaf_struct, top_blocks, top_dinv):
    leafs, columns, wide = rhs_leaf.shape
    tops = top_blocks.shape[0]
    turn = leafs // TURNS
    starts = [turn * sum(CHUNKS[:k]) for k in range(len(CHUNKS) + 1)]
    above = ancestors_of(tops)
    most = max(len(row) for row in above)
    width = most + 1
    paths = paths_of(tops, above)
    groups = min(tops, columns // 8)
    part = columns // groups

    core, zh, zl = lax.axis_index("core"), lax.axis_index("zh"), lax.axis_index("zl")
    xy = lax.axis_index("xy")

    def swap(value):
        return lax.ppermute(value, ("core", "zh"), [(0, 0), (1, 2), (2, 1), (3, 3)])

    def to_keeper(value):
        return lax.ppermute(value, ("core", "zh"), [(1, 0), (2, 3)])

    def to_trader(value):
        return lax.ppermute(value, ("core", "zh"), [(0, 2), (3, 1)])

    def keepers(value):
        return lax.ppermute(value, ("core", "zh", "zl"), [(0, 1), (1, 0), (6, 7), (7, 6)])

    def other(value, *axes):
        last = 2 ** len(axes) - 1
        return lax.ppermute(value, axes, [(i, last - i) for i in range(last + 1)])

    def after(first, value):
        return lax.optimization_barrier((first, value))[1]

    chosen = jnp.take(top_blocks[:, 0], jnp.asarray(padded(above, most))[2 * xy + core], axis=0)
    top = jnp.concatenate([chosen, top_dinv], axis=0)
    top = jnp.stack([top, other(top, "zh")])
    top = jnp.concatenate([top, other(top, "zl")])

    names = jnp.zeros((8, wide), f32).at[:3, :leafs].set(leaf_struct.T.astype(f32))
    sides = jnp.concatenate([rhs_leaf.reshape(-1, wide), rhs_top.reshape(-1, wide), names], axis=0)
    def joined(at):
        return jnp.concatenate([leaf_blocks[at], leaf_dinv[at][:, None]], axis=1)

    own = joined(slice(None))
    parts = [joined(slice(at, end)) for at, end in zip(starts, starts[1:])]
    own, parts, sides = after(top, (own, parts, sides))

    near = keepers(own)
    sides = swap(sides)
    far = [to_keeper(part) for part in parts]
    across = [keepers(far[0])]
    early = [to_trader(value) for value in (own, near, far[0])]
    across += [keepers(after(early, value)) for value in far[1:]]
    top = lax.all_gather(after((far[-1], sides), top), ("xy", "core"), axis=0, tiled=False)

    names = sides[(leafs + 1) * columns :][:3, :leafs].T.astype(jnp.int32).reshape(-1)
    path = jnp.asarray(padded(paths, width))[2 * xy + zh]
    places = jnp.stack([2 * zh + zl, 2 * zh + 1 - zl, 2 - 2 * zh + zl, 3 - 2 * zh - zl])
    keeps = (core == zh).astype(jnp.int32)
    meta = jnp.concatenate([names, places.astype(jnp.int32), path, keeps[None]])

    vectors = jax.ShapeDtypeStruct((leafs + tops, columns, wide), f32)
    cost = pl.CostEstimate(flops=4 * 10**9, bytes_accessed=8 * 2**20, transcendentals=0)
    factors, state = [], None
    for k, base in enumerate(starts[:-1]):
        last = k == len(CHUNKS) - 1
        steps = starts[k + 1] - base
        merged = jax.ShapeDtypeStruct((steps, 3 * wide, wide), bf16)
        chunk = jax.ShapeDtypeStruct((steps, columns, wide), f32)
        shapes = [vectors, merged, merged, chunk]
        if k == 0:
            passed = (early[2], to_trader(after(far[-1], across[k])))
        else:
            passed = (to_trader(far[k]), to_trader(after(state, across[k])))
        specs = [SMEM] + [pl.BlockSpec(memory_space=pl.ANY)] * 8 + [
            pl.BlockSpec((steps * columns, wide), functools.partial(lambda k, i: (k, 0), base // steps)),
            pl.BlockSpec((columns, wide), lambda i: (leafs, 0)),
        ]
        if last:
            shapes.append(jax.ShapeDtypeStruct((tops, width + 1, part, wide), f32))
        before = () if k == 0 else (state,)
        results = pl.pallas_call(
            functools.partial(forward_kernel, base, leafs, k == 0, last, width),
            grid=(1,),
            in_specs=specs + [VMEM] * (k > 0),
            out_specs=[VMEM] * len(shapes),
            out_shape=shapes,
            scratch_shapes=[
                pltpu.VMEM((steps, 4, wide, wide), f32),
                pltpu.SemaphoreType.DMA((steps // GROUP, 4)),
            ],
            compiler_params=params(),
            cost_estimate=cost,
            name="leaf_forward",
        )(meta, own, near, far[k], across[k], *early[:2], *passed, sides, sides, *before)
        state = results[0]
        factors.append(results[1:4])

    def whole(*shape):
        return pl.BlockSpec((1,) + shape, lambda t: (t,) + (0,) * len(shape))

    top_places = jnp.stack([2 * zh + zl, 2 - 2 * zh + zl, 2 * zh + 1 - zl, 3 - 2 * zh - zl])
    top_factor = pl.pallas_call(
        top_prepare_kernel,
        grid=(tops,),
        in_specs=[SMEM, whole(*top.shape[1:])],
        out_specs=[whole(most * wide, wide)] * 2 + [whole(wide, wide)] * 2,
        out_shape=[jax.ShapeDtypeStruct((tops, most * wide, wide), bf16)] * 2
        + [jax.ShapeDtypeStruct((tops, wide, wide), bf16)] * 2,
        scratch_shapes=[pltpu.VMEM((width, wide, wide), f32)],
        compiler_params=params(),
        name="top_prepare",
    )(top_places.astype(jnp.int32), after(results[4], top))

    incoming = lax.all_to_all(results[4], ("xy", "zh"), split_axis=0, concat_axis=0, tiled=True)
    outgoing = pl.pallas_call(
        functools.partial(top_kernel, above, paths),
        in_specs=[VMEM] * 5,
        out_specs=VMEM,
        out_shape=jax.ShapeDtypeStruct((tops, width + 1, part, wide), f32),
        compiler_params=params(),
        name="top_solve",
    )(incoming, *top_factor)
    state = lax.all_to_all(outgoing, ("xy", "zh"), split_axis=0, concat_axis=0, tiled=True)
    own_top = state[:groups, width].reshape(1, columns, wide)

    found = [None] * TURNS
    chunk = jax.ShapeDtypeStruct((turn, columns, wide), f32)
    for k in range(TURNS - 1, -1, -1):
        held = max(i for i, at in enumerate(starts[:-1]) if at <= k * turn)
        part_of = [
            pl.BlockSpec(
                (turn,) + shape, functools.partial(lambda at, i: (at, 0, 0), k - starts[held] // turn)
            )
            for shape in ((3 * wide, wide), (3 * wide, wide), (columns, wide))
        ]
        found[k], state = pl.pallas_call(
            functools.partial(backward_kernel, k * turn, k == TURNS - 1, width),
            grid=(1,),
            in_specs=[SMEM] + part_of + [VMEM],
            out_specs=[VMEM] * 2,
            out_shape=[chunk, vectors],
            compiler_params=params(),
            cost_estimate=cost,
            name="leaf_backward",
        )(meta, *factors[held], state)
    late = swap(found[-1])
    middle = swap(jnp.concatenate(found[1:-1] + [own_top], axis=0))
    first = swap(after(late, found[0]))
    leaf_solution = jnp.concatenate([first, middle[:-1], late], axis=0)
    return (leaf_solution, middle[-1:])


def solution(mesh):
    subtrees, quarters = mesh.devices.shape
    fine = Mesh(
        mesh.devices.reshape(subtrees // 2, 2, 2, quarters // 2), ("xy", "core", "zh", "zl")
    )
    sn, rhs = ("xy", "core"), ("zh", "zl")
    return jax.shard_map(
        local,
        mesh=fine,
        in_specs=(
            P(sn, rhs, None),
            P(sn, rhs, None),
            P(sn, None, rhs, None),
            P(sn, rhs, None),
            P(sn, None),
            P(None, sn, rhs, None),
            P(sn, rhs, None),
        ),
        out_specs=(P(sn, rhs, None), P(sn, rhs, None)),
        check_vma=False,
    )
```

```python
import functools

import jax
import jax.numpy as jnp
import numpy as np
from jax import lax
from jax.experimental import pallas as pl
from jax.experimental.pallas import tpu as pltpu
from jax.sharding import Mesh
from jax.sharding import PartitionSpec as P

CHUNKS = (3, 1)
TURNS = 4
GROUP = 4
f32 = jnp.float32
bf16 = jnp.bfloat16
SMEM = pl.BlockSpec(memory_space=pltpu.SMEM)
VMEM = pl.BlockSpec(memory_space=pltpu.VMEM)


def params():
    return pltpu.CompilerParams(vmem_limit_bytes=28 * 2**20)


def split(value):
    high = value.astype(bf16)
    return high, (value - high.astype(f32)).astype(bf16)


def product(left, right, transposed):
    dims = (((1,), (1 if transposed else 0,)), ((), ()))

    def dot(a, b):
        return lax.dot_general(a, b, dims, preferred_element_type=f32)

    rows = left[0].shape[0]
    if rows % 16:
        return dot(left[0], right[0]) + (dot(left[1], right[0]) + dot(left[0], right[1]))
    both = dot(jnp.concatenate(left, axis=0), right[0])
    return both[:rows] + (both[rows:] + dot(left[0], right[1]))


def ancestors_of(tops):
    def level(t):
        return ((t + 1) & -(t + 1)).bit_length() - 1

    return [[t for t in range(j + 1, tops) if t + 1 - 2 ** level(t) <= j] for j in range(tops)]


def paths_of(subtrees, above):
    return [[4 * (d // 4)] + above[4 * (d // 4)] for d in range(subtrees)]


def padded(rows, width):
    return np.array([row + [row[0] if row else 0] * (width - len(row)) for row in rows], np.int32)


def forward_kernel(base, leafs, first, last, width, *refs):
    meta, kept, passed, rhs, rhs_top = refs[0], refs[1:5], refs[5:9], refs[9], refs[10]
    refs = refs[11:]
    if not first:
        acc_in, refs = refs[0], refs[1:]
    acc, high, low, scaled, refs = refs[0], refs[1], refs[2], refs[3], refs[4:]
    if last:
        payload, refs = refs[0], refs[1:]
    full, arrived = refs
    steps, columns, rows = scaled.shape[0], scaled.shape[1], kept[0].shape[2]
    wide = full.shape[2]

    def copies(pieces, group):
        made = []
        for place, piece in enumerate(pieces):
            offset = pl.multiple_of(meta[3 * leafs + place] * rows, rows)
            start = group * GROUP + (base if piece.shape[0] > steps else 0)
            made.append(
                pltpu.make_async_copy(
                    piece.at[pl.ds(start, GROUP)],
                    full.at[pl.ds(group * GROUP, GROUP), :, pl.ds(offset, rows), :],
                    arrived.at[group, place],
                )
            )
        return made

    def start(pieces):
        for group in range(steps // GROUP):
            for copy in copies(pieces, group):
                copy.start()

    keeps = meta[3 * leafs + 4 + width]
    pl.when(keeps == 1)(lambda: start(kept))
    pl.when(keeps == 0)(lambda: start(passed))
    if first:
        acc[...] = jnp.zeros_like(acc)
    else:
        acc[...] = acc_in[...]
    for group in range(steps // GROUP):
        for copy in copies(kept, group):
            copy.wait()
        members = range(group * GROUP, (group + 1) * GROUP)
        for s in members:
            blocks = split(full[s, 0:3].reshape(3 * wide, wide))
            merged = split(product(blocks, split(full[s, 3]), False))
            high[s] = merged[0]
            low[s] = merged[1]
        for s in members:
            at = s * columns
            source = split(rhs[at : at + columns] - acc[base + s])
            outgoing = product(source, (high[s], low[s]), True)
            for r in range(3):
                target = meta[3 * (base + s) + r]
                acc[target] = acc[target] + outgoing[:, r * wide : (r + 1) * wide]
            inverse = split(full[s, 3])
            solved = split(product(source, inverse, True))
            scaled[s] = product(solved, inverse, False)
    if last:
        peers, part = payload.shape[0], payload.shape[2]
        groups = columns // part
        for i in range(width + 1):
            node = acc[leafs + meta[3 * leafs + 4 + i]] if i < width else rhs_top[...]
            for p in range(peers):
                at = (p % groups) * part
                payload[p, i] = node[at : at + part]


def backward_kernel(base, first, width, meta, high, low, scaled, state, out, z):
    steps, wide = scaled.shape[0], scaled.shape[2]
    leafs = steps * TURNS
    if first:
        part = state.shape[2]
        groups = scaled.shape[1] // part
        z[...] = jnp.zeros_like(z)
        for i in range(width):
            node = leafs + meta[3 * leafs + 4 + i]
            for p in range(groups):
                z[node, p * part : (p + 1) * part, :] = state[p, i]
    else:
        z[...] = state[...]
    for s in range(steps - 1, -1, -1):
        total = scaled[s]
        for r in (2, 1, 0):
            source = split(z[meta[3 * (base + s) + r]])
            at = slice(r * wide, (r + 1) * wide)
            total = total - product(source, (high[s, at], low[s, at]), False)
        z[base + s] = total
        out[s] = total


def top_prepare_kernel(places, top, high, low, inverse_high, inverse_low, full):
    blocks, rows, wide = top.shape[2], top.shape[3], top.shape[4]
    for place in range(top.shape[1]):
        offset = pl.multiple_of(places[place] * rows, rows)
        full[:, pl.ds(offset, rows), :] = top[0, place]
    inverse = split(full[blocks - 1])
    merged = product(split(full[: blocks - 1].reshape((blocks - 1) * wide, wide)), inverse, False)
    high[0], low[0] = split(merged)
    inverse_high[0], inverse_low[0] = inverse


def top_kernel(above, paths, incoming, high, low, inverse_high, inverse_low, outgoing):
    tops, wide = len(above), high.shape[2]
    width = outgoing.shape[1] - 1
    sources = [incoming[t, width] for t in range(tops)]
    for d, path in enumerate(paths):
        for i, t in enumerate(path):
            sources[t] = sources[t] - incoming[d, i]
    scaled = []
    for j in range(tops):
        source = split(sources[j])
        count = len(above[j])
        if count:
            rows = slice(0, count * wide)
            updates = product(source, (high[j, rows], low[j, rows]), True)
            for i, t in enumerate(above[j]):
                sources[t] = sources[t] - updates[:, i * wide : (i + 1) * wide]
        inverse = (inverse_high[j], inverse_low[j])
        scaled.append(product(split(product(source, inverse, True)), inverse, False))
    solved = [None] * tops
    parts = [None] * tops
    for j in range(tops - 1, -1, -1):
        total = scaled[j]
        for i, t in enumerate(above[j]):
            rows = slice(i * wide, (i + 1) * wide)
            total = total - product(parts[t], (high[j, rows], low[j, rows]), False)
        solved[j] = total
        parts[j] = split(total)
    for p in range(outgoing.shape[0]):
        path = paths[p]
        for i in range(width):
            outgoing[p, i] = solved[path[i] if i < len(path) else path[0]]
        outgoing[p, width] = solved[p]


def local(rhs_leaf, rhs_top, leaf_blocks, leaf_dinv, leaf_struct, top_blocks, top_dinv):
    leafs, columns, wide = rhs_leaf.shape
    tops = top_blocks.shape[0]
    turn = leafs // TURNS
    starts = [turn * sum(CHUNKS[:k]) for k in range(len(CHUNKS) + 1)]
    above = ancestors_of(tops)
    most = max(len(row) for row in above)
    width = most + 1
    paths = paths_of(tops, above)
    groups = min(tops, columns // 8)
    part = columns // groups

    core, zh, zl = lax.axis_index("core"), lax.axis_index("zh"), lax.axis_index("zl")
    xy = lax.axis_index("xy")

    def swap(value):
        return lax.ppermute(value, ("core", "zh"), [(0, 0), (1, 2), (2, 1), (3, 3)])

    def to_keeper(value):
        return lax.ppermute(value, ("core", "zh"), [(1, 0), (2, 3)])

    def to_trader(value):
        return lax.ppermute(value, ("core", "zh"), [(0, 2), (3, 1)])

    def keepers(value):
        return lax.ppermute(value, ("core", "zh", "zl"), [(0, 1), (1, 0), (6, 7), (7, 6)])

    def other(value, *axes):
        last = 2 ** len(axes) - 1
        return lax.ppermute(value, axes, [(i, last - i) for i in range(last + 1)])

    def after(first, value):
        return lax.optimization_barrier((first, value))[1]

    chosen = jnp.take(top_blocks[:, 0], jnp.asarray(padded(above, most))[2 * xy + core], axis=0)
    top = jnp.concatenate([chosen, top_dinv], axis=0)
    names = jnp.zeros((8, wide), f32).at[:3, :leafs].set(leaf_struct.T.astype(f32))
    sides = jnp.concatenate([rhs_leaf.reshape(-1, wide), rhs_top.reshape(-1, wide), names], axis=0)
    def joined(at):
        return jnp.concatenate([leaf_blocks[at], leaf_dinv[at][:, None]], axis=1)

    own = joined(slice(None))
    parts = [joined(slice(at, end)) for at, end in zip(starts, starts[1:])]

    near = keepers(own)
    sides = swap(sides)
    far = [to_keeper(part) for part in parts]
    across = [keepers(far[0])]
    early = [to_trader(value) for value in (own, near, far[0])]
    across += [keepers(after(early, value)) for value in far[1:]]
    top = after(early[:2], top)
    top = jnp.stack([top, other(top, "zh")])
    top = jnp.concatenate([top, other(top, "zl")])
    top = lax.all_gather(after((far[-1], sides), top), ("xy", "core"), axis=0, tiled=False)

    names = sides[(leafs + 1) * columns :][:3, :leafs].T.astype(jnp.int32).reshape(-1)
    path = jnp.asarray(padded(paths, width))[2 * xy + zh]
    places = jnp.stack([2 * zh + zl, 2 * zh + 1 - zl, 2 - 2 * zh + zl, 3 - 2 * zh - zl])
    keeps = (core == zh).astype(jnp.int32)
    meta = jnp.concatenate([names, places.astype(jnp.int32), path, keeps[None]])

    vectors = jax.ShapeDtypeStruct((leafs + tops, columns, wide), f32)
    cost = pl.CostEstimate(flops=4 * 10**9, bytes_accessed=8 * 2**20, transcendentals=0)
    factors, state = [], None
    for k, base in enumerate(starts[:-1]):
        last = k == len(CHUNKS) - 1
        steps = starts[k + 1] - base
        merged = jax.ShapeDtypeStruct((steps, 3 * wide, wide), bf16)
        chunk = jax.ShapeDtypeStruct((steps, columns, wide), f32)
        shapes = [vectors, merged, merged, chunk]
        if k == 0:
            passed = (early[2], to_trader(after(far[-1], across[k])))
        else:
            passed = (to_trader(far[k]), to_trader(after(state, across[k])))
        specs = [SMEM] + [pl.BlockSpec(memory_space=pl.ANY)] * 8 + [
            pl.BlockSpec((steps * columns, wide), functools.partial(lambda k, i: (k, 0), base // steps)),
            pl.BlockSpec((columns, wide), lambda i: (leafs, 0)),
        ]
        if last:
            shapes.append(jax.ShapeDtypeStruct((tops, width + 1, part, wide), f32))
        before = () if k == 0 else (state,)
        results = pl.pallas_call(
            functools.partial(forward_kernel, base, leafs, k == 0, last, width),
            grid=(1,),
            in_specs=specs + [VMEM] * (k > 0),
            out_specs=[VMEM] * len(shapes),
            out_shape=shapes,
            scratch_shapes=[
                pltpu.VMEM((steps, 4, wide, wide), f32),
                pltpu.SemaphoreType.DMA((steps // GROUP, 4)),
            ],
            compiler_params=params(),
            cost_estimate=cost,
            name="leaf_forward",
        )(meta, own, near, far[k], across[k], *early[:2], *passed, sides, sides, *before)
        state = results[0]
        factors.append(results[1:4])

    def whole(*shape):
        return pl.BlockSpec((1,) + shape, lambda t: (t,) + (0,) * len(shape))

    top_places = jnp.stack([2 * zh + zl, 2 - 2 * zh + zl, 2 * zh + 1 - zl, 3 - 2 * zh - zl])
    top_factor = pl.pallas_call(
        top_prepare_kernel,
        grid=(tops,),
        in_specs=[SMEM, whole(*top.shape[1:])],
        out_specs=[whole(most * wide, wide)] * 2 + [whole(wide, wide)] * 2,
        out_shape=[jax.ShapeDtypeStruct((tops, most * wide, wide), bf16)] * 2
        + [jax.ShapeDtypeStruct((tops, wide, wide), bf16)] * 2,
        scratch_shapes=[pltpu.VMEM((width, wide, wide), f32)],
        compiler_params=params(),
        name="top_prepare",
    )(top_places.astype(jnp.int32), after(results[4], top))

    incoming = lax.all_to_all(results[4], ("xy", "zh"), split_axis=0, concat_axis=0, tiled=True)
    outgoing = pl.pallas_call(
        functools.partial(top_kernel, above, paths),
        in_specs=[VMEM] * 5,
        out_specs=VMEM,
        out_shape=jax.ShapeDtypeStruct((tops, width + 1, part, wide), f32),
        compiler_params=params(),
        name="top_solve",
    )(incoming, *top_factor)
    state = lax.all_to_all(outgoing, ("xy", "zh"), split_axis=0, concat_axis=0, tiled=True)
    own_top = state[:groups, width].reshape(1, columns, wide)

    found = [None] * TURNS
    chunk = jax.ShapeDtypeStruct((turn, columns, wide), f32)
    for k in range(TURNS - 1, -1, -1):
        held = max(i for i, at in enumerate(starts[:-1]) if at <= k * turn)
        part_of = [
            pl.BlockSpec(
                (turn,) + shape, functools.partial(lambda at, i: (at, 0, 0), k - starts[held] // turn)
            )
            for shape in ((3 * wide, wide), (3 * wide, wide), (columns, wide))
        ]
        found[k], state = pl.pallas_call(
            functools.partial(backward_kernel, k * turn, k == TURNS - 1, width),
            grid=(1,),
            in_specs=[SMEM] + part_of + [VMEM],
            out_specs=[VMEM] * 2,
            out_shape=[chunk, vectors],
            compiler_params=params(),
            cost_estimate=cost,
            name="leaf_backward",
        )(meta, *factors[held], state)
    late = swap(found[-1])
    middle = swap(jnp.concatenate(found[1:-1] + [own_top], axis=0))
    first = swap(found[0])
    leaf_solution = jnp.concatenate([first, middle[:-1], late], axis=0)
    return (leaf_solution, middle[-1:])


def solution(mesh):
    subtrees, quarters = mesh.devices.shape
    fine = Mesh(
        mesh.devices.reshape(subtrees // 2, 2, 2, quarters // 2), ("xy", "core", "zh", "zl")
    )
    sn, rhs = ("xy", "core"), ("zh", "zl")
    return jax.shard_map(
        local,
        mesh=fine,
        in_specs=(
            P(sn, rhs, None),
            P(sn, rhs, None),
            P(sn, None, rhs, None),
            P(sn, rhs, None),
            P(sn, None),
            P(None, sn, rhs, None),
            P(sn, rhs, None),
        ),
        out_specs=(P(sn, rhs, None), P(sn, rhs, None)),
        check_vma=False,
    )
```

```python
import functools

import jax
import jax.numpy as jnp
import numpy as np
from jax import lax
from jax.experimental import pallas as pl
from jax.experimental.pallas import tpu as pltpu
from jax.sharding import Mesh
from jax.sharding import PartitionSpec as P

CHUNKS = (3, 1)
TURNS = 4
GROUP = 4
f32 = jnp.float32
bf16 = jnp.bfloat16
SMEM = pl.BlockSpec(memory_space=pltpu.SMEM)
VMEM = pl.BlockSpec(memory_space=pltpu.VMEM)


def params():
    return pltpu.CompilerParams(vmem_limit_bytes=28 * 2**20)


def split(value):
    high = value.astype(bf16)
    return high, (value - high.astype(f32)).astype(bf16)


def product(left, right, transposed):
    dims = (((1,), (1 if transposed else 0,)), ((), ()))

    def dot(a, b):
        return lax.dot_general(a, b, dims, preferred_element_type=f32)

    rows = left[0].shape[0]
    if rows % 16:
        return dot(left[0], right[0]) + (dot(left[1], right[0]) + dot(left[0], right[1]))
    both = dot(jnp.concatenate(left, axis=0), right[0])
    return both[:rows] + (both[rows:] + dot(left[0], right[1]))


def ancestors_of(tops):
    def level(t):
        return ((t + 1) & -(t + 1)).bit_length() - 1

    return [[t for t in range(j + 1, tops) if t + 1 - 2 ** level(t) <= j] for j in range(tops)]


def paths_of(subtrees, above):
    return [[4 * (d // 4)] + above[4 * (d // 4)] for d in range(subtrees)]


def padded(rows, width):
    return np.array([row + [row[0] if row else 0] * (width - len(row)) for row in rows], np.int32)


def forward_kernel(base, leafs, first, last, width, *refs):
    meta, kept, passed, rhs, rhs_top = refs[0], refs[1:5], refs[5:9], refs[9], refs[10]
    refs = refs[11:]
    if not first:
        acc_in, refs = refs[0], refs[1:]
    acc, high, low, scaled, refs = refs[0], refs[1], refs[2], refs[3], refs[4:]
    if last:
        payload, refs = refs[0], refs[1:]
    full, arrived = refs
    steps, columns, rows = scaled.shape[0], scaled.shape[1], kept[0].shape[2]
    wide = full.shape[2]

    def copies(pieces, group):
        made = []
        for place, piece in enumerate(pieces):
            offset = pl.multiple_of(meta[3 * leafs + place] * rows, rows)
            start = group * GROUP + (base if piece.shape[0] > steps else 0)
            made.append(
                pltpu.make_async_copy(
                    piece.at[pl.ds(start, GROUP)],
                    full.at[pl.ds(group * GROUP, GROUP), :, pl.ds(offset, rows), :],
                    arrived.at[group, place],
                )
            )
        return made

    def start(pieces):
        for group in range(steps // GROUP):
            for copy in copies(pieces, group):
                copy.start()

    keeps = meta[3 * leafs + 4 + width]
    pl.when(keeps == 1)(lambda: start(kept))
    pl.when(keeps == 0)(lambda: start(passed))
    if first:
        acc[...] = jnp.zeros_like(acc)
    else:
        acc[...] = acc_in[...]
    for group in range(steps // GROUP):
        for copy in copies(kept, group):
            copy.wait()
        members = range(group * GROUP, (group + 1) * GROUP)
        for s in members:
            blocks = split(full[s, 0:3].reshape(3 * wide, wide))
            merged = split(product(blocks, split(full[s, 3]), False))
            high[s] = merged[0]
            low[s] = merged[1]
        for s in members:
            at = s * columns
            source = split(rhs[at : at + columns] - acc[base + s])
            outgoing = product(source, (high[s], low[s]), True)
            for r in range(3):
                target = meta[3 * (base + s) + r]
                acc[target] = acc[target] + outgoing[:, r * wide : (r + 1) * wide]
            inverse = split(full[s, 3])
            solved = split(product(source, inverse, True))
            scaled[s] = product(solved, inverse, False)
    if last:
        peers, part = payload.shape[0], payload.shape[2]
        groups = columns // part
        for i in range(width + 1):
            node = acc[leafs + meta[3 * leafs + 4 + i]] if i < width else rhs_top[...]
            for p in range(peers):
                at = (p % groups) * part
                payload[p, i] = node[at : at + part]


def backward_kernel(base, first, width, meta, high, low, scaled, state, out, z):
    steps, wide = scaled.shape[0], scaled.shape[2]
    leafs = steps * TURNS
    if first:
        part = state.shape[2]
        groups = scaled.shape[1] // part
        z[...] = jnp.zeros_like(z)
        for i in range(width):
            node = leafs + meta[3 * leafs + 4 + i]
            for p in range(groups):
                z[node, p * part : (p + 1) * part, :] = state[p, i]
    else:
        z[...] = state[...]
    for s in range(steps - 1, -1, -1):
        total = scaled[s]
        for r in (2, 1, 0):
            source = split(z[meta[3 * (base + s) + r]])
            at = slice(r * wide, (r + 1) * wide)
            total = total - product(source, (high[s, at], low[s, at]), False)
        z[base + s] = total
        out[s] = total


def top_prepare_kernel(places, top, high, low, inverse_high, inverse_low, full):
    blocks, rows, wide = top.shape[2], top.shape[3], top.shape[4]
    for place in range(top.shape[1]):
        offset = pl.multiple_of(places[place] * rows, rows)
        full[:, pl.ds(offset, rows), :] = top[0, place]
    inverse = split(full[blocks - 1])
    merged = product(split(full[: blocks - 1].reshape((blocks - 1) * wide, wide)), inverse, False)
    high[0], low[0] = split(merged)
    inverse_high[0], inverse_low[0] = inverse


def top_kernel(above, paths, incoming, high, low, inverse_high, inverse_low, outgoing):
    tops, wide = len(above), high.shape[2]
    width = outgoing.shape[1] - 1
    sources = [incoming[t, width] for t in range(tops)]
    for d, path in enumerate(paths):
        for i, t in enumerate(path):
            sources[t] = sources[t] - incoming[d, i]
    scaled = []
    for j in range(tops):
        source = split(sources[j])
        count = len(above[j])
        if count:
            rows = slice(0, count * wide)
            updates = product(source, (high[j, rows], low[j, rows]), True)
            for i, t in enumerate(above[j]):
                sources[t] = sources[t] - updates[:, i * wide : (i + 1) * wide]
        inverse = (inverse_high[j], inverse_low[j])
        scaled.append(product(split(product(source, inverse, True)), inverse, False))
    solved = [None] * tops
    parts = [None] * tops
    for j in range(tops - 1, -1, -1):
        total = scaled[j]
        for i, t in enumerate(above[j]):
            rows = slice(i * wide, (i + 1) * wide)
            total = total - product(parts[t], (high[j, rows], low[j, rows]), False)
        solved[j] = total
        parts[j] = split(total)
    for p in range(outgoing.shape[0]):
        path = paths[p]
        for i in range(width):
            outgoing[p, i] = solved[path[i] if i < len(path) else path[0]]
        outgoing[p, width] = solved[p]


def local(rhs_leaf, rhs_top, leaf_blocks, leaf_dinv, leaf_struct, top_blocks, top_dinv):
    leafs, columns, wide = rhs_leaf.shape
    tops = top_blocks.shape[0]
    turn = leafs // TURNS
    starts = [turn * sum(CHUNKS[:k]) for k in range(len(CHUNKS) + 1)]
    above = ancestors_of(tops)
    most = max(len(row) for row in above)
    width = most + 1
    paths = paths_of(tops, above)
    groups = min(tops, columns // 8)
    part = columns // groups

    core, zh, zl = lax.axis_index("core"), lax.axis_index("zh"), lax.axis_index("zl")
    xy = lax.axis_index("xy")

    def swap(value):
        return lax.ppermute(value, ("core", "zh"), [(0, 0), (1, 2), (2, 1), (3, 3)])

    def to_keeper(value):
        return lax.ppermute(value, ("core", "zh"), [(1, 0), (2, 3)])

    def to_trader(value):
        return lax.ppermute(value, ("core", "zh"), [(0, 2), (3, 1)])

    def keepers(value):
        return lax.ppermute(value, ("core", "zh", "zl"), [(0, 1), (1, 0), (6, 7), (7, 6)])

    def other(value, *axes):
        last = 2 ** len(axes) - 1
        return lax.ppermute(value, axes, [(i, last - i) for i in range(last + 1)])

    def after(first, value):
        return lax.optimization_barrier((first, value))[1]

    chosen = jnp.take(top_blocks[:, 0], jnp.asarray(padded(above, most))[2 * xy + core], axis=0)
    top = jnp.concatenate([chosen, top_dinv], axis=0)
    top = jnp.stack([top, other(top, "zh")])
    top = jnp.concatenate([top, other(top, "zl")])

    names = jnp.zeros((8, wide), f32).at[:3, :leafs].set(leaf_struct.T.astype(f32))
    sides = jnp.concatenate([rhs_leaf.reshape(-1, wide), rhs_top.reshape(-1, wide), names], axis=0)
    def joined(at):
        return jnp.concatenate([leaf_blocks[at], leaf_dinv[at][:, None]], axis=1)

    own = joined(slice(None))
    parts = [joined(slice(at, end)) for at, end in zip(starts, starts[1:])]
    own, parts, sides = after(top, (own, parts, sides))

    near = keepers(own)
    sides = swap(sides)
    far = [to_keeper(part) for part in parts]
    across = [keepers(far[0])]
    early = [to_trader(value) for value in (own, near, far[0])]
    across += [keepers(after(early, value)) for value in far[1:]]
    top = lax.all_gather(after((far[-1], sides), top), ("xy", "core"), axis=0, tiled=False)

    names = sides[(leafs + 1) * columns :][:3, :leafs].T.astype(jnp.int32).reshape(-1)
    path = jnp.asarray(padded(paths, width))[2 * xy + zh]
    places = jnp.stack([2 * zh + zl, 2 * zh + 1 - zl, 2 - 2 * zh + zl, 3 - 2 * zh - zl])
    keeps = (core == zh).astype(jnp.int32)
    meta = jnp.concatenate([names, places.astype(jnp.int32), path, keeps[None]])

    vectors = jax.ShapeDtypeStruct((leafs + tops, columns, wide), f32)
    cost = pl.CostEstimate(flops=4 * 10**9, bytes_accessed=8 * 2**20, transcendentals=0)
    factors, state = [], None
    for k, base in enumerate(starts[:-1]):
        last = k == len(CHUNKS) - 1
        steps = starts[k + 1] - base
        merged = jax.ShapeDtypeStruct((steps, 3 * wide, wide), bf16)
        chunk = jax.ShapeDtypeStruct((steps, columns, wide), f32)
        shapes = [vectors, merged, merged, chunk]
        if k == 0:
            last_far = to_trader(far[-1])
            passed = (early[2], to_trader(after(last_far, across[k])))
        else:
            passed = (last_far, to_trader(after(state, across[k])))
        specs = [SMEM] + [pl.BlockSpec(memory_space=pl.ANY)] * 8 + [
            pl.BlockSpec((steps * columns, wide), functools.partial(lambda k, i: (k, 0), base // steps)),
            pl.BlockSpec((columns, wide), lambda i: (leafs, 0)),
        ]
        if last:
            shapes.append(jax.ShapeDtypeStruct((tops, width + 1, part, wide), f32))
        before = () if k == 0 else (state,)
        results = pl.pallas_call(
            functools.partial(forward_kernel, base, leafs, k == 0, last, width),
            grid=(1,),
            in_specs=specs + [VMEM] * (k > 0),
            out_specs=[VMEM] * len(shapes),
            out_shape=shapes,
            scratch_shapes=[
                pltpu.VMEM((steps, 4, wide, wide), f32),
                pltpu.SemaphoreType.DMA((steps // GROUP, 4)),
            ],
            compiler_params=params(),
            cost_estimate=cost,
            name="leaf_forward",
        )(meta, own, near, far[k], across[k], *early[:2], *passed, sides, sides, *before)
        state = results[0]
        factors.append(results[1:4])

    def whole(*shape):
        return pl.BlockSpec((1,) + shape, lambda t: (t,) + (0,) * len(shape))

    top_places = jnp.stack([2 * zh + zl, 2 - 2 * zh + zl, 2 * zh + 1 - zl, 3 - 2 * zh - zl])
    top_factor = pl.pallas_call(
        top_prepare_kernel,
        grid=(tops,),
        in_specs=[SMEM, whole(*top.shape[1:])],
        out_specs=[whole(most * wide, wide)] * 2 + [whole(wide, wide)] * 2,
        out_shape=[jax.ShapeDtypeStruct((tops, most * wide, wide), bf16)] * 2
        + [jax.ShapeDtypeStruct((tops, wide, wide), bf16)] * 2,
        scratch_shapes=[pltpu.VMEM((width, wide, wide), f32)],
        compiler_params=params(),
        name="top_prepare",
    )(top_places.astype(jnp.int32), after(results[4], top))

    incoming = lax.all_to_all(results[4], ("xy", "zh"), split_axis=0, concat_axis=0, tiled=True)
    outgoing = pl.pallas_call(
        functools.partial(top_kernel, above, paths),
        in_specs=[VMEM] * 5,
        out_specs=VMEM,
        out_shape=jax.ShapeDtypeStruct((tops, width + 1, part, wide), f32),
        compiler_params=params(),
        name="top_solve",
    )(incoming, *top_factor)
    state = lax.all_to_all(outgoing, ("xy", "zh"), split_axis=0, concat_axis=0, tiled=True)
    own_top = state[:groups, width].reshape(1, columns, wide)

    found = [None] * TURNS
    chunk = jax.ShapeDtypeStruct((turn, columns, wide), f32)
    for k in range(TURNS - 1, -1, -1):
        held = max(i for i, at in enumerate(starts[:-1]) if at <= k * turn)
        part_of = [
            pl.BlockSpec(
                (turn,) + shape, functools.partial(lambda at, i: (at, 0, 0), k - starts[held] // turn)
            )
            for shape in ((3 * wide, wide), (3 * wide, wide), (columns, wide))
        ]
        found[k], state = pl.pallas_call(
            functools.partial(backward_kernel, k * turn, k == TURNS - 1, width),
            grid=(1,),
            in_specs=[SMEM] + part_of + [VMEM],
            out_specs=[VMEM] * 2,
            out_shape=[chunk, vectors],
            compiler_params=params(),
            cost_estimate=cost,
            name="leaf_backward",
        )(meta, *factors[held], state)
    late = swap(found[-1])
    middle = swap(jnp.concatenate(found[1:-1] + [own_top], axis=0))
    first = swap(found[0])
    leaf_solution = jnp.concatenate([first, middle[:-1], late], axis=0)
    return (leaf_solution, middle[-1:])


def solution(mesh):
    subtrees, quarters = mesh.devices.shape
    fine = Mesh(
        mesh.devices.reshape(subtrees // 2, 2, 2, quarters // 2), ("xy", "core", "zh", "zl")
    )
    sn, rhs = ("xy", "core"), ("zh", "zl")
    return jax.shard_map(
        local,
        mesh=fine,
        in_specs=(
            P(sn, rhs, None),
            P(sn, rhs, None),
            P(sn, None, rhs, None),
            P(sn, rhs, None),
            P(sn, None),
            P(None, sn, rhs, None),
            P(sn, rhs, None),
        ),
        out_specs=(P(sn, rhs, None), P(sn, rhs, None)),
        check_vma=False,
    )
```

```python
import functools

import jax
import jax.numpy as jnp
import numpy as np
from jax import lax
from jax.experimental import pallas as pl
from jax.experimental.pallas import tpu as pltpu
from jax.sharding import Mesh
from jax.sharding import PartitionSpec as P

CHUNKS = (2, 2)
TURNS = 4
GROUP = 4
f32 = jnp.float32
bf16 = jnp.bfloat16
SMEM = pl.BlockSpec(memory_space=pltpu.SMEM)
VMEM = pl.BlockSpec(memory_space=pltpu.VMEM)


def params():
    return pltpu.CompilerParams(vmem_limit_bytes=28 * 2**20)


def split(value):
    high = value.astype(bf16)
    return high, (value - high.astype(f32)).astype(bf16)


def product(left, right, transposed):
    dims = (((1,), (1 if transposed else 0,)), ((), ()))

    def dot(a, b):
        return lax.dot_general(a, b, dims, preferred_element_type=f32)

    rows = left[0].shape[0]
    if rows % 16:
        return dot(left[0], right[0]) + (dot(left[1], right[0]) + dot(left[0], right[1]))
    both = dot(jnp.concatenate(left, axis=0), right[0])
    return both[:rows] + (both[rows:] + dot(left[0], right[1]))


def ancestors_of(tops):
    def level(t):
        return ((t + 1) & -(t + 1)).bit_length() - 1

    return [[t for t in range(j + 1, tops) if t + 1 - 2 ** level(t) <= j] for j in range(tops)]


def paths_of(subtrees, above):
    return [[4 * (d // 4)] + above[4 * (d // 4)] for d in range(subtrees)]


def padded(rows, width):
    return np.array([row + [row[0] if row else 0] * (width - len(row)) for row in rows], np.int32)


def forward_kernel(base, leafs, first, last, width, *refs):
    meta, kept, passed, rhs, rhs_top = refs[0], refs[1:5], refs[5:9], refs[9], refs[10]
    refs = refs[11:]
    if not first:
        acc_in, refs = refs[0], refs[1:]
    acc, high, low, scaled, refs = refs[0], refs[1], refs[2], refs[3], refs[4:]
    if last:
        payload, refs = refs[0], refs[1:]
    full, arrived = refs
    steps, columns, rows = scaled.shape[0], scaled.shape[1], kept[0].shape[2]
    wide = full.shape[2]

    def copies(pieces, group):
        made = []
        for place, piece in enumerate(pieces):
            offset = pl.multiple_of(meta[3 * leafs + place] * rows, rows)
            start = group * GROUP + (base if piece.shape[0] > steps else 0)
            made.append(
                pltpu.make_async_copy(
                    piece.at[pl.ds(start, GROUP)],
                    full.at[pl.ds(group * GROUP, GROUP), :, pl.ds(offset, rows), :],
                    arrived.at[group, place],
                )
            )
        return made

    def start(pieces):
        for group in range(steps // GROUP):
            for copy in copies(pieces, group):
                copy.start()

    keeps = meta[3 * leafs + 4 + width]
    pl.when(keeps == 1)(lambda: start(kept))
    pl.when(keeps == 0)(lambda: start(passed))
    if first:
        acc[...] = jnp.zeros_like(acc)
    else:
        acc[...] = acc_in[...]
    for group in range(steps // GROUP):
        for copy in copies(kept, group):
            copy.wait()
        members = range(group * GROUP, (group + 1) * GROUP)
        for s in members:
            blocks = split(full[s, 0:3].reshape(3 * wide, wide))
            merged = split(product(blocks, split(full[s, 3]), False))
            high[s] = merged[0]
            low[s] = merged[1]
        for s in members:
            at = s * columns
            source = split(rhs[at : at + columns] - acc[base + s])
            outgoing = product(source, (high[s], low[s]), True)
            for r in range(3):
                target = meta[3 * (base + s) + r]
                acc[target] = acc[target] + outgoing[:, r * wide : (r + 1) * wide]
            inverse = split(full[s, 3])
            solved = split(product(source, inverse, True))
            scaled[s] = product(solved, inverse, False)
    if last:
        peers, part = payload.shape[0], payload.shape[2]
        groups = columns // part
        for i in range(width + 1):
            node = acc[leafs + meta[3 * leafs + 4 + i]] if i < width else rhs_top[...]
            for p in range(peers):
                at = (p % groups) * part
                payload[p, i] = node[at : at + part]


def backward_kernel(base, first, width, meta, high, low, scaled, state, out, z):
    steps, wide = scaled.shape[0], scaled.shape[2]
    leafs = steps * TURNS
    if first:
        part = state.shape[2]
        groups = scaled.shape[1] // part
        z[...] = jnp.zeros_like(z)
        for i in range(width):
            node = leafs + meta[3 * leafs + 4 + i]
            for p in range(groups):
                z[node, p * part : (p + 1) * part, :] = state[p, i]
    else:
        z[...] = state[...]
    for s in range(steps - 1, -1, -1):
        total = scaled[s]
        for r in (2, 1, 0):
            source = split(z[meta[3 * (base + s) + r]])
            at = slice(r * wide, (r + 1) * wide)
            total = total - product(source, (high[s, at], low[s, at]), False)
        z[base + s] = total
        out[s] = total


def top_prepare_kernel(places, top, high, low, inverse_high, inverse_low, full):
    blocks, rows, wide = top.shape[2], top.shape[3], top.shape[4]
    for place in range(top.shape[1]):
        offset = pl.multiple_of(places[place] * rows, rows)
        full[:, pl.ds(offset, rows), :] = top[0, place]
    inverse = split(full[blocks - 1])
    merged = product(split(full[: blocks - 1].reshape((blocks - 1) * wide, wide)), inverse, False)
    high[0], low[0] = split(merged)
    inverse_high[0], inverse_low[0] = inverse


def top_kernel(above, paths, incoming, high, low, inverse_high, inverse_low, outgoing):
    tops, wide = len(above), high.shape[2]
    width = outgoing.shape[1] - 1
    sources = [incoming[t, width] for t in range(tops)]
    for d, path in enumerate(paths):
        for i, t in enumerate(path):
            sources[t] = sources[t] - incoming[d, i]
    scaled = []
    for j in range(tops):
        source = split(sources[j])
        count = len(above[j])
        if count:
            rows = slice(0, count * wide)
            updates = product(source, (high[j, rows], low[j, rows]), True)
            for i, t in enumerate(above[j]):
                sources[t] = sources[t] - updates[:, i * wide : (i + 1) * wide]
        inverse = (inverse_high[j], inverse_low[j])
        scaled.append(product(split(product(source, inverse, True)), inverse, False))
    solved = [None] * tops
    parts = [None] * tops
    for j in range(tops - 1, -1, -1):
        total = scaled[j]
        for i, t in enumerate(above[j]):
            rows = slice(i * wide, (i + 1) * wide)
            total = total - product(parts[t], (high[j, rows], low[j, rows]), False)
        solved[j] = total
        parts[j] = split(total)
    for p in range(outgoing.shape[0]):
        path = paths[p]
        for i in range(width):
            outgoing[p, i] = solved[path[i] if i < len(path) else path[0]]
        outgoing[p, width] = solved[p]


def local(rhs_leaf, rhs_top, leaf_blocks, leaf_dinv, leaf_struct, top_blocks, top_dinv):
    leafs, columns, wide = rhs_leaf.shape
    tops = top_blocks.shape[0]
    turn = leafs // TURNS
    starts = [turn * sum(CHUNKS[:k]) for k in range(len(CHUNKS) + 1)]
    above = ancestors_of(tops)
    most = max(len(row) for row in above)
    width = most + 1
    paths = paths_of(tops, above)
    groups = min(tops, columns // 8)
    part = columns // groups

    core, zh, zl = lax.axis_index("core"), lax.axis_index("zh"), lax.axis_index("zl")
    xy = lax.axis_index("xy")

    def swap(value):
        return lax.ppermute(value, ("core", "zh"), [(0, 0), (1, 2), (2, 1), (3, 3)])

    def to_keeper(value):
        return lax.ppermute(value, ("core", "zh"), [(1, 0), (2, 3)])

    def to_trader(value):
        return lax.ppermute(value, ("core", "zh"), [(0, 2), (3, 1)])

    def keepers(value):
        return lax.ppermute(value, ("core", "zh", "zl"), [(0, 1), (1, 0), (6, 7), (7, 6)])

    def other(value, *axes):
        last = 2 ** len(axes) - 1
        return lax.ppermute(value, axes, [(i, last - i) for i in range(last + 1)])

    def after(first, value):
        return lax.optimization_barrier((first, value))[1]

    chosen = jnp.take(top_blocks[:, 0], jnp.asarray(padded(above, most))[2 * xy + core], axis=0)
    top = jnp.concatenate([chosen, top_dinv], axis=0)
    top = jnp.stack([top, other(top, "zh")])
    top = jnp.concatenate([top, other(top, "zl")])

    names = jnp.zeros((8, wide), f32).at[:3, :leafs].set(leaf_struct.T.astype(f32))
    sides = jnp.concatenate([rhs_leaf.reshape(-1, wide), rhs_top.reshape(-1, wide), names], axis=0)
    def joined(at):
        return jnp.concatenate([leaf_blocks[at], leaf_dinv[at][:, None]], axis=1)

    own = joined(slice(None))
    parts = [joined(slice(at, end)) for at, end in zip(starts, starts[1:])]
    own, parts, sides = after(top, (own, parts, sides))

    near = keepers(own)
    sides = swap(sides)
    far = [to_keeper(part) for part in parts]
    across = [keepers(far[0])]
    early = [to_trader(value) for value in (own, near, far[0])]
    across += [keepers(after(early, value)) for value in far[1:]]
    top = lax.all_gather(after((far[-1], sides), top), ("xy", "core"), axis=0, tiled=False)

    names = sides[(leafs + 1) * columns :][:3, :leafs].T.astype(jnp.int32).reshape(-1)
    path = jnp.asarray(padded(paths, width))[2 * xy + zh]
    places = jnp.stack([2 * zh + zl, 2 * zh + 1 - zl, 2 - 2 * zh + zl, 3 - 2 * zh - zl])
    keeps = (core == zh).astype(jnp.int32)
    meta = jnp.concatenate([names, places.astype(jnp.int32), path, keeps[None]])

    vectors = jax.ShapeDtypeStruct((leafs + tops, columns, wide), f32)
    cost = pl.CostEstimate(flops=4 * 10**9, bytes_accessed=8 * 2**20, transcendentals=0)
    factors, state = [], None
    for k, base in enumerate(starts[:-1]):
        last = k == len(CHUNKS) - 1
        steps = starts[k + 1] - base
        merged = jax.ShapeDtypeStruct((steps, 3 * wide, wide), bf16)
        chunk = jax.ShapeDtypeStruct((steps, columns, wide), f32)
        shapes = [vectors, merged, merged, chunk]
        if k == 0:
            last_far = to_trader(far[-1])
            passed = (early[2], to_trader(after(last_far, across[k])))
        else:
            passed = (last_far, to_trader(after(state, across[k])))
        specs = [SMEM] + [pl.BlockSpec(memory_space=pl.ANY)] * 8 + [
            pl.BlockSpec((steps * columns, wide), functools.partial(lambda k, i: (k, 0), base // steps)),
            pl.BlockSpec((columns, wide), lambda i: (leafs, 0)),
        ]
        if last:
            shapes.append(jax.ShapeDtypeStruct((tops, width + 1, part, wide), f32))
        before = () if k == 0 else (state,)
        results = pl.pallas_call(
            functools.partial(forward_kernel, base, leafs, k == 0, last, width),
            grid=(1,),
            in_specs=specs + [VMEM] * (k > 0),
            out_specs=[VMEM] * len(shapes),
            out_shape=shapes,
            scratch_shapes=[
                pltpu.VMEM((steps, 4, wide, wide), f32),
                pltpu.SemaphoreType.DMA((steps // GROUP, 4)),
            ],
            compiler_params=params(),
            cost_estimate=cost,
            name="leaf_forward",
        )(meta, own, near, far[k], across[k], *early[:2], *passed, sides, sides, *before)
        state = results[0]
        factors.append(results[1:4])

    def whole(*shape):
        return pl.BlockSpec((1,) + shape, lambda t: (t,) + (0,) * len(shape))

    top_places = jnp.stack([2 * zh + zl, 2 - 2 * zh + zl, 2 * zh + 1 - zl, 3 - 2 * zh - zl])
    top_factor = pl.pallas_call(
        top_prepare_kernel,
        grid=(tops,),
        in_specs=[SMEM, whole(*top.shape[1:])],
        out_specs=[whole(most * wide, wide)] * 2 + [whole(wide, wide)] * 2,
        out_shape=[jax.ShapeDtypeStruct((tops, most * wide, wide), bf16)] * 2
        + [jax.ShapeDtypeStruct((tops, wide, wide), bf16)] * 2,
        scratch_shapes=[pltpu.VMEM((width, wide, wide), f32)],
        compiler_params=params(),
        name="top_prepare",
    )(top_places.astype(jnp.int32), after(results[4], top))

    incoming = lax.all_to_all(results[4], ("xy", "zh"), split_axis=0, concat_axis=0, tiled=True)
    outgoing = pl.pallas_call(
        functools.partial(top_kernel, above, paths),
        in_specs=[VMEM] * 5,
        out_specs=VMEM,
        out_shape=jax.ShapeDtypeStruct((tops, width + 1, part, wide), f32),
        compiler_params=params(),
        name="top_solve",
    )(incoming, *top_factor)
    state = lax.all_to_all(outgoing, ("xy", "zh"), split_axis=0, concat_axis=0, tiled=True)
    own_top = state[:groups, width].reshape(1, columns, wide)

    found = [None] * TURNS
    chunk = jax.ShapeDtypeStruct((turn, columns, wide), f32)
    for k in range(TURNS - 1, -1, -1):
        held = max(i for i, at in enumerate(starts[:-1]) if at <= k * turn)
        part_of = [
            pl.BlockSpec(
                (turn,) + shape, functools.partial(lambda at, i: (at, 0, 0), k - starts[held] // turn)
            )
            for shape in ((3 * wide, wide), (3 * wide, wide), (columns, wide))
        ]
        found[k], state = pl.pallas_call(
            functools.partial(backward_kernel, k * turn, k == TURNS - 1, width),
            grid=(1,),
            in_specs=[SMEM] + part_of + [VMEM],
            out_specs=[VMEM] * 2,
            out_shape=[chunk, vectors],
            compiler_params=params(),
            cost_estimate=cost,
            name="leaf_backward",
        )(meta, *factors[held], state)
    late = swap(jnp.concatenate([own_top, found[-1]], axis=0))
    middle = swap(jnp.concatenate(found[1:-1], axis=0))
    first = swap(found[0])
    leaf_solution = jnp.concatenate([first, middle, late[1:]], axis=0)
    return (leaf_solution, late[:1])


def solution(mesh):
    subtrees, quarters = mesh.devices.shape
    fine = Mesh(
        mesh.devices.reshape(subtrees // 2, 2, 2, quarters // 2), ("xy", "core", "zh", "zl")
    )
    sn, rhs = ("xy", "core"), ("zh", "zl")
    return jax.shard_map(
        local,
        mesh=fine,
        in_specs=(
            P(sn, rhs, None),
            P(sn, rhs, None),
            P(sn, None, rhs, None),
            P(sn, rhs, None),
            P(sn, None),
            P(None, sn, rhs, None),
            P(sn, rhs, None),
        ),
        out_specs=(P(sn, rhs, None), P(sn, rhs, None)),
        check_vma=False,
    )
```

```python
import functools

import jax
import jax.numpy as jnp
import numpy as np
from jax import lax
from jax.experimental import pallas as pl
from jax.experimental.pallas import tpu as pltpu
from jax.sharding import Mesh
from jax.sharding import PartitionSpec as P

CHUNKS = (3, 1)
TURNS = 4
GROUP = 4
f32 = jnp.float32
bf16 = jnp.bfloat16
SMEM = pl.BlockSpec(memory_space=pltpu.SMEM)
VMEM = pl.BlockSpec(memory_space=pltpu.VMEM)
HBM = pl.BlockSpec(memory_space=pltpu.HBM)


def params():
    return pltpu.CompilerParams(vmem_limit_bytes=28 * 2**20)


def split(value):
    high = value.astype(bf16)
    return high, (value - high.astype(f32)).astype(bf16)


def product(left, right, transposed):
    dims = (((1,), (1 if transposed else 0,)), ((), ()))

    def dot(a, b):
        return lax.dot_general(a, b, dims, preferred_element_type=f32)

    rows = left[0].shape[0]
    if rows % 16:
        return dot(left[0], right[0]) + (dot(left[1], right[0]) + dot(left[0], right[1]))
    both = dot(jnp.concatenate(left, axis=0), right[0])
    return both[:rows] + (both[rows:] + dot(left[0], right[1]))


def ancestors_of(tops):
    def level(t):
        return ((t + 1) & -(t + 1)).bit_length() - 1

    return [[t for t in range(j + 1, tops) if t + 1 - 2 ** level(t) <= j] for j in range(tops)]


def paths_of(subtrees, above):
    return [[4 * (d // 4)] + above[4 * (d // 4)] for d in range(subtrees)]


def padded(rows, width):
    return np.array([row + [row[0] if row else 0] * (width - len(row)) for row in rows], np.int32)


def forward_kernel(base, leafs, first, last, width, *refs):
    meta, kept, passed, rhs, rhs_top = refs[0], refs[1:5], refs[5:9], refs[9], refs[10]
    refs = refs[11:]
    if not first:
        acc_in, refs = refs[0], refs[1:]
    acc, high_out, low_out, scaled, refs = refs[0], refs[1], refs[2], refs[3], refs[4:]
    if last:
        payload, refs = refs[0], refs[1:]
    full, high, low, arrived, stored = refs
    steps, columns, rows = scaled.shape[0], scaled.shape[1], kept[0].shape[2]
    wide = full.shape[2]

    def copies(pieces, group):
        made = []
        for place, piece in enumerate(pieces):
            offset = pl.multiple_of(meta[3 * leafs + place] * rows, rows)
            start = group * GROUP + (base if piece.shape[0] > steps else 0)
            made.append(
                pltpu.make_async_copy(
                    piece.at[pl.ds(start, GROUP)],
                    full.at[pl.ds(group * GROUP, GROUP), :, pl.ds(offset, rows), :],
                    arrived.at[group, place],
                )
            )
        return made

    def stores(group):
        at = pl.ds(group * GROUP, GROUP)
        return [
            pltpu.make_async_copy(high.at[at], high_out.at[at], stored.at[group, 0]),
            pltpu.make_async_copy(low.at[at], low_out.at[at], stored.at[group, 1]),
        ]

    def start(pieces):
        for group in range(steps // GROUP):
            for copy in copies(pieces, group):
                copy.start()

    keeps = meta[3 * leafs + 4 + width]
    pl.when(keeps == 1)(lambda: start(kept))
    pl.when(keeps == 0)(lambda: start(passed))
    if first:
        acc[...] = jnp.zeros_like(acc)
    else:
        acc[...] = acc_in[...]
    for group in range(steps // GROUP):
        for copy in copies(kept, group):
            copy.wait()
        members = range(group * GROUP, (group + 1) * GROUP)
        for s in members:
            blocks = split(full[s, 0:3].reshape(3 * wide, wide))
            merged = split(product(blocks, split(full[s, 3]), False))
            high[s] = merged[0]
            low[s] = merged[1]
        for store in stores(group):
            store.start()
        for s in members:
            at = s * columns
            source = split(rhs[at : at + columns] - acc[base + s])
            outgoing = product(source, (high[s], low[s]), True)
            for r in range(3):
                target = meta[3 * (base + s) + r]
                acc[target] = acc[target] + outgoing[:, r * wide : (r + 1) * wide]
            inverse = split(full[s, 3])
            solved = split(product(source, inverse, True))
            scaled[s] = product(solved, inverse, False)
    if last:
        peers, part = payload.shape[0], payload.shape[2]
        groups = columns // part
        for i in range(width + 1):
            node = acc[leafs + meta[3 * leafs + 4 + i]] if i < width else rhs_top[...]
            for p in range(peers):
                at = (p % groups) * part
                payload[p, i] = node[at : at + part]
    for group in range(steps // GROUP):
        for store in stores(group):
            store.wait()


def backward_kernel(base, first, width, meta, high, low, scaled, state, out, z):
    steps, wide = scaled.shape[0], scaled.shape[2]
    leafs = steps * TURNS
    if first:
        part = state.shape[2]
        groups = scaled.shape[1] // part
        z[...] = jnp.zeros_like(z)
        for i in range(width):
            node = leafs + meta[3 * leafs + 4 + i]
            for p in range(groups):
                z[node, p * part : (p + 1) * part, :] = state[p, i]
    else:
        z[...] = state[...]
    for s in range(steps - 1, -1, -1):
        total = scaled[s]
        for r in (2, 1, 0):
            source = split(z[meta[3 * (base + s) + r]])
            at = slice(r * wide, (r + 1) * wide)
            total = total - product(source, (high[s, at], low[s, at]), False)
        z[base + s] = total
        out[s] = total


def top_prepare_kernel(places, top, high, low, inverse_high, inverse_low, full):
    blocks, rows, wide = top.shape[2], top.shape[3], top.shape[4]
    for place in range(top.shape[1]):
        offset = pl.multiple_of(places[place] * rows, rows)
        full[:, pl.ds(offset, rows), :] = top[0, place]
    inverse = split(full[blocks - 1])
    merged = product(split(full[: blocks - 1].reshape((blocks - 1) * wide, wide)), inverse, False)
    high[0], low[0] = split(merged)
    inverse_high[0], inverse_low[0] = inverse


def top_kernel(above, paths, incoming, high, low, inverse_high, inverse_low, outgoing):
    tops, wide = len(above), high.shape[2]
    width = outgoing.shape[1] - 1
    sources = [incoming[t, width] for t in range(tops)]
    for d, path in enumerate(paths):
        for i, t in enumerate(path):
            sources[t] = sources[t] - incoming[d, i]
    scaled = []
    for j in range(tops):
        source = split(sources[j])
        count = len(above[j])
        if count:
            rows = slice(0, count * wide)
            updates = product(source, (high[j, rows], low[j, rows]), True)
            for i, t in enumerate(above[j]):
                sources[t] = sources[t] - updates[:, i * wide : (i + 1) * wide]
        inverse = (inverse_high[j], inverse_low[j])
        scaled.append(product(split(product(source, inverse, True)), inverse, False))
    solved = [None] * tops
    parts = [None] * tops
    for j in range(tops - 1, -1, -1):
        total = scaled[j]
        for i, t in enumerate(above[j]):
            rows = slice(i * wide, (i + 1) * wide)
            total = total - product(parts[t], (high[j, rows], low[j, rows]), False)
        solved[j] = total
        parts[j] = split(total)
    for p in range(outgoing.shape[0]):
        path = paths[p]
        for i in range(width):
            outgoing[p, i] = solved[path[i] if i < len(path) else path[0]]
        outgoing[p, width] = solved[p]


def local(rhs_leaf, rhs_top, leaf_blocks, leaf_dinv, leaf_struct, top_blocks, top_dinv):
    leafs, columns, wide = rhs_leaf.shape
    tops = top_blocks.shape[0]
    turn = leafs // TURNS
    starts = [turn * sum(CHUNKS[:k]) for k in range(len(CHUNKS) + 1)]
    above = ancestors_of(tops)
    most = max(len(row) for row in above)
    width = most + 1
    paths = paths_of(tops, above)
    groups = min(tops, columns // 8)
    part = columns // groups

    core, zh, zl = lax.axis_index("core"), lax.axis_index("zh"), lax.axis_index("zl")
    xy = lax.axis_index("xy")

    def swap(value):
        return lax.ppermute(value, ("core", "zh"), [(0, 0), (1, 2), (2, 1), (3, 3)])

    def to_keeper(value):
        return lax.ppermute(value, ("core", "zh"), [(1, 0), (2, 3)])

    def to_trader(value):
        return lax.ppermute(value, ("core", "zh"), [(0, 2), (3, 1)])

    def keepers(value):
        return lax.ppermute(value, ("core", "zh", "zl"), [(0, 1), (1, 0), (6, 7), (7, 6)])

    def other(value, *axes):
        last = 2 ** len(axes) - 1
        return lax.ppermute(value, axes, [(i, last - i) for i in range(last + 1)])

    def after(first, value):
        return lax.optimization_barrier((first, value))[1]

    chosen = jnp.take(top_blocks[:, 0], jnp.asarray(padded(above, most))[2 * xy + core], axis=0)
    top = jnp.concatenate([chosen, top_dinv], axis=0)
    top = jnp.stack([top, other(top, "zh")])
    top = jnp.concatenate([top, other(top, "zl")])

    names = jnp.zeros((8, wide), f32).at[:3, :leafs].set(leaf_struct.T.astype(f32))
    sides = jnp.concatenate([rhs_leaf.reshape(-1, wide), rhs_top.reshape(-1, wide), names], axis=0)
    def joined(at):
        return jnp.concatenate([leaf_blocks[at], leaf_dinv[at][:, None]], axis=1)

    own = joined(slice(None))
    parts = [joined(slice(at, end)) for at, end in zip(starts, starts[1:])]
    own, parts, sides = after(top, (own, parts, sides))

    near = keepers(own)
    sides = swap(sides)
    far = [to_keeper(part) for part in parts]
    across = [keepers(far[0])]
    early = [to_trader(value) for value in (own, near, far[0])]
    across += [keepers(after(early, value)) for value in far[1:]]
    top = lax.all_gather(after((far[-1], sides), top), ("xy", "core"), axis=0, tiled=False)

    names = sides[(leafs + 1) * columns :][:3, :leafs].T.astype(jnp.int32).reshape(-1)
    path = jnp.asarray(padded(paths, width))[2 * xy + zh]
    places = jnp.stack([2 * zh + zl, 2 * zh + 1 - zl, 2 - 2 * zh + zl, 3 - 2 * zh - zl])
    keeps = (core == zh).astype(jnp.int32)
    meta = jnp.concatenate([names, places.astype(jnp.int32), path, keeps[None]])

    vectors = jax.ShapeDtypeStruct((leafs + tops, columns, wide), f32)
    cost = pl.CostEstimate(flops=4 * 10**9, bytes_accessed=8 * 2**20, transcendentals=0)
    factors, state = [], None
    for k, base in enumerate(starts[:-1]):
        last = k == len(CHUNKS) - 1
        steps = starts[k + 1] - base
        merged = jax.ShapeDtypeStruct((steps, 3 * wide, wide), bf16)
        chunk = jax.ShapeDtypeStruct((steps, columns, wide), f32)
        shapes = [vectors, merged, merged, chunk]
        if k == 0:
            last_far = to_trader(far[-1])
            passed = (early[2], to_trader(after(last_far, across[k])))
        else:
            passed = (last_far, to_trader(after(state, across[k])))
        specs = [SMEM] + [pl.BlockSpec(memory_space=pl.ANY)] * 8 + [
            pl.BlockSpec((steps * columns, wide), functools.partial(lambda k, i: (k, 0), base // steps)),
            pl.BlockSpec((columns, wide), lambda i: (leafs, 0)),
        ]
        if last:
            shapes.append(jax.ShapeDtypeStruct((tops, width + 1, part, wide), f32))
        before = () if k == 0 else (state,)
        results = pl.pallas_call(
            functools.partial(forward_kernel, base, leafs, k == 0, last, width),
            grid=(1,),
            in_specs=specs + [VMEM] * (k > 0),
            out_specs=[VMEM, HBM, HBM, VMEM] + [VMEM] * last,
            out_shape=shapes,
            scratch_shapes=[
                pltpu.VMEM((steps, 4, wide, wide), f32),
                pltpu.VMEM((steps, 3 * wide, wide), bf16),
                pltpu.VMEM((steps, 3 * wide, wide), bf16),
                pltpu.SemaphoreType.DMA((steps // GROUP, 4)),
                pltpu.SemaphoreType.DMA((steps // GROUP, 2)),
            ],
            compiler_params=params(),
            cost_estimate=cost,
            name="leaf_forward",
        )(meta, own, near, far[k], across[k], *early[:2], *passed, sides, sides, *before)
        state = results[0]
        factors.append(results[1:4])

    def whole(*shape):
        return pl.BlockSpec((1,) + shape, lambda t: (t,) + (0,) * len(shape))

    top_places = jnp.stack([2 * zh + zl, 2 - 2 * zh + zl, 2 * zh + 1 - zl, 3 - 2 * zh - zl])
    top_factor = pl.pallas_call(
        top_prepare_kernel,
        grid=(tops,),
        in_specs=[SMEM, whole(*top.shape[1:])],
        out_specs=[whole(most * wide, wide)] * 2 + [whole(wide, wide)] * 2,
        out_shape=[jax.ShapeDtypeStruct((tops, most * wide, wide), bf16)] * 2
        + [jax.ShapeDtypeStruct((tops, wide, wide), bf16)] * 2,
        scratch_shapes=[pltpu.VMEM((width, wide, wide), f32)],
        compiler_params=params(),
        name="top_prepare",
    )(top_places.astype(jnp.int32), after(results[4], top))

    incoming = lax.all_to_all(results[4], ("xy", "zh"), split_axis=0, concat_axis=0, tiled=True)
    outgoing = pl.pallas_call(
        functools.partial(top_kernel, above, paths),
        in_specs=[VMEM] * 5,
        out_specs=VMEM,
        out_shape=jax.ShapeDtypeStruct((tops, width + 1, part, wide), f32),
        compiler_params=params(),
        name="top_solve",
    )(incoming, *top_factor)
    state = lax.all_to_all(outgoing, ("xy", "zh"), split_axis=0, concat_axis=0, tiled=True)
    own_top = state[:groups, width].reshape(1, columns, wide)

    found = [None] * TURNS
    chunk = jax.ShapeDtypeStruct((turn, columns, wide), f32)
    for k in range(TURNS - 1, -1, -1):
        held = max(i for i, at in enumerate(starts[:-1]) if at <= k * turn)
        part_of = [
            pl.BlockSpec(
                (turn,) + shape, functools.partial(lambda at, i: (at, 0, 0), k - starts[held] // turn)
            )
            for shape in ((3 * wide, wide), (3 * wide, wide), (columns, wide))
        ]
        found[k], state = pl.pallas_call(
            functools.partial(backward_kernel, k * turn, k == TURNS - 1, width),
            grid=(1,),
            in_specs=[SMEM] + part_of + [VMEM],
            out_specs=[VMEM] * 2,
            out_shape=[chunk, vectors],
            compiler_params=params(),
            cost_estimate=cost,
            name="leaf_backward",
        )(meta, *factors[held], state)
    late = swap(jnp.concatenate([own_top, found[-1]], axis=0))
    middle = swap(jnp.concatenate(found[1:-1], axis=0))
    first = swap(found[0])
    leaf_solution = jnp.concatenate([first, middle, late[1:]], axis=0)
    return (leaf_solution, late[:1])


def solution(mesh):
    subtrees, quarters = mesh.devices.shape
    fine = Mesh(
        mesh.devices.reshape(subtrees // 2, 2, 2, quarters // 2), ("xy", "core", "zh", "zl")
    )
    sn, rhs = ("xy", "core"), ("zh", "zl")
    return jax.shard_map(
        local,
        mesh=fine,
        in_specs=(
            P(sn, rhs, None),
            P(sn, rhs, None),
            P(sn, None, rhs, None),
            P(sn, rhs, None),
            P(sn, None),
            P(None, sn, rhs, None),
            P(sn, rhs, None),
        ),
        out_specs=(P(sn, rhs, None), P(sn, rhs, None)),
        check_vma=False,
    )
```

```python
import functools

import jax
import jax.numpy as jnp
import numpy as np
from jax import lax
from jax.experimental import pallas as pl
from jax.experimental.pallas import tpu as pltpu
from jax.sharding import Mesh
from jax.sharding import PartitionSpec as P

CHUNKS = (3, 1)
TURNS = 4
GROUP = 4
f32 = jnp.float32
bf16 = jnp.bfloat16
SMEM = pl.BlockSpec(memory_space=pltpu.SMEM)
VMEM = pl.BlockSpec(memory_space=pltpu.VMEM)


def params():
    return pltpu.CompilerParams(vmem_limit_bytes=28 * 2**20)


def split(value):
    high = value.astype(bf16)
    return high, (value - high.astype(f32)).astype(bf16)


def product(left, right, transposed):
    dims = (((1,), (1 if transposed else 0,)), ((), ()))

    def dot(a, b):
        return lax.dot_general(a, b, dims, preferred_element_type=f32)

    rows = left[0].shape[0]
    if rows % 16:
        return dot(left[0], right[0]) + (dot(left[1], right[0]) + dot(left[0], right[1]))
    both = dot(jnp.concatenate(left, axis=0), right[0])
    return both[:rows] + (both[rows:] + dot(left[0], right[1]))


def ancestors_of(tops):
    def level(t):
        return ((t + 1) & -(t + 1)).bit_length() - 1

    return [[t for t in range(j + 1, tops) if t + 1 - 2 ** level(t) <= j] for j in range(tops)]


def paths_of(subtrees, above):
    return [[4 * (d // 4)] + above[4 * (d // 4)] for d in range(subtrees)]


def padded(rows, width):
    return np.array([row + [row[0] if row else 0] * (width - len(row)) for row in rows], np.int32)


def forward_kernel(base, leafs, first, last, width, *refs):
    meta, kept, passed, rhs, rhs_top = refs[0], refs[1:5], refs[5:9], refs[9], refs[10]
    refs = refs[11:]
    if not first:
        acc_in, refs = refs[0], refs[1:]
    acc, high, low, scaled, refs = refs[0], refs[1], refs[2], refs[3], refs[4:]
    if last:
        payload, refs = refs[0], refs[1:]
    full, arrived = refs
    steps, columns, rows = scaled.shape[0], scaled.shape[1], kept[0].shape[2]
    wide = full.shape[2]

    def copies(pieces, group):
        made = []
        for place, piece in enumerate(pieces):
            offset = pl.multiple_of(meta[3 * leafs + place] * rows, rows)
            start = group * GROUP + (base if piece.shape[0] > steps else 0)
            made.append(
                pltpu.make_async_copy(
                    piece.at[pl.ds(start, GROUP)],
                    full.at[pl.ds(group * GROUP, GROUP), :, pl.ds(offset, rows), :],
                    arrived.at[group, place],
                )
            )
        return made

    def start(pieces):
        for group in range(steps // GROUP):
            for copy in copies(pieces, group):
                copy.start()

    keeps = meta[3 * leafs + 4 + width]
    pl.when(keeps == 1)(lambda: start(kept))
    pl.when(keeps == 0)(lambda: start(passed))
    if first:
        acc[...] = jnp.zeros_like(acc)
    else:
        acc[...] = acc_in[...]
    for group in range(steps // GROUP):
        for copy in copies(kept, group):
            copy.wait()
        members = range(group * GROUP, (group + 1) * GROUP)
        for s in members:
            blocks = split(full[s, 0:3].reshape(3 * wide, wide))
            merged = split(product(blocks, split(full[s, 3]), False))
            high[s] = merged[0]
            low[s] = merged[1]
        for s in members:
            at = s * columns
            source = split(rhs[at : at + columns] - acc[base + s])
            outgoing = product(source, (high[s], low[s]), True)
            for r in range(3):
                target = meta[3 * (base + s) + r]
                acc[target] = acc[target] + outgoing[:, r * wide : (r + 1) * wide]
            inverse = split(full[s, 3])
            solved = split(product(source, inverse, True))
            scaled[s] = product(solved, inverse, False)
    if last:
        peers, part = payload.shape[0], payload.shape[2]
        groups = columns // part
        for i in range(width + 1):
            node = acc[leafs + meta[3 * leafs + 4 + i]] if i < width else rhs_top[...]
            for p in range(peers):
                at = (p % groups) * part
                payload[p, i] = node[at : at + part]


def backward_kernel(base, first, width, meta, high, low, scaled, state, out, z):
    steps, wide = scaled.shape[0], scaled.shape[2]
    leafs = steps * TURNS
    if first:
        part = state.shape[2]
        groups = scaled.shape[1] // part
        z[...] = jnp.zeros_like(z)
        for i in range(width):
            node = leafs + meta[3 * leafs + 4 + i]
            for p in range(groups):
                z[node, p * part : (p + 1) * part, :] = state[p, i]
    else:
        z[...] = state[...]
    for s in range(steps - 1, -1, -1):
        total = scaled[s]
        for r in (2, 1, 0):
            source = split(z[meta[3 * (base + s) + r]])
            at = slice(r * wide, (r + 1) * wide)
            total = total - product(source, (high[s, at], low[s, at]), False)
        z[base + s] = total
        out[s] = total


def top_prepare_kernel(places, top, high, low, inverse_high, inverse_low, full):
    blocks, rows, wide = top.shape[2], top.shape[3], top.shape[4]
    for place in range(top.shape[1]):
        offset = pl.multiple_of(places[place] * rows, rows)
        full[:, pl.ds(offset, rows), :] = top[0, place]
    inverse = split(full[blocks - 1])
    merged = product(split(full[: blocks - 1].reshape((blocks - 1) * wide, wide)), inverse, False)
    high[0], low[0] = split(merged)
    inverse_high[0], inverse_low[0] = inverse


def top_kernel(above, paths, incoming, high, low, inverse_high, inverse_low, outgoing):
    tops, wide = len(above), high.shape[2]
    width = outgoing.shape[1] - 1
    sources = [incoming[t, width] for t in range(tops)]
    for d, path in enumerate(paths):
        for i, t in enumerate(path):
            sources[t] = sources[t] - incoming[d, i]
    scaled = []
    for j in range(tops):
        source = split(sources[j])
        count = len(above[j])
        if count:
            rows = slice(0, count * wide)
            updates = product(source, (high[j, rows], low[j, rows]), True)
            for i, t in enumerate(above[j]):
                sources[t] = sources[t] - updates[:, i * wide : (i + 1) * wide]
        inverse = (inverse_high[j], inverse_low[j])
        scaled.append(product(split(product(source, inverse, True)), inverse, False))
    solved = [None] * tops
    parts = [None] * tops
    for j in range(tops - 1, -1, -1):
        total = scaled[j]
        for i, t in enumerate(above[j]):
            rows = slice(i * wide, (i + 1) * wide)
            total = total - product(parts[t], (high[j, rows], low[j, rows]), False)
        solved[j] = total
        parts[j] = split(total)
    for p in range(outgoing.shape[0]):
        path = paths[p]
        for i in range(width):
            outgoing[p, i] = solved[path[i] if i < len(path) else path[0]]
        outgoing[p, width] = solved[p]


def local(rhs_leaf, rhs_top, leaf_blocks, leaf_dinv, leaf_struct, top_blocks, top_dinv):
    leafs, columns, wide = rhs_leaf.shape
    tops = top_blocks.shape[0]
    turn = leafs // TURNS
    starts = [turn * sum(CHUNKS[:k]) for k in range(len(CHUNKS) + 1)]
    above = ancestors_of(tops)
    most = max(len(row) for row in above)
    width = most + 1
    paths = paths_of(tops, above)
    groups = min(tops, columns // 8)
    part = columns // groups

    core, zh, zl = lax.axis_index("core"), lax.axis_index("zh"), lax.axis_index("zl")
    xy = lax.axis_index("xy")

    def swap(value):
        return lax.ppermute(value, ("core", "zh"), [(0, 0), (1, 2), (2, 1), (3, 3)])

    def to_keeper(value):
        return lax.ppermute(value, ("core", "zh"), [(1, 0), (2, 3)])

    def to_trader(value):
        return lax.ppermute(value, ("core", "zh"), [(0, 2), (3, 1)])

    def keepers(value):
        return lax.ppermute(value, ("core", "zh", "zl"), [(0, 1), (1, 0), (6, 7), (7, 6)])

    def other(value, *axes):
        last = 2 ** len(axes) - 1
        return lax.ppermute(value, axes, [(i, last - i) for i in range(last + 1)])

    def after(first, value):
        return lax.optimization_barrier((first, value))[1]

    chosen = jnp.take(top_blocks[:, 0], jnp.asarray(padded(above, most))[2 * xy + core], axis=0)
    top = jnp.concatenate([chosen, top_dinv], axis=0)
    top = jnp.stack([top, other(top, "zh")])
    top = jnp.concatenate([top, other(top, "zl")])

    names = jnp.zeros((8, wide), f32).at[:3, :leafs].set(leaf_struct.T.astype(f32))
    sides = jnp.concatenate([rhs_leaf.reshape(-1, wide), rhs_top.reshape(-1, wide), names], axis=0)
    def joined(at):
        return jnp.concatenate([leaf_blocks[at], leaf_dinv[at][:, None]], axis=1)

    own = joined(slice(None))
    parts = [joined(slice(at, end)) for at, end in zip(starts, starts[1:])]
    own, parts, sides = after(top, (own, parts, sides))

    near = keepers(own)
    sides = swap(sides)
    far = [to_keeper(part) for part in parts]
    across = [keepers(far[0])]
    early = [to_trader(value) for value in (own, near, far[0])]
    across += [keepers(after(early, value)) for value in far[1:]]
    top = lax.all_gather(after((far[-1], sides), top), ("xy", "core"), axis=0, tiled=False)

    names = sides[(leafs + 1) * columns :][:3, :leafs].T.astype(jnp.int32).reshape(-1)
    path = jnp.asarray(padded(paths, width))[2 * xy + zh]
    places = jnp.stack([2 * zh + zl, 2 * zh + 1 - zl, 2 - 2 * zh + zl, 3 - 2 * zh - zl])
    keeps = (core == zh).astype(jnp.int32)
    meta = jnp.concatenate([names, places.astype(jnp.int32), path, keeps[None]])

    vectors = jax.ShapeDtypeStruct((leafs + tops, columns, wide), f32)
    cost = pl.CostEstimate(flops=4 * 10**9, bytes_accessed=8 * 2**20, transcendentals=0)
    factors, state = [], None
    for k, base in enumerate(starts[:-1]):
        last = k == len(CHUNKS) - 1
        steps = starts[k + 1] - base
        merged = jax.ShapeDtypeStruct((steps, 3 * wide, wide), bf16)
        chunk = jax.ShapeDtypeStruct((steps, columns, wide), f32)
        shapes = [vectors, merged, merged, chunk]
        if k == 0:
            last_far = to_trader(far[-1])
            passed = (early[2], to_trader(after(last_far, across[k])))
        else:
            passed = (last_far, to_trader(after(state, across[k])))
        specs = [SMEM] + [pl.BlockSpec(memory_space=pl.ANY)] * 8 + [
            pl.BlockSpec((steps * columns, wide), functools.partial(lambda k, i: (k, 0), base // steps)),
            pl.BlockSpec((columns, wide), lambda i: (leafs, 0)),
        ]
        if last:
            shapes.append(jax.ShapeDtypeStruct((tops, width + 1, part, wide), f32))
        before = () if k == 0 else (state,)
        results = pl.pallas_call(
            functools.partial(forward_kernel, base, leafs, k == 0, last, width),
            grid=(1,),
            in_specs=specs + [VMEM] * (k > 0),
            out_specs=[VMEM] * len(shapes),
            out_shape=shapes,
            scratch_shapes=[
                pltpu.VMEM((steps, 4, wide, wide), f32),
                pltpu.SemaphoreType.DMA((steps // GROUP, 4)),
            ],
            compiler_params=params(),
            cost_estimate=cost,
            name="leaf_forward",
        )(meta, own, near, far[k], across[k], *early[:2], *passed, sides, sides, *before)
        state = results[0]
        factors.append(results[1:4])

    def whole(*shape):
        return pl.BlockSpec((1,) + shape, lambda t: (t,) + (0,) * len(shape))

    top_places = jnp.stack([2 * zh + zl, 2 - 2 * zh + zl, 2 * zh + 1 - zl, 3 - 2 * zh - zl])
    top_factor = pl.pallas_call(
        top_prepare_kernel,
        grid=(tops,),
        in_specs=[SMEM, whole(*top.shape[1:])],
        out_specs=[whole(most * wide, wide)] * 2 + [whole(wide, wide)] * 2,
        out_shape=[jax.ShapeDtypeStruct((tops, most * wide, wide), bf16)] * 2
        + [jax.ShapeDtypeStruct((tops, wide, wide), bf16)] * 2,
        scratch_shapes=[pltpu.VMEM((width, wide, wide), f32)],
        compiler_params=params(),
        name="top_prepare",
    )(top_places.astype(jnp.int32), after(results[4], top))

    incoming = lax.all_to_all(results[4], ("xy", "zh"), split_axis=0, concat_axis=0, tiled=True)
    outgoing = pl.pallas_call(
        functools.partial(top_kernel, above, paths),
        in_specs=[VMEM] * 5,
        out_specs=VMEM,
        out_shape=jax.ShapeDtypeStruct((tops, width + 1, part, wide), f32),
        compiler_params=params(),
        name="top_solve",
    )(incoming, *top_factor)
    state = lax.all_to_all(outgoing, ("xy", "zh"), split_axis=0, concat_axis=0, tiled=True)
    own_top = state[:groups, width].reshape(1, columns, wide)

    found = [None] * TURNS
    chunk = jax.ShapeDtypeStruct((turn, columns, wide), f32)
    for k in range(TURNS - 1, -1, -1):
        held = max(i for i, at in enumerate(starts[:-1]) if at <= k * turn)
        part_of = [
            pl.BlockSpec(
                (turn,) + shape, functools.partial(lambda at, i: (at, 0, 0), k - starts[held] // turn)
            )
            for shape in ((3 * wide, wide), (3 * wide, wide), (columns, wide))
        ]
        found[k], state = pl.pallas_call(
            functools.partial(backward_kernel, k * turn, k == TURNS - 1, width),
            grid=(1,),
            in_specs=[SMEM] + part_of + [VMEM],
            out_specs=[VMEM] * 2,
            out_shape=[chunk, vectors],
            compiler_params=params(),
            cost_estimate=cost,
            name="leaf_backward",
        )(meta, *factors[held], state)
    late = swap(found[-1])
    middle = swap(after(late, jnp.concatenate(found[1:-1] + [own_top], axis=0)))
    first = swap(found[0])
    leaf_solution = jnp.concatenate([first, middle[:-1], late], axis=0)
    return (leaf_solution, middle[-1:])


def solution(mesh):
    subtrees, quarters = mesh.devices.shape
    fine = Mesh(
        mesh.devices.reshape(subtrees // 2, 2, 2, quarters // 2), ("xy", "core", "zh", "zl")
    )
    sn, rhs = ("xy", "core"), ("zh", "zl")
    return jax.shard_map(
        local,
        mesh=fine,
        in_specs=(
            P(sn, rhs, None),
            P(sn, rhs, None),
            P(sn, None, rhs, None),
            P(sn, rhs, None),
            P(sn, None),
            P(None, sn, rhs, None),
            P(sn, rhs, None),
        ),
        out_specs=(P(sn, rhs, None), P(sn, rhs, None)),
        check_vma=False,
    )
```

```python
import functools

import jax
import jax.numpy as jnp
import numpy as np
from jax import lax
from jax.experimental import pallas as pl
from jax.experimental.pallas import tpu as pltpu
from jax.sharding import Mesh
from jax.sharding import PartitionSpec as P

CHUNKS = (3, 1)
TURNS = 4
GROUP = 4
f32 = jnp.float32
bf16 = jnp.bfloat16
SMEM = pl.BlockSpec(memory_space=pltpu.SMEM)
VMEM = pl.BlockSpec(memory_space=pltpu.VMEM)


def params():
    return pltpu.CompilerParams(vmem_limit_bytes=28 * 2**20)


def split(value):
    high = value.astype(bf16)
    return high, (value - high.astype(f32)).astype(bf16)


def product(left, right, transposed):
    dims = (((1,), (1 if transposed else 0,)), ((), ()))

    def dot(a, b):
        return lax.dot_general(a, b, dims, preferred_element_type=f32)

    rows = left[0].shape[0]
    if rows % 16:
        return dot(left[0], right[0]) + (dot(left[1], right[0]) + dot(left[0], right[1]))
    both = dot(jnp.concatenate(left, axis=0), right[0])
    return both[:rows] + (both[rows:] + dot(left[0], right[1]))


def ancestors_of(tops):
    def level(t):
        return ((t + 1) & -(t + 1)).bit_length() - 1

    return [[t for t in range(j + 1, tops) if t + 1 - 2 ** level(t) <= j] for j in range(tops)]


def paths_of(subtrees, above):
    return [[4 * (d // 4)] + above[4 * (d // 4)] for d in range(subtrees)]


def padded(rows, width):
    return np.array([row + [row[0] if row else 0] * (width - len(row)) for row in rows], np.int32)


def forward_kernel(base, leafs, first, last, width, *refs):
    meta, kept, passed, rhs, rhs_top = refs[0], refs[1:5], refs[5:9], refs[9], refs[10]
    refs = refs[11:]
    if not first:
        acc_in, refs = refs[0], refs[1:]
    acc, high, low, scaled, refs = refs[0], refs[1], refs[2], refs[3], refs[4:]
    if last:
        payload, refs = refs[0], refs[1:]
    full, arrived = refs
    steps, columns, rows = scaled.shape[0], scaled.shape[1], kept[0].shape[2]
    wide = full.shape[2]

    def copies(pieces, group):
        made = []
        for place, piece in enumerate(pieces):
            offset = pl.multiple_of(meta[3 * leafs + place] * rows, rows)
            start = group * GROUP + (base if piece.shape[0] > steps else 0)
            made.append(
                pltpu.make_async_copy(
                    piece.at[pl.ds(start, GROUP)],
                    full.at[pl.ds(group * GROUP, GROUP), :, pl.ds(offset, rows), :],
                    arrived.at[group, place],
                )
            )
        return made

    def start(pieces):
        for group in range(steps // GROUP):
            for copy in copies(pieces, group):
                copy.start()

    keeps = meta[3 * leafs + 4 + width]
    pl.when(keeps == 1)(lambda: start(kept))
    pl.when(keeps == 0)(lambda: start(passed))
    if first:
        acc[...] = jnp.zeros_like(acc)
    else:
        acc[...] = acc_in[...]
    for group in range(steps // GROUP):
        for copy in copies(kept, group):
            copy.wait()
        members = range(group * GROUP, (group + 1) * GROUP)
        for s in members:
            blocks = split(full[s, 0:3].reshape(3 * wide, wide))
            merged = split(product(blocks, split(full[s, 3]), False))
            high[s] = merged[0]
            low[s] = merged[1]
        for s in members:
            at = s * columns
            source = split(rhs[at : at + columns] - acc[base + s])
            outgoing = product(source, (high[s], low[s]), True)
            for r in range(3):
                target = meta[3 * (base + s) + r]
                acc[target] = acc[target] + outgoing[:, r * wide : (r + 1) * wide]
            inverse = split(full[s, 3])
            solved = split(product(source, inverse, True))
            scaled[s] = product(solved, inverse, False)
    if last:
        peers, part = payload.shape[0], payload.shape[2]
        groups = columns // part
        for i in range(width + 1):
            node = acc[leafs + meta[3 * leafs + 4 + i]] if i < width else rhs_top[...]
            for p in range(peers):
                at = (p % groups) * part
                payload[p, i] = node[at : at + part]


def backward_kernel(base, first, width, meta, high, low, scaled, state, out, z):
    steps, wide = scaled.shape[0], scaled.shape[2]
    leafs = steps * TURNS
    if first:
        part = state.shape[2]
        groups = scaled.shape[1] // part
        z[...] = jnp.zeros_like(z)
        for i in range(width):
            node = leafs + meta[3 * leafs + 4 + i]
            for p in range(groups):
                z[node, p * part : (p + 1) * part, :] = state[p, i]
    else:
        z[...] = state[...]
    for s in range(steps - 1, -1, -1):
        total = scaled[s]
        for r in (2, 1, 0):
            source = split(z[meta[3 * (base + s) + r]])
            at = slice(r * wide, (r + 1) * wide)
            total = total - product(source, (high[s, at], low[s, at]), False)
        z[base + s] = total
        out[s] = total


def top_prepare_kernel(places, top, high, low, inverse_high, inverse_low, full):
    blocks, rows, wide = top.shape[2], top.shape[3], top.shape[4]
    for place in range(top.shape[1]):
        offset = pl.multiple_of(places[place] * rows, rows)
        full[:, pl.ds(offset, rows), :] = top[0, place]
    inverse = split(full[blocks - 1])
    merged = product(split(full[: blocks - 1].reshape((blocks - 1) * wide, wide)), inverse, False)
    high[0], low[0] = split(merged)
    inverse_high[0], inverse_low[0] = inverse


def top_kernel(above, paths, incoming, high, low, inverse_high, inverse_low, outgoing):
    tops, wide = len(above), high.shape[2]
    width = outgoing.shape[1] - 1
    sources = [incoming[t, width] for t in range(tops)]
    for d, path in enumerate(paths):
        for i, t in enumerate(path):
            sources[t] = sources[t] - incoming[d, i]
    scaled = []
    for j in range(tops):
        source = split(sources[j])
        count = len(above[j])
        if count:
            rows = slice(0, count * wide)
            updates = product(source, (high[j, rows], low[j, rows]), True)
            for i, t in enumerate(above[j]):
                sources[t] = sources[t] - updates[:, i * wide : (i + 1) * wide]
        inverse = (inverse_high[j], inverse_low[j])
        scaled.append(product(split(product(source, inverse, True)), inverse, False))
    solved = [None] * tops
    parts = [None] * tops
    for j in range(tops - 1, -1, -1):
        total = scaled[j]
        for i, t in enumerate(above[j]):
            rows = slice(i * wide, (i + 1) * wide)
            total = total - product(parts[t], (high[j, rows], low[j, rows]), False)
        solved[j] = total
        parts[j] = split(total)
    for p in range(outgoing.shape[0]):
        path = paths[p]
        for i in range(width):
            outgoing[p, i] = solved[path[i] if i < len(path) else path[0]]
        outgoing[p, width] = solved[p]


def local(rhs_leaf, rhs_top, leaf_blocks, leaf_dinv, leaf_struct, top_blocks, top_dinv):
    leafs, columns, wide = rhs_leaf.shape
    tops = top_blocks.shape[0]
    turn = leafs // TURNS
    starts = [turn * sum(CHUNKS[:k]) for k in range(len(CHUNKS) + 1)]
    above = ancestors_of(tops)
    most = max(len(row) for row in above)
    width = most + 1
    paths = paths_of(tops, above)
    groups = min(tops, columns // 8)
    part = columns // groups

    core, zh, zl = lax.axis_index("core"), lax.axis_index("zh"), lax.axis_index("zl")
    xy = lax.axis_index("xy")

    def swap(value):
        return lax.ppermute(value, ("core", "zh"), [(0, 0), (1, 2), (2, 1), (3, 3)])

    def to_keeper(value):
        return lax.ppermute(value, ("core", "zh"), [(1, 0), (2, 3)])

    def to_trader(value):
        return lax.ppermute(value, ("core", "zh"), [(0, 2), (3, 1)])

    def keepers(value):
        return lax.ppermute(value, ("core", "zh", "zl"), [(0, 1), (1, 0), (6, 7), (7, 6)])

    def other(value, *axes):
        last = 2 ** len(axes) - 1
        return lax.ppermute(value, axes, [(i, last - i) for i in range(last + 1)])

    def after(first, value):
        return lax.optimization_barrier((first, value))[1]

    chosen = jnp.take(top_blocks[:, 0], jnp.asarray(padded(above, most))[2 * xy + core], axis=0)
    top = jnp.concatenate([chosen, top_dinv], axis=0)
    top = jnp.stack([top, other(top, "zh"), other(top, "zl"), other(top, "zh", "zl")])

    names = jnp.zeros((8, wide), f32).at[:3, :leafs].set(leaf_struct.T.astype(f32))
    sides = jnp.concatenate([rhs_leaf.reshape(-1, wide), rhs_top.reshape(-1, wide), names], axis=0)
    def joined(at):
        return jnp.concatenate([leaf_blocks[at], leaf_dinv[at][:, None]], axis=1)

    own = joined(slice(None))
    parts = [joined(slice(at, end)) for at, end in zip(starts, starts[1:])]
    own, parts, sides = after(top, (own, parts, sides))

    near = keepers(own)
    sides = swap(sides)
    far = [to_keeper(part) for part in parts]
    across = [keepers(far[0])]
    early = [to_trader(value) for value in (own, near, far[0])]
    across += [keepers(after(early, value)) for value in far[1:]]
    top = lax.all_gather(after((far[-1], sides), top), ("xy", "core"), axis=0, tiled=False)

    names = sides[(leafs + 1) * columns :][:3, :leafs].T.astype(jnp.int32).reshape(-1)
    path = jnp.asarray(padded(paths, width))[2 * xy + zh]
    places = jnp.stack([2 * zh + zl, 2 * zh + 1 - zl, 2 - 2 * zh + zl, 3 - 2 * zh - zl])
    keeps = (core == zh).astype(jnp.int32)
    meta = jnp.concatenate([names, places.astype(jnp.int32), path, keeps[None]])

    vectors = jax.ShapeDtypeStruct((leafs + tops, columns, wide), f32)
    cost = pl.CostEstimate(flops=4 * 10**9, bytes_accessed=8 * 2**20, transcendentals=0)
    factors, state = [], None
    for k, base in enumerate(starts[:-1]):
        last = k == len(CHUNKS) - 1
        steps = starts[k + 1] - base
        merged = jax.ShapeDtypeStruct((steps, 3 * wide, wide), bf16)
        chunk = jax.ShapeDtypeStruct((steps, columns, wide), f32)
        shapes = [vectors, merged, merged, chunk]
        if k == 0:
            last_far = to_trader(far[-1])
            passed = (early[2], to_trader(after(last_far, across[k])))
        else:
            passed = (last_far, to_trader(after(state, across[k])))
        specs = [SMEM] + [pl.BlockSpec(memory_space=pl.ANY)] * 8 + [
            pl.BlockSpec((steps * columns, wide), functools.partial(lambda k, i: (k, 0), base // steps)),
            pl.BlockSpec((columns, wide), lambda i: (leafs, 0)),
        ]
        if last:
            shapes.append(jax.ShapeDtypeStruct((tops, width + 1, part, wide), f32))
        before = () if k == 0 else (state,)
        results = pl.pallas_call(
            functools.partial(forward_kernel, base, leafs, k == 0, last, width),
            grid=(1,),
            in_specs=specs + [VMEM] * (k > 0),
            out_specs=[VMEM] * len(shapes),
            out_shape=shapes,
            scratch_shapes=[
                pltpu.VMEM((steps, 4, wide, wide), f32),
                pltpu.SemaphoreType.DMA((steps // GROUP, 4)),
            ],
            compiler_params=params(),
            cost_estimate=cost,
            name="leaf_forward",
        )(meta, own, near, far[k], across[k], *early[:2], *passed, sides, sides, *before)
        state = results[0]
        factors.append(results[1:4])

    def whole(*shape):
        return pl.BlockSpec((1,) + shape, lambda t: (t,) + (0,) * len(shape))

    top_places = jnp.stack([2 * zh + zl, 2 - 2 * zh + zl, 2 * zh + 1 - zl, 3 - 2 * zh - zl])
    top_factor = pl.pallas_call(
        top_prepare_kernel,
        grid=(tops,),
        in_specs=[SMEM, whole(*top.shape[1:])],
        out_specs=[whole(most * wide, wide)] * 2 + [whole(wide, wide)] * 2,
        out_shape=[jax.ShapeDtypeStruct((tops, most * wide, wide), bf16)] * 2
        + [jax.ShapeDtypeStruct((tops, wide, wide), bf16)] * 2,
        scratch_shapes=[pltpu.VMEM((width, wide, wide), f32)],
        compiler_params=params(),
        name="top_prepare",
    )(top_places.astype(jnp.int32), after(results[4], top))

    incoming = lax.all_to_all(results[4], ("xy", "zh"), split_axis=0, concat_axis=0, tiled=True)
    outgoing = pl.pallas_call(
        functools.partial(top_kernel, above, paths),
        in_specs=[VMEM] * 5,
        out_specs=VMEM,
        out_shape=jax.ShapeDtypeStruct((tops, width + 1, part, wide), f32),
        compiler_params=params(),
        name="top_solve",
    )(incoming, *top_factor)
    state = lax.all_to_all(outgoing, ("xy", "zh"), split_axis=0, concat_axis=0, tiled=True)
    own_top = state[:groups, width].reshape(1, columns, wide)

    found = [None] * TURNS
    chunk = jax.ShapeDtypeStruct((turn, columns, wide), f32)
    for k in range(TURNS - 1, -1, -1):
        held = max(i for i, at in enumerate(starts[:-1]) if at <= k * turn)
        part_of = [
            pl.BlockSpec(
                (turn,) + shape, functools.partial(lambda at, i: (at, 0, 0), k - starts[held] // turn)
            )
            for shape in ((3 * wide, wide), (3 * wide, wide), (columns, wide))
        ]
        found[k], state = pl.pallas_call(
            functools.partial(backward_kernel, k * turn, k == TURNS - 1, width),
            grid=(1,),
            in_specs=[SMEM] + part_of + [VMEM],
            out_specs=[VMEM] * 2,
            out_shape=[chunk, vectors],
            compiler_params=params(),
            cost_estimate=cost,
            name="leaf_backward",
        )(meta, *factors[held], state)
    late = swap(found[-1])
    middle = swap(jnp.concatenate(found[1:-1] + [own_top], axis=0))
    first = swap(found[0])
    leaf_solution = jnp.concatenate([first, middle[:-1], late], axis=0)
    return (leaf_solution, middle[-1:])


def solution(mesh):
    subtrees, quarters = mesh.devices.shape
    fine = Mesh(
        mesh.devices.reshape(subtrees // 2, 2, 2, quarters // 2), ("xy", "core", "zh", "zl")
    )
    sn, rhs = ("xy", "core"), ("zh", "zl")
    return jax.shard_map(
        local,
        mesh=fine,
        in_specs=(
            P(sn, rhs, None),
            P(sn, rhs, None),
            P(sn, None, rhs, None),
            P(sn, rhs, None),
            P(sn, None),
            P(None, sn, rhs, None),
            P(sn, rhs, None),
        ),
        out_specs=(P(sn, rhs, None), P(sn, rhs, None)),
        check_vma=False,
    )
```

```python
import functools

import jax
import jax.numpy as jnp
import numpy as np
from jax import lax
from jax.experimental import pallas as pl
from jax.experimental.pallas import tpu as pltpu
from jax.sharding import Mesh
from jax.sharding import PartitionSpec as P

CHUNKS = (3, 1)
TURNS = 4
GROUP = 4
f32 = jnp.float32
bf16 = jnp.bfloat16
SMEM = pl.BlockSpec(memory_space=pltpu.SMEM)
VMEM = pl.BlockSpec(memory_space=pltpu.VMEM)


def params():
    return pltpu.CompilerParams(vmem_limit_bytes=28 * 2**20)


def split(value):
    high = value.astype(bf16)
    return high, (value - high.astype(f32)).astype(bf16)


def product(left, right, transposed):
    dims = (((1,), (1 if transposed else 0,)), ((), ()))

    def dot(a, b):
        return lax.dot_general(a, b, dims, preferred_element_type=f32)

    rows = left[0].shape[0]
    if rows % 16:
        return dot(left[0], right[0]) + (dot(left[1], right[0]) + dot(left[0], right[1]))
    both = dot(jnp.concatenate(left, axis=0), right[0])
    return both[:rows] + (both[rows:] + dot(left[0], right[1]))


def ancestors_of(tops):
    def level(t):
        return ((t + 1) & -(t + 1)).bit_length() - 1

    return [[t for t in range(j + 1, tops) if t + 1 - 2 ** level(t) <= j] for j in range(tops)]


def paths_of(subtrees, above):
    return [[4 * (d // 4)] + above[4 * (d // 4)] for d in range(subtrees)]


def padded(rows, width):
    return np.array([row + [row[0] if row else 0] * (width - len(row)) for row in rows], np.int32)


def forward_kernel(base, leafs, first, last, width, *refs):
    meta, kept, passed, rhs, rhs_top = refs[0], refs[1:5], refs[5:9], refs[9], refs[10]
    refs = refs[11:]
    if not first:
        acc_in, refs = refs[0], refs[1:]
    acc, high, low, scaled, refs = refs[0], refs[1], refs[2], refs[3], refs[4:]
    if last:
        payload, refs = refs[0], refs[1:]
    full, arrived = refs
    steps, columns, rows = scaled.shape[0], scaled.shape[1], kept[0].shape[2]
    wide = full.shape[2]

    def copies(pieces, group):
        made = []
        for place, piece in enumerate(pieces):
            offset = pl.multiple_of(meta[3 * leafs + place] * rows, rows)
            start = group * GROUP + (base if piece.shape[0] > steps else 0)
            made.append(
                pltpu.make_async_copy(
                    piece.at[pl.ds(start, GROUP)],
                    full.at[pl.ds(group * GROUP, GROUP), :, pl.ds(offset, rows), :],
                    arrived.at[group, place],
                )
            )
        return made

    def start(pieces):
        for group in range(steps // GROUP):
            for copy in copies(pieces, group):
                copy.start()

    keeps = meta[3 * leafs + 4 + width]
    pl.when(keeps == 1)(lambda: start(kept))
    pl.when(keeps == 0)(lambda: start(passed))
    if first:
        acc[...] = jnp.zeros_like(acc)
    else:
        acc[...] = acc_in[...]
    for group in range(steps // GROUP):
        for copy in copies(kept, group):
            copy.wait()
        members = range(group * GROUP, (group + 1) * GROUP)
        for s in members:
            blocks = split(full[s, 0:3].reshape(3 * wide, wide))
            merged = split(product(blocks, split(full[s, 3]), False))
            high[s] = merged[0]
            low[s] = merged[1]
        for s in members:
            at = s * columns
            source = split(rhs[at : at + columns] - acc[base + s])
            outgoing = product(source, (high[s], low[s]), True)
            for r in range(3):
                target = meta[3 * (base + s) + r]
                acc[target] = acc[target] + outgoing[:, r * wide : (r + 1) * wide]
            inverse = split(full[s, 3])
            solved = split(product(source, inverse, True))
            scaled[s] = product(solved, inverse, False)
    if last:
        peers, part = payload.shape[0], payload.shape[2]
        groups = columns // part
        for i in range(width + 1):
            node = acc[leafs + meta[3 * leafs + 4 + i]] if i < width else rhs_top[...]
            for p in range(peers):
                at = (p % groups) * part
                payload[p, i] = node[at : at + part]


def backward_kernel(base, first, width, meta, high, low, scaled, state, out, z):
    steps, wide = scaled.shape[0], scaled.shape[2]
    leafs = steps * TURNS
    if first:
        part = state.shape[2]
        groups = scaled.shape[1] // part
        z[...] = jnp.zeros_like(z)
        for i in range(width):
            node = leafs + meta[3 * leafs + 4 + i]
            for p in range(groups):
                z[node, p * part : (p + 1) * part, :] = state[p, i]
    else:
        z[...] = state[...]
    for s in range(steps - 1, -1, -1):
        total = scaled[s]
        for r in (2, 1, 0):
            source = split(z[meta[3 * (base + s) + r]])
            at = slice(r * wide, (r + 1) * wide)
            total = total - product(source, (high[s, at], low[s, at]), False)
        z[base + s] = total
        out[s] = total


def top_prepare_kernel(places, top, high, low, inverse_high, inverse_low, full):
    blocks, rows, wide = top.shape[2], top.shape[3], top.shape[4]
    for place in range(top.shape[1]):
        offset = pl.multiple_of(places[place] * rows, rows)
        full[:, pl.ds(offset, rows), :] = top[0, place]
    inverse = split(full[blocks - 1])
    merged = product(split(full[: blocks - 1].reshape((blocks - 1) * wide, wide)), inverse, False)
    high[0], low[0] = split(merged)
    inverse_high[0], inverse_low[0] = inverse


def top_kernel(above, paths, incoming, high, low, inverse_high, inverse_low, outgoing):
    tops, wide = len(above), high.shape[2]
    width = outgoing.shape[1] - 1
    sources = [incoming[t, width] for t in range(tops)]
    for d, path in enumerate(paths):
        for i, t in enumerate(path):
            sources[t] = sources[t] - incoming[d, i]
    scaled = []
    for j in range(tops):
        source = split(sources[j])
        count = len(above[j])
        if count:
            rows = slice(0, count * wide)
            updates = product(source, (high[j, rows], low[j, rows]), True)
            for i, t in enumerate(above[j]):
                sources[t] = sources[t] - updates[:, i * wide : (i + 1) * wide]
        inverse = (inverse_high[j], inverse_low[j])
        scaled.append(product(split(product(source, inverse, True)), inverse, False))
    solved = [None] * tops
    parts = [None] * tops
    for j in range(tops - 1, -1, -1):
        total = scaled[j]
        for i, t in enumerate(above[j]):
            rows = slice(i * wide, (i + 1) * wide)
            total = total - product(parts[t], (high[j, rows], low[j, rows]), False)
        solved[j] = total
        parts[j] = split(total)
    for p in range(outgoing.shape[0]):
        path = paths[p]
        for i in range(width):
            outgoing[p, i] = solved[path[i] if i < len(path) else path[0]]
        outgoing[p, width] = solved[p]


def local(rhs_leaf, rhs_top, leaf_blocks, leaf_dinv, leaf_struct, top_blocks, top_dinv):
    leafs, columns, wide = rhs_leaf.shape
    tops = top_blocks.shape[0]
    turn = leafs // TURNS
    starts = [turn * sum(CHUNKS[:k]) for k in range(len(CHUNKS) + 1)]
    above = ancestors_of(tops)
    most = max(len(row) for row in above)
    width = most + 1
    paths = paths_of(tops, above)
    groups = min(tops, columns // 8)
    part = columns // groups

    core, zh, zl = lax.axis_index("core"), lax.axis_index("zh"), lax.axis_index("zl")
    xy = lax.axis_index("xy")

    def swap(value):
        return lax.ppermute(value, ("core", "zh"), [(0, 0), (1, 2), (2, 1), (3, 3)])

    def to_keeper(value):
        return lax.ppermute(value, ("core", "zh"), [(1, 0), (2, 3)])

    def to_trader(value):
        return lax.ppermute(value, ("core", "zh"), [(0, 2), (3, 1)])

    def keepers(value):
        return lax.ppermute(value, ("core", "zh", "zl"), [(0, 1), (1, 0), (6, 7), (7, 6)])

    def other(value, *axes):
        last = 2 ** len(axes) - 1
        return lax.ppermute(value, axes, [(i, last - i) for i in range(last + 1)])

    def after(first, value):
        return lax.optimization_barrier((first, value))[1]

    chosen = jnp.take(top_blocks[:, 0], jnp.asarray(padded(above, most))[2 * xy + core], axis=0)
    top = jnp.concatenate([chosen, top_dinv], axis=0)
    top = jnp.stack([top, other(top, "zh"), other(top, "zl"), other(top, "zh", "zl")])

    names = jnp.zeros((8, wide), f32).at[:3, :leafs].set(leaf_struct.T.astype(f32))
    sides = jnp.concatenate([rhs_leaf.reshape(-1, wide), rhs_top.reshape(-1, wide), names], axis=0)
    def joined(at):
        return jnp.concatenate([leaf_blocks[at], leaf_dinv[at][:, None]], axis=1)

    own = joined(slice(None))
    parts = [joined(slice(at, end)) for at, end in zip(starts, starts[1:])]
    own, parts, sides = after(top, (own, parts, sides))

    near = keepers(own)
    sides = swap(sides)
    far = [to_keeper(part) for part in parts]
    across = [keepers(far[0])]
    early = [to_trader(value) for value in (own, near, far[0])]
    across += [keepers(after(early[:2], value)) for value in far[1:]]
    top = lax.all_gather(after((far[-1], sides), top), ("xy", "core"), axis=0, tiled=False)

    names = sides[(leafs + 1) * columns :][:3, :leafs].T.astype(jnp.int32).reshape(-1)
    path = jnp.asarray(padded(paths, width))[2 * xy + zh]
    places = jnp.stack([2 * zh + zl, 2 * zh + 1 - zl, 2 - 2 * zh + zl, 3 - 2 * zh - zl])
    keeps = (core == zh).astype(jnp.int32)
    meta = jnp.concatenate([names, places.astype(jnp.int32), path, keeps[None]])

    vectors = jax.ShapeDtypeStruct((leafs + tops, columns, wide), f32)
    cost = pl.CostEstimate(flops=4 * 10**9, bytes_accessed=8 * 2**20, transcendentals=0)
    factors, state = [], None
    for k, base in enumerate(starts[:-1]):
        last = k == len(CHUNKS) - 1
        steps = starts[k + 1] - base
        merged = jax.ShapeDtypeStruct((steps, 3 * wide, wide), bf16)
        chunk = jax.ShapeDtypeStruct((steps, columns, wide), f32)
        shapes = [vectors, merged, merged, chunk]
        if k == 0:
            last_far = to_trader(far[-1])
            passed = (early[2], to_trader(after(last_far, across[k])))
        else:
            passed = (last_far, to_trader(after(state, across[k])))
        specs = [SMEM] + [pl.BlockSpec(memory_space=pl.ANY)] * 8 + [
            pl.BlockSpec((steps * columns, wide), functools.partial(lambda k, i: (k, 0), base // steps)),
            pl.BlockSpec((columns, wide), lambda i: (leafs, 0)),
        ]
        if last:
            shapes.append(jax.ShapeDtypeStruct((tops, width + 1, part, wide), f32))
        before = () if k == 0 else (state,)
        results = pl.pallas_call(
            functools.partial(forward_kernel, base, leafs, k == 0, last, width),
            grid=(1,),
            in_specs=specs + [VMEM] * (k > 0),
            out_specs=[VMEM] * len(shapes),
            out_shape=shapes,
            scratch_shapes=[
                pltpu.VMEM((steps, 4, wide, wide), f32),
                pltpu.SemaphoreType.DMA((steps // GROUP, 4)),
            ],
            compiler_params=params(),
            cost_estimate=cost,
            name="leaf_forward",
        )(meta, own, near, far[k], across[k], *early[:2], *passed, sides, sides, *before)
        state = results[0]
        factors.append(results[1:4])

    def whole(*shape):
        return pl.BlockSpec((1,) + shape, lambda t: (t,) + (0,) * len(shape))

    top_places = jnp.stack([2 * zh + zl, 2 - 2 * zh + zl, 2 * zh + 1 - zl, 3 - 2 * zh - zl])
    top_factor = pl.pallas_call(
        top_prepare_kernel,
        grid=(tops,),
        in_specs=[SMEM, whole(*top.shape[1:])],
        out_specs=[whole(most * wide, wide)] * 2 + [whole(wide, wide)] * 2,
        out_shape=[jax.ShapeDtypeStruct((tops, most * wide, wide), bf16)] * 2
        + [jax.ShapeDtypeStruct((tops, wide, wide), bf16)] * 2,
        scratch_shapes=[pltpu.VMEM((width, wide, wide), f32)],
        compiler_params=params(),
        name="top_prepare",
    )(top_places.astype(jnp.int32), after(results[4], top))

    incoming = lax.all_to_all(results[4], ("xy", "zh"), split_axis=0, concat_axis=0, tiled=True)
    outgoing = pl.pallas_call(
        functools.partial(top_kernel, above, paths),
        in_specs=[VMEM] * 5,
        out_specs=VMEM,
        out_shape=jax.ShapeDtypeStruct((tops, width + 1, part, wide), f32),
        compiler_params=params(),
        name="top_solve",
    )(incoming, *top_factor)
    state = lax.all_to_all(outgoing, ("xy", "zh"), split_axis=0, concat_axis=0, tiled=True)
    own_top = state[:groups, width].reshape(1, columns, wide)

    found = [None] * TURNS
    chunk = jax.ShapeDtypeStruct((turn, columns, wide), f32)
    for k in range(TURNS - 1, -1, -1):
        held = max(i for i, at in enumerate(starts[:-1]) if at <= k * turn)
        part_of = [
            pl.BlockSpec(
                (turn,) + shape, functools.partial(lambda at, i: (at, 0, 0), k - starts[held] // turn)
            )
            for shape in ((3 * wide, wide), (3 * wide, wide), (columns, wide))
        ]
        found[k], state = pl.pallas_call(
            functools.partial(backward_kernel, k * turn, k == TURNS - 1, width),
            grid=(1,),
            in_specs=[SMEM] + part_of + [VMEM],
            out_specs=[VMEM] * 2,
            out_shape=[chunk, vectors],
            compiler_params=params(),
            cost_estimate=cost,
            name="leaf_backward",
        )(meta, *factors[held], state)
    late = swap(found[-1])
    middle = swap(jnp.concatenate(found[1:-1] + [own_top], axis=0))
    first = swap(found[0])
    leaf_solution = jnp.concatenate([first, middle[:-1], late], axis=0)
    return (leaf_solution, middle[-1:])


def solution(mesh):
    subtrees, quarters = mesh.devices.shape
    fine = Mesh(
        mesh.devices.reshape(subtrees // 2, 2, 2, quarters // 2), ("xy", "core", "zh", "zl")
    )
    sn, rhs = ("xy", "core"), ("zh", "zl")
    return jax.shard_map(
        local,
        mesh=fine,
        in_specs=(
            P(sn, rhs, None),
            P(sn, rhs, None),
            P(sn, None, rhs, None),
            P(sn, rhs, None),
            P(sn, None),
            P(None, sn, rhs, None),
            P(sn, rhs, None),
        ),
        out_specs=(P(sn, rhs, None), P(sn, rhs, None)),
        check_vma=False,
    )
```

```python
import functools

import jax
import jax.numpy as jnp
import numpy as np
from jax import lax
from jax.experimental import pallas as pl
from jax.experimental.pallas import tpu as pltpu
from jax.sharding import Mesh
from jax.sharding import PartitionSpec as P

CHUNKS = (3, 1)
TURNS = 4
GROUP = 4
f32 = jnp.float32
bf16 = jnp.bfloat16
SMEM = pl.BlockSpec(memory_space=pltpu.SMEM)
VMEM = pl.BlockSpec(memory_space=pltpu.VMEM)


def params():
    return pltpu.CompilerParams(vmem_limit_bytes=28 * 2**20)


def split(value):
    high = value.astype(bf16)
    return high, (value - high.astype(f32)).astype(bf16)


def product(left, right, transposed):
    dims = (((1,), (1 if transposed else 0,)), ((), ()))

    def dot(a, b):
        return lax.dot_general(a, b, dims, preferred_element_type=f32)

    rows = left[0].shape[0]
    if rows % 16:
        return dot(left[0], right[0]) + (dot(left[1], right[0]) + dot(left[0], right[1]))
    both = dot(jnp.concatenate(left, axis=0), right[0])
    return both[:rows] + (both[rows:] + dot(left[0], right[1]))


def ancestors_of(tops):
    def level(t):
        return ((t + 1) & -(t + 1)).bit_length() - 1

    return [[t for t in range(j + 1, tops) if t + 1 - 2 ** level(t) <= j] for j in range(tops)]


def paths_of(subtrees, above):
    return [[4 * (d // 4)] + above[4 * (d // 4)] for d in range(subtrees)]


def padded(rows, width):
    return np.array([row + [row[0] if row else 0] * (width - len(row)) for row in rows], np.int32)


def forward_kernel(base, leafs, first, last, width, *refs):
    meta, kept, passed, rhs, rhs_top = refs[0], refs[1:5], refs[5:9], refs[9], refs[10]
    refs = refs[11:]
    if not first:
        acc_in, refs = refs[0], refs[1:]
    acc, high, low, scaled, refs = refs[0], refs[1], refs[2], refs[3], refs[4:]
    if last:
        payload, refs = refs[0], refs[1:]
    full, arrived = refs
    steps, columns, rows = scaled.shape[0], scaled.shape[1], kept[0].shape[2]
    wide = full.shape[2]

    def copies(pieces, group):
        made = []
        for place, piece in enumerate(pieces):
            offset = pl.multiple_of(meta[3 * leafs + place] * rows, rows)
            start = group * GROUP + (base if piece.shape[0] > steps else 0)
            made.append(
                pltpu.make_async_copy(
                    piece.at[pl.ds(start, GROUP)],
                    full.at[pl.ds(group * GROUP, GROUP), :, pl.ds(offset, rows), :],
                    arrived.at[group, place],
                )
            )
        return made

    def start(pieces):
        for group in range(steps // GROUP):
            for copy in copies(pieces, group):
                copy.start()

    keeps = meta[3 * leafs + 4 + width]
    pl.when(keeps == 1)(lambda: start(kept))
    pl.when(keeps == 0)(lambda: start(passed))
    if first:
        acc[...] = jnp.zeros_like(acc)
    else:
        acc[...] = acc_in[...]
    for group in range(steps // GROUP):
        for copy in copies(kept, group):
            copy.wait()
        members = range(group * GROUP, (group + 1) * GROUP)
        for s in members:
            blocks = split(full[s, 0:3].reshape(3 * wide, wide))
            merged = split(product(blocks, split(full[s, 3]), False))
            high[s] = merged[0]
            low[s] = merged[1]
        for s in members:
            at = s * columns
            source = split(rhs[at : at + columns] - acc[base + s])
            outgoing = product(source, (high[s], low[s]), True)
            for r in range(3):
                target = meta[3 * (base + s) + r]
                acc[target] = acc[target] + outgoing[:, r * wide : (r + 1) * wide]
            inverse = split(full[s, 3])
            solved = split(product(source, inverse, True))
            scaled[s] = product(solved, inverse, False)
    if last:
        peers, part = payload.shape[0], payload.shape[2]
        groups = columns // part
        for i in range(width + 1):
            node = acc[leafs + meta[3 * leafs + 4 + i]] if i < width else rhs_top[...]
            for p in range(peers):
                at = (p % groups) * part
                payload[p, i] = node[at : at + part]


def backward_kernel(base, first, width, meta, high, low, scaled, state, out, z):
    steps, wide = scaled.shape[0], scaled.shape[2]
    leafs = steps * TURNS
    if first:
        part = state.shape[2]
        groups = scaled.shape[1] // part
        z[...] = jnp.zeros_like(z)
        for i in range(width):
            node = leafs + meta[3 * leafs + 4 + i]
            for p in range(groups):
                z[node, p * part : (p + 1) * part, :] = state[p, i]
    else:
        z[...] = state[...]
    for s in range(steps - 1, -1, -1):
        total = scaled[s]
        for r in (2, 1, 0):
            source = split(z[meta[3 * (base + s) + r]])
            at = slice(r * wide, (r + 1) * wide)
            total = total - product(source, (high[s, at], low[s, at]), False)
        z[base + s] = total
        out[s] = total


def top_prepare_kernel(places, top, high, low, inverse_high, inverse_low, full):
    blocks, rows, wide = top.shape[2], top.shape[3], top.shape[4]
    for place in range(top.shape[1]):
        offset = pl.multiple_of(places[place] * rows, rows)
        full[:, pl.ds(offset, rows), :] = top[0, place]
    inverse = split(full[blocks - 1])
    merged = product(split(full[: blocks - 1].reshape((blocks - 1) * wide, wide)), inverse, False)
    high[0], low[0] = split(merged)
    inverse_high[0], inverse_low[0] = inverse


def top_kernel(above, paths, incoming, high, low, inverse_high, inverse_low, outgoing):
    tops, wide = len(above), high.shape[2]
    width = outgoing.shape[1] - 1
    sources = [incoming[t, width] for t in range(tops)]
    for d, path in enumerate(paths):
        for i, t in enumerate(path):
            sources[t] = sources[t] - incoming[d, i]
    scaled = []
    for j in range(tops):
        source = split(sources[j])
        count = len(above[j])
        if count:
            rows = slice(0, count * wide)
            updates = product(source, (high[j, rows], low[j, rows]), True)
            for i, t in enumerate(above[j]):
                sources[t] = sources[t] - updates[:, i * wide : (i + 1) * wide]
        inverse = (inverse_high[j], inverse_low[j])
        scaled.append(product(split(product(source, inverse, True)), inverse, False))
    solved = [None] * tops
    parts = [None] * tops
    for j in range(tops - 1, -1, -1):
        total = scaled[j]
        for i, t in enumerate(above[j]):
            rows = slice(i * wide, (i + 1) * wide)
            total = total - product(parts[t], (high[j, rows], low[j, rows]), False)
        solved[j] = total
        parts[j] = split(total)
    for p in range(outgoing.shape[0]):
        path = paths[p]
        for i in range(width):
            outgoing[p, i] = solved[path[i] if i < len(path) else path[0]]
        outgoing[p, width] = solved[p]


def local(rhs_leaf, rhs_top, leaf_blocks, leaf_dinv, leaf_struct, top_blocks, top_dinv):
    leafs, columns, wide = rhs_leaf.shape
    tops = top_blocks.shape[0]
    turn = leafs // TURNS
    starts = [turn * sum(CHUNKS[:k]) for k in range(len(CHUNKS) + 1)]
    above = ancestors_of(tops)
    most = max(len(row) for row in above)
    width = most + 1
    paths = paths_of(tops, above)
    groups = min(tops, columns // 8)
    part = columns // groups

    core, zh, zl = lax.axis_index("core"), lax.axis_index("zh"), lax.axis_index("zl")
    xy = lax.axis_index("xy")

    def swap(value):
        return lax.ppermute(value, ("core", "zh"), [(0, 0), (1, 2), (2, 1), (3, 3)])

    def to_keeper(value):
        return lax.ppermute(value, ("core", "zh"), [(1, 0), (2, 3)])

    def to_trader(value):
        return lax.ppermute(value, ("core", "zh"), [(0, 2), (3, 1)])

    def keepers(value):
        return lax.ppermute(value, ("core", "zh", "zl"), [(0, 1), (1, 0), (6, 7), (7, 6)])

    def other(value, *axes):
        last = 2 ** len(axes) - 1
        return lax.ppermute(value, axes, [(i, last - i) for i in range(last + 1)])

    def after(first, value):
        return lax.optimization_barrier((first, value))[1]

    chosen = jnp.take(top_blocks[:, 0], jnp.asarray(padded(above, most))[2 * xy + core], axis=0)
    top = jnp.concatenate([chosen, top_dinv], axis=0)
    top = jnp.stack([top, other(top, "zh"), other(top, "zl"), other(top, "zh", "zl")])

    names = jnp.zeros((8, wide), f32).at[:3, :leafs].set(leaf_struct.T.astype(f32))
    sides = jnp.concatenate([rhs_leaf.reshape(-1, wide), rhs_top.reshape(-1, wide), names], axis=0)
    def joined(at):
        return jnp.concatenate([leaf_blocks[at], leaf_dinv[at][:, None]], axis=1)

    own = joined(slice(None))
    parts = [joined(slice(at, end)) for at, end in zip(starts, starts[1:])]
    own, parts, sides = after(top, (own, parts, sides))

    near = keepers(own)
    sides = swap(sides)
    far = [to_keeper(part) for part in parts]
    across = [keepers(far[0])]
    early = [to_trader(value) for value in (own, near, far[0])]
    across += [keepers(after(early[:2], value)) for value in far[1:]]
    top = lax.all_gather(after((far[-1], sides), top), ("xy", "core"), axis=0, tiled=False)

    names = sides[(leafs + 1) * columns :][:3, :leafs].T.astype(jnp.int32).reshape(-1)
    path = jnp.asarray(padded(paths, width))[2 * xy + zh]
    places = jnp.stack([2 * zh + zl, 2 * zh + 1 - zl, 2 - 2 * zh + zl, 3 - 2 * zh - zl])
    keeps = (core == zh).astype(jnp.int32)
    meta = jnp.concatenate([names, places.astype(jnp.int32), path, keeps[None]])

    vectors = jax.ShapeDtypeStruct((leafs + tops, columns, wide), f32)
    cost = pl.CostEstimate(flops=4 * 10**9, bytes_accessed=8 * 2**20, transcendentals=0)
    factors, state = [], None
    for k, base in enumerate(starts[:-1]):
        last = k == len(CHUNKS) - 1
        steps = starts[k + 1] - base
        merged = jax.ShapeDtypeStruct((steps, 3 * wide, wide), bf16)
        chunk = jax.ShapeDtypeStruct((steps, columns, wide), f32)
        shapes = [vectors, merged, merged, chunk]
        if k == 0:
            last_far = to_trader(far[-1])
            passed = (early[2], to_trader(after(last_far, across[k])))
        else:
            passed = (last_far, to_trader(after(state, across[k])))
        specs = [SMEM] + [pl.BlockSpec(memory_space=pl.ANY)] * 8 + [
            pl.BlockSpec((steps * columns, wide), functools.partial(lambda k, i: (k, 0), base // steps)),
            pl.BlockSpec((columns, wide), lambda i: (leafs, 0)),
        ]
        if last:
            shapes.append(jax.ShapeDtypeStruct((tops, width + 1, part, wide), f32))
        before = () if k == 0 else (state,)
        results = pl.pallas_call(
            functools.partial(forward_kernel, base, leafs, k == 0, last, width),
            grid=(1,),
            in_specs=specs + [VMEM] * (k > 0),
            out_specs=[VMEM] * len(shapes),
            out_shape=shapes,
            scratch_shapes=[
                pltpu.VMEM((steps, 4, wide, wide), f32),
                pltpu.SemaphoreType.DMA((steps // GROUP, 4)),
            ],
            compiler_params=params(),
            cost_estimate=cost,
            name="leaf_forward",
        )(meta, own, near, far[k], across[k], *early[:2], *passed, sides, sides, *before)
        state = results[0]
        factors.append(results[1:4])

    def whole(*shape):
        return pl.BlockSpec((1,) + shape, lambda t: (t,) + (0,) * len(shape))

    top_places = jnp.stack([2 * zh + zl, 2 - 2 * zh + zl, 2 * zh + 1 - zl, 3 - 2 * zh - zl])
    top_factor = pl.pallas_call(
        top_prepare_kernel,
        grid=(tops,),
        in_specs=[SMEM, whole(*top.shape[1:])],
        out_specs=[whole(most * wide, wide)] * 2 + [whole(wide, wide)] * 2,
        out_shape=[jax.ShapeDtypeStruct((tops, most * wide, wide), bf16)] * 2
        + [jax.ShapeDtypeStruct((tops, wide, wide), bf16)] * 2,
        scratch_shapes=[pltpu.VMEM((width, wide, wide), f32)],
        compiler_params=params(),
        name="top_prepare",
    )(top_places.astype(jnp.int32), after(results[4], top))

    incoming = lax.all_to_all(results[4], ("xy", "zh"), split_axis=0, concat_axis=0, tiled=True)
    outgoing = pl.pallas_call(
        functools.partial(top_kernel, above, paths),
        in_specs=[VMEM] * 5,
        out_specs=VMEM,
        out_shape=jax.ShapeDtypeStruct((tops, width + 1, part, wide), f32),
        compiler_params=params(),
        name="top_solve",
    )(incoming, *top_factor)
    state = lax.all_to_all(outgoing, ("xy", "zh"), split_axis=0, concat_axis=0, tiled=True)
    own_top = state[:groups, width].reshape(1, columns, wide)

    found = [None] * TURNS
    chunk = jax.ShapeDtypeStruct((turn, columns, wide), f32)
    for k in range(TURNS - 1, -1, -1):
        held = max(i for i, at in enumerate(starts[:-1]) if at <= k * turn)
        part_of = [
            pl.BlockSpec(
                (turn,) + shape, functools.partial(lambda at, i: (at, 0, 0), k - starts[held] // turn)
            )
            for shape in ((3 * wide, wide), (3 * wide, wide), (columns, wide))
        ]
        found[k], state = pl.pallas_call(
            functools.partial(backward_kernel, k * turn, k == TURNS - 1, width),
            grid=(1,),
            in_specs=[SMEM] + part_of + [VMEM],
            out_specs=[VMEM] * 2,
            out_shape=[chunk, vectors],
            compiler_params=params(),
            cost_estimate=cost,
            name="leaf_backward",
        )(meta, *factors[held], state)
    most_of = swap(jnp.concatenate(found[1:] + [own_top], axis=0))
    first = swap(found[0])
    leaf_solution = jnp.concatenate([first, most_of[:-1]], axis=0)
    return (leaf_solution, most_of[-1:])


def solution(mesh):
    subtrees, quarters = mesh.devices.shape
    fine = Mesh(
        mesh.devices.reshape(subtrees // 2, 2, 2, quarters // 2), ("xy", "core", "zh", "zl")
    )
    sn, rhs = ("xy", "core"), ("zh", "zl")
    return jax.shard_map(
        local,
        mesh=fine,
        in_specs=(
            P(sn, rhs, None),
            P(sn, rhs, None),
            P(sn, None, rhs, None),
            P(sn, rhs, None),
            P(sn, None),
            P(None, sn, rhs, None),
            P(sn, rhs, None),
        ),
        out_specs=(P(sn, rhs, None), P(sn, rhs, None)),
        check_vma=False,
    )
```
